32 devices in a mesh: queue: 16 (over z, y, x), tok: 2 (over core).
Axes of the slice: x: 2, y: 2, z: 4, core: 2. Of those that a mesh axis runs over, the one named last changes fastest.
Arguments:
- latent: float32 [16, 64, 64], P('queue', 'tok'), may hold values from -1.5 to 1.5
- fresh_noise: float32 [3, 64, 64], P(None, 'tok'), may hold values from -1.5 to 1.5
- frame_slot: int32 [16], replicated, may hold values from 0 to 15
- frame_reach: int32 [16], replicated, may hold values from 0 to 3, as said below
- level_embed: bfloat16 [19, 3072], P(None, 'tok'), may hold values from -0.59765625 to 0.59765625
- embed_weight: bfloat16 [64, 3072], P(None, 'tok'), may hold values from -0.75 to 0.75
- qkv_weight: bfloat16 [3, 1536, 3072], P(None, 'tok'), may hold values from -0.1100574 to 0.1100574
- qk_gain: float32 [2, 1536], P(None, 'tok'), may hold values from 0.5 to 6
- out_weight: bfloat16 [1536, 3072], P('tok'), may hold values from -0.5 to 0.5
- vel_weight: bfloat16 [3072, 64], P('tok'), may hold values from -0.5390625 to 0.5390625
Outputs:
- velocity: float32 [3, 16, 64, 64], P(None, 'queue', 'tok')
- queue_out: float32 [16, 64, 64], P('queue', 'tok')
The draws below stay inside these ranges and needn't reach their ends.
Inputs may be any that keep to these rules, and one draw needn't show every extreme that they name: `frame_reach`: some position has width 3.
All inputs are finite; a program needn't handle non-finite values.
Results may differ from the reference program's by a relative error of at most 0.024.
Values may be sent and summed in bfloat16 or wider, within the bound.
No kernel may reach another device: no remote copies, remote signals or barrier semaphores. Data moves between devices by JAX's collectives and lax.ppermute only.
A program may use at most 64 MiB of HBM per device.

```python
import math
import jax
import jax.numpy as jnp
from jax import lax

D = 3072
HEADS = 24
HD = 64
C = 64
STEPS = 3
HALO = 3
FRAMES = 16
FRAME_TOK = 64
HL = 1536
LEVELS = 19


def draw_frame_slot(key, part):
    key = jax.random.fold_in(key, 11)
    positions = jnp.arange(FRAMES, dtype=jnp.int32)
    jitter = jax.random.randint(key, (FRAMES,), -3, 4, dtype=jnp.int32)
    return jnp.clip(positions + jitter, 0, FRAMES - 1).astype(jnp.int32)


def draw_frame_reach(key, part):
    key = jax.random.fold_in(key, 12)
    first_key, second_key = jax.random.split(key)
    widths = jax.random.randint(first_key, (FRAMES,), 0, HALO + 1, dtype=jnp.int32)
    chosen = jax.random.randint(second_key, (), 0, FRAMES, dtype=jnp.int32)
    positions = jnp.arange(FRAMES, dtype=jnp.int32)
    return jnp.where(positions == chosen, HALO, widths).astype(jnp.int32)


def draw_qkv_weight(key, part):
    key = jax.random.fold_in(key, 13)
    first_key, second_key, third_key = jax.random.split(key, 3)
    query_part = jnp.clip(jax.random.normal(first_key, (D, HL), jnp.float32), -6.0, 6.0)
    key_part = jnp.clip(jax.random.normal(second_key, (D, HL), jnp.float32), -6.0, 6.0)
    value_part = jnp.clip(jax.random.normal(third_key, (D, HL), jnp.float32), -6.0, 6.0)
    stacked = jnp.stack([query_part, key_part, value_part]) / math.sqrt(D)
    return jnp.swapaxes(stacked, 1, 2).astype(jnp.bfloat16)


def draw_qk_gain(key, part):
    key = jax.random.fold_in(key, 14)
    second_key = jax.random.fold_in(key, 1)
    third_key = jax.random.fold_in(key, 2)
    query_gain = jax.random.uniform(second_key, (HL,), jnp.float32, 1.0, 2.0)
    key_gain = jax.random.uniform(third_key, (HL,), jnp.float32, 1.0, 2.0)
    return jnp.stack([query_gain, key_gain]).astype(jnp.float32)


def block_levels(own_key, dims, cuts, smallest, high):
    loudness, own = 1.0, jax.random.fold_in(own_key, 6)
    for axis_at, shards_of in cuts:
        draws = jnp.exp(jax.random.uniform(jax.random.fold_in(own, axis_at), (shards_of,), jnp.float32, smallest / len(cuts), high / len(cuts)))
        loudness = loudness * jnp.repeat(draws, dims[axis_at] // shards_of).reshape([-1 if axis == axis_at else 1 for axis in range(len(dims))])
    return loudness


def centred(key, extent, scale, most, pieces=(), kind=jnp.bfloat16):
    entries = scale * jax.random.normal(key, extent, jnp.float32)
    if pieces:
        entries = entries * block_levels(key, extent, pieces, -0.22, 0.18)
    return jnp.clip(entries, -most, most).astype(kind)


def setup_inputs(seed: int = 0) -> dict:
    key_of = jax.random.split(jax.random.key(seed), 11)
    return {
        "latent": centred(key_of[0], (FRAMES, FRAME_TOK, C), 0.25, 1.5, ((0, 16), (1, 2)), jnp.float32),
        "fresh_noise": centred(key_of[1], (STEPS, FRAME_TOK, C), 0.25, 1.5, ((1, 2),), jnp.float32),
        "frame_slot": draw_frame_slot(jax.random.fold_in(key_of[10], 71), 0),
        "frame_reach": draw_frame_reach(jax.random.fold_in(key_of[10], 71), 0),
        "level_embed": centred(key_of[4], (LEVELS, D), 0.1, 0.59765625, ((1, 2),)),
        "embed_weight": centred(key_of[5], (C, D), C ** -0.5, 0.75, ((1, 2),)),
        "qkv_weight": draw_qkv_weight(jax.random.fold_in(key_of[10], 71), 0),
        "qk_gain": draw_qk_gain(jax.random.fold_in(key_of[10], 71), 0),
        "out_weight": centred(key_of[8], (HL, D), (2.0 / HL ** 0.5), 0.5, ((0, 2),)),
        "vel_weight": centred(key_of[9], (D, C), (5.0 / D ** 0.5), 0.5390625, ((0, 2),)),
    }


EPS = 1e-06

def widen(values_bf16):
    return lax.optimization_barrier(values_bf16).astype(jnp.float32)

def head_norm(projection, gain_row):
    per_head = projection.reshape(projection.shape[0], projection.shape[1], HEADS, HD)
    scaled = per_head * lax.rsqrt(lax.optimization_barrier(jnp.mean(per_head * per_head, axis=-1, keepdims=True)) + EPS)
    return (scaled * gain_row.reshape(HEADS, HD)).astype(jnp.bfloat16)

def reference(latent, fresh_noise, frame_slot, frame_reach, level_embed, embed_weight, qkv_weight, qk_gain, out_weight, vel_weight):
    frames = jnp.arange(FRAMES, dtype=jnp.int32)
    offsets = jnp.arange(2 * HALO + 1, dtype=jnp.int32) - HALO
    embed_f = embed_weight.astype(jnp.float32)
    qkv_f = qkv_weight.astype(jnp.float32)
    out_f = out_weight.astype(jnp.float32)
    vel_f = vel_weight.astype(jnp.float32)
    target = frames[:, None] + offsets[None, :]
    counted = (jnp.abs(offsets)[None, :] <= frame_reach[:, None]) & (target >= 0) & (target < FRAMES)
    queue_state = latent
    outputs = []
    for step_index in range(STEPS):
        queue_state = jnp.concatenate([fresh_noise[step_index][None], queue_state[:-1]], axis=0)
        source = jnp.clip(frames - step_index - 1, 0, FRAMES - 1)
        noise_level = jnp.where(frames >= step_index + 1, frame_slot[source] + step_index, frames).astype(jnp.int32)
        hidden = jnp.einsum('ftc,cd->ftd', widen(queue_state.astype(jnp.bfloat16)), embed_f)
        hidden = hidden + level_embed[noise_level].astype(jnp.float32)[:, None, :]
        normed = (hidden * lax.rsqrt(lax.optimization_barrier(jnp.mean(hidden * hidden, axis=-1, keepdims=True)) + EPS)).astype(jnp.bfloat16)
        normed_f = widen(normed)
        queries = head_norm(jnp.einsum('ftd,hd->fth', normed_f, qkv_f[0]), qk_gain[0])
        key_rows = head_norm(jnp.einsum('ftd,hd->fth', normed_f, qkv_f[1]), qk_gain[1])
        values = jnp.einsum('ftd,hd->fth', normed_f, qkv_f[2]).astype(jnp.bfloat16)
        values = values.reshape(FRAMES, FRAME_TOK, HEADS, HD)
        pad_spec = ((HALO, HALO), (0, 0), (0, 0), (0, 0))
        key_pad = jnp.pad(key_rows, pad_spec)
        value_pad = jnp.pad(values, pad_spec)

        def attend(inputs):
            frame_query, frame_pos, frame_ok = inputs
            key_window = lax.dynamic_slice_in_dim(key_pad, frame_pos, 2 * HALO + 1, 0)
            value_window = lax.dynamic_slice_in_dim(value_pad, frame_pos, 2 * HALO + 1, 0)
            scores = jnp.einsum('qhc,jkhc->hqjk', widen(frame_query), widen(key_window)) * HD ** (-0.5)
            scores = jnp.where(frame_ok[None, None, :, None], scores, -1e+30)
            row_max = lax.optimization_barrier(jnp.max(scores, axis=(2, 3), keepdims=True))
            expo = jnp.exp(scores - row_max)
            row_total = lax.optimization_barrier(jnp.sum(expo, axis=(2, 3), keepdims=True))
            weights = (expo / row_total).astype(jnp.bfloat16)
            attended = jnp.einsum('hqjk,jkhc->qhc', widen(weights), widen(value_window)).astype(jnp.bfloat16)
            return attended.reshape(FRAME_TOK, HL)
        attended = lax.map(attend, (queries, frames, counted))
        combined = hidden + jnp.einsum('fth,hd->ftd', widen(attended), out_f)
        velocity = jnp.einsum('ftd,dc->ftc', combined, vel_f, precision=lax.Precision.HIGHEST)
        queue_state = queue_state - velocity / LEVELS
        outputs.append(velocity)
    return (jnp.stack(outputs), queue_state)
```

```python
import functools
import math

import jax
import jax.numpy as jnp
from jax import lax
from jax.experimental import pallas as pl
from jax.experimental.pallas import tpu as pltpu
from jax.sharding import PartitionSpec as P

HD = 64
STEPS = 3
HALO = 3
LANES = 128
EPS = 1e-06
F32, BF16 = jnp.float32, jnp.bfloat16


def round_up(value, unit):
    return -(-value // unit) * unit


def dot(a, b):
    return jnp.dot(a, b, preferred_element_type=F32)


def dot_nt(a, b):
    return lax.dot_general(a, b, (((1,), (1,)), ((), ())), preferred_element_type=F32)


def halves(value, axis):
    high = value.astype(BF16)
    low = (value - high.astype(F32)).astype(BF16)
    return jnp.concatenate([high, low], axis=axis)


def weights_kernel(rows, base, g_ref, qkv_hbm, out_hbm, mq_ref, mk_ref, mv_ref, wo_ref, gram_ref, buf, sems):
    width = out_hbm.shape[0]
    per = width // rows
    parts, _, depth = g_ref.shape
    copies = []
    for chunk in range(4 * per):
        source = qkv_hbm.at[chunk // per] if chunk < 3 * per else out_hbm
        copy = pltpu.make_async_copy(
            source.at[pl.ds((chunk % per) * rows, rows)], buf.at[chunk], sems.at[chunk]
        )
        copy.start()
        copies.append(copy)
    gram = sum(dot_nt(g_ref[t], g_ref[t, :base]) for t in range(parts))
    gram_ref[...] = halves(gram, 1)
    for chunk in range(4 * per):
        copies[chunk].wait()
        where = pl.ds((chunk % per) * rows, rows)
        blocks = [buf[chunk, :, t * depth : (t + 1) * depth] for t in range(parts)]
        kind = chunk // per
        if kind in (0, 2):
            target = mq_ref if kind == 0 else mv_ref
            target[where, :] = halves(sum(dot_nt(blocks[t], g_ref[t, :base]) for t in range(parts)), 1)
        elif kind == 1:
            mk_ref[:, where] = halves(sum(dot_nt(g_ref[t, :base], blocks[t]) for t in range(parts)), 0)
        else:
            wo_ref[:, where] = halves(sum(dot_nt(g_ref[t, base:], blocks[t]) for t in range(parts)), 0)


def advance(level_count, tok, first, g_ref, hpart_ref, xq_ref):
    shared = g_ref[0]
    for t in range(1, g_ref.shape[0]):
        shared = shared + g_ref[t]
    velocity = shared + hpart_ref[...]
    moved = xq_ref[...] - velocity * (1.0 / level_count)
    if first is None:
        return velocity, moved
    lane_frame = lax.broadcasted_iota(jnp.int32, (1, shared.shape[1]), 1) // tok
    return velocity, jnp.where(lane_frame + first == -1, shared, moved)


def own_rows(block, tok, part_rows, index, scratch):
    scratch[...] = block.T
    return scratch[pl.ds(pl.multiple_of(index * part_rows, 8), part_rows), :]


def step_kernel(step, cfg, *refs):
    tok, frames, channels, base, depth, level_count, heads, part_rows = cfg
    query_block = max(1, LANES // tok)
    n_query = query_block + 2 * HALO * (STEPS - 1 - step)
    n_key = n_query + 2 * HALO
    key_lanes, query_lanes = n_key * tok, n_query * tok
    width = heads * HD
    window = (2 * HALO + query_block) * tok
    position, tok_index = lax.axis_index("queue"), lax.axis_index("tok")
    first_key = position - HALO - (HALO + 1) * (STEPS - 1 - step)
    refs = list(refs)
    slot_ref, reach_ref = refs[0], refs[1]
    if step == 0:
        lat_ref = refs[2]
        refs = refs[3:]
    else:
        g_ref, hprev_ref, xprev_ref = refs[2:5]
        refs = refs[5:]
    fresh_ref = None
    if step < STEPS - 1:
        fresh_ref = refs.pop(0)
    gain_ref, mq_ref, mk_ref, mv_ref, wo_ref, gram_ref = refs[:6]
    refs = refs[6:]
    part_ref, hpart_ref, xq_ref = refs[:3]
    refs = refs[3:]
    own_ref = None
    if step > 0:
        own_ref = refs.pop(0)
    kbuf, vbuf, qbuf, att, tbuf = refs

    if step == 0:
        pieces = []
        for w in range(n_key):
            source = lax.rem(first_key - 1 + w + 2 * frames, frames)
            pieces.append(lat_ref[pl.ds(pl.multiple_of(source * tok, 8), tok), :])
        state = jnp.concatenate(pieces, axis=0).T
    else:
        velocity, state = advance(level_count, tok, first_key - 1, g_ref, hprev_ref, xprev_ref)
        mine = (HALO + 1) * (STEPS - step)
        own_ref[...] = own_rows(velocity[:, mine * tok : (mine + 1) * tok], tok, part_rows, tok_index, tbuf)

    key_frame = lax.broadcasted_iota(jnp.int32, (1, key_lanes), 1) // tok
    level_row = jnp.full((1, key_lanes), -1, jnp.int32)
    for w in range(n_key):
        frame = first_key + w
        known = slot_ref[jnp.clip(frame - step - 1, 0, frames - 1)] + step
        level_row = jnp.where(key_frame == w, jnp.where(frame >= step + 1, known, frame), level_row)
    row = lax.broadcasted_iota(jnp.int32, (base - channels, key_lanes), 0)
    aug_t = jnp.concatenate([state, jnp.where(row == level_row, 1.0, 0.0)], axis=0)
    aug_t = aug_t.astype(BF16).astype(F32)
    aug = aug_t.T
    aug_b, aug_tb = aug.astype(BF16), aug_t.astype(BF16)
    aug_q = aug_t[:, HALO * tok : HALO * tok + query_lanes]
    aug_qb = aug_q.astype(BF16)
    both = jnp.concatenate([aug_b, aug_b], axis=1)
    both_t = jnp.concatenate([aug_tb, aug_tb], axis=0)
    both_q = jnp.concatenate([aug_qb, aug_qb], axis=0)
    gram = gram_ref[:base, :]
    mean_t = jnp.sum(dot(gram, both_t) * aug_t, axis=0, keepdims=True) * (1.0 / depth)
    mean_q = jnp.sum(dot(gram, both_q) * aug_q, axis=0, keepdims=True) * (1.0 / depth)
    mean_c = jnp.sum(dot_nt(both, gram) * aug, axis=1, keepdims=True) * (1.0 / depth)
    mean_t, mean_q, mean_c = (jnp.maximum(m, 0.0) + EPS for m in (mean_t, mean_q, mean_c))

    hpart_ref[...] = dot(gram_ref[base:, :], both_q)
    xq_ref[...] = state[:, HALO * tok : HALO * tok + query_lanes]

    gain = gain_ref[0:1, :] * gain_ref[1:2, :] * (HD ** -0.5 * math.log2(math.e))
    span = 256 if width % 256 == 0 else 128
    head_of = lambda axis: lax.broadcasted_iota(jnp.int32, (span, span), axis) // HD
    average = jnp.where(head_of(0) == head_of(1), 1.0 / HD, 0.0).astype(BF16)
    for at in range(0, width, span):
        raw = dot(both, mk_ref[:, at : at + span])
        spread = dot((raw * raw).astype(BF16), average)
        kbuf[:, at : at + span] = (raw * lax.rsqrt(spread + EPS * mean_c) * gain[:, at : at + span]).astype(BF16)
    vbuf[...] = (dot(mv_ref[...], both_t) * lax.rsqrt(mean_t)).astype(BF16)
    raw = dot(mq_ref[...], both_q).reshape(heads, HD, query_lanes)
    spread = jnp.sum(raw * raw, axis=1, keepdims=True) * (1.0 / HD)
    qbuf[...] = (raw * lax.rsqrt(spread + EPS * mean_q)[:, :, :]).reshape(width, query_lanes).astype(BF16)

    def block(b, carry):
        lead = (b * LANES) // tok
        keys = pl.ds(pl.multiple_of(lead * tok, LANES), window)
        lanes = pl.ds(pl.multiple_of(b * LANES, LANES), LANES)
        lane = lax.broadcasted_iota(jnp.int32, (1, 2 * LANES), 1)
        within = lax.rem(lane, LANES) // tok
        bias_rows = []
        reach = []
        for j in range(query_block):
            frame = first_key + HALO + lead + j
            reach.append(reach_ref[jnp.clip(frame, 0, frames - 1)])
        for k in range(2 * HALO + query_block):
            target = first_key + lead + k
            inside = (target >= 0) & (target < frames)
            bias = jnp.zeros((1, 2 * LANES), F32)
            for j in range(query_block):
                counted = inside & (abs(k - HALO - j) <= reach[j])
                value = jnp.where(counted, 0.0, -1e30)
                bias = jnp.where(within == j, value, bias) if query_block > 1 else bias + value
            bias_rows.append(bias)
        ones = jnp.ones((16, window), BF16)
        upper = lax.broadcasted_iota(jnp.int32, (2 * HD, LANES), 0) < HD
        for pair in range(heads // 2):
            cols = slice(pair * 2 * HD, (pair + 1) * 2 * HD)
            query = qbuf[cols, lanes]
            zero = jnp.zeros_like(query)
            query = jnp.concatenate([jnp.where(upper, query, zero), jnp.where(upper, zero, query)], axis=1)
            score = dot(kbuf[keys, cols], query)
            score = jnp.concatenate(
                [score[k * tok : (k + 1) * tok] + bias_rows[k] for k in range(len(bias_rows))], axis=0
            )
            weight = jnp.exp2(score - jnp.max(score, axis=0, keepdims=True)).astype(BF16)
            mixed = dot(jnp.concatenate([vbuf[cols, keys], ones], axis=0), weight)
            total = 1.0 / mixed[2 * HD : 2 * HD + 1, :]
            top = mixed[:HD, :LANES] * total[:, :LANES]
            bottom = mixed[HD : 2 * HD, LANES:] * total[:, LANES:]
            att[cols, lanes] = jnp.concatenate([top, bottom], axis=0).astype(BF16)
        return carry

    blocks = query_lanes // LANES
    if blocks == 1:
        block(0, 0)
    else:
        lax.fori_loop(0, blocks, block, 0)
    mixed = dot(wo_ref[...], att[...])
    partial = mixed[:channels] + mixed[channels:]
    if step < STEPS - 1:
        tbuf[...] = jnp.zeros_like(tbuf)
        tbuf[pl.ds(pl.multiple_of(tok_index * part_rows, 8), part_rows), :] = fresh_ref[step + 1]
        fresh_t = tbuf[...].T
        fresh_t = jnp.concatenate([fresh_t] * n_query, axis=1)
        slot = lax.broadcasted_iota(jnp.int32, (1, query_lanes), 1) // tok + first_key + HALO
        partial = jnp.where(slot == -1, fresh_t, partial)
    part_ref[...] = partial[:, : part_ref.shape[1]]


def last_kernel(cfg, *refs):
    tok, frames, channels, base, depth, level_count, heads, part_rows = cfg
    g_ref, hpart_ref, xq_ref = refs[:3]
    own = refs[3 : 3 + STEPS - 1]
    velocity_ref, queue_ref, tbuf = refs[3 + STEPS - 1 :]
    tok_index = lax.axis_index("tok")
    velocity, moved = advance(level_count, tok, None, g_ref, hpart_ref, xq_ref)
    for s in range(STEPS - 1):
        velocity_ref[s, 0] = own[s][...]
    velocity_ref[STEPS - 1, 0] = own_rows(velocity[:, :tok], tok, part_rows, tok_index, tbuf)
    queue_ref[0] = own_rows(moved[:, :tok], tok, part_rows, tok_index, tbuf)


def body(
    latent,
    fresh_noise,
    frame_slot,
    frame_reach,
    level_embed,
    embed_weight,
    qkv_weight,
    qk_gain,
    out_weight,
    vel_weight,
):
    frames, parts = lax.axis_size("queue"), lax.axis_size("tok")
    position = lax.axis_index("queue")
    part_rows, channels = latent.shape[1], latent.shape[2]
    tok = part_rows * parts
    level_count = level_embed.shape[0]
    depth = qkv_weight.shape[2]
    width = qkv_weight.shape[1]
    spare = round_up(width, 2 * LANES) - width
    if spare:
        qkv_weight = jnp.pad(qkv_weight, ((0, 0), (0, spare), (0, 0)))
        qk_gain = jnp.pad(qk_gain, ((0, 0), (0, spare)))
        out_weight = jnp.pad(out_weight, ((0, spare), (0, 0)))
        width += spare
    heads = width // HD
    base = round_up(channels + level_count, LANES)
    cfg = (tok, frames, channels, base, depth, level_count, heads, part_rows)
    vmem, smem, anywhere = (
        pl.BlockSpec(memory_space=pltpu.VMEM),
        pl.BlockSpec(memory_space=pltpu.SMEM),
        pl.BlockSpec(memory_space=pl.ANY),
    )
    shape = jax.ShapeDtypeStruct

    sent = jnp.where(position == frames - 1, fresh_noise[0], latent[0])
    latents = lax.all_gather(sent, ("queue", "tok"), axis=0, tiled=True)

    filler = jnp.zeros((base - channels - level_count, embed_weight.shape[1]), BF16)
    table = jnp.concatenate([embed_weight, level_embed, filler, vel_weight.T], axis=0)
    table = lax.all_gather(table, "tok", axis=0, tiled=False)

    rows = 256
    chunks = 4 * width // rows
    mq, mk, mv, wo, gram = pl.pallas_call(
        functools.partial(weights_kernel, rows, base),
        out_shape=(
            shape((width, 2 * base), BF16),
            shape((2 * base, width), BF16),
            shape((width, 2 * base), BF16),
            shape((2 * channels, width), BF16),
            shape((base + channels, 2 * base), BF16),
        ),
        in_specs=[vmem, anywhere, anywhere],
        out_specs=(vmem,) * 5,
        scratch_shapes=[
            pltpu.VMEM((chunks, rows, depth), BF16),
            pltpu.SemaphoreType.DMA((chunks,)),
        ],
        compiler_params=pltpu.CompilerParams(vmem_limit_bytes=40 * 2**20),
        cost_estimate=pl.CostEstimate(
            flops=2 * base * 4 * width * depth, bytes_accessed=8 * width * depth, transcendentals=0
        ),
        name="weights",
    )(table, qkv_weight, out_weight)

    query_block = max(1, LANES // tok)
    owned = []
    for step in range(STEPS):
        n_query = query_block + 2 * HALO * (STEPS - 1 - step)
        query_lanes, key_lanes = n_query * tok, (n_query + 2 * HALO) * tok
        args = [frame_slot, frame_reach]
        specs = [smem, smem]
        if step == 0:
            args += [latents]
            specs += [vmem]
        else:
            args += [gathered, hpart, xq]
            specs += [vmem] * 3
        if step < STEPS - 1:
            args += [fresh_noise]
            specs += [vmem]
        args += [qk_gain, mq, mk, mv, wo, gram]
        specs += [vmem] * 6
        outs = [shape((channels, query_lanes), F32)] * 3
        if step > 0:
            outs += [shape((part_rows, channels), F32)]
        window = (2 * HALO + query_block) * tok
        result = pl.pallas_call(
            functools.partial(step_kernel, step, cfg),
            out_shape=tuple(outs),
            in_specs=specs,
            out_specs=(vmem,) * len(outs),
            scratch_shapes=[
                pltpu.VMEM((key_lanes, width), BF16),
                pltpu.VMEM((width, key_lanes), BF16),
                pltpu.VMEM((width, query_lanes), BF16),
                pltpu.VMEM((width, query_lanes), BF16),
                pltpu.VMEM((tok, channels), F32),
            ],
            compiler_params=pltpu.CompilerParams(vmem_limit_bytes=48 * 2**20),
            cost_estimate=pl.CostEstimate(
                flops=4 * query_lanes * window * width + 12 * key_lanes * base * width,
                bytes_accessed=8 * width * base,
                transcendentals=query_lanes * window * heads,
            ),
            name="step%d" % step,
        )(*args)
        part, hpart, xq = result[:3]
        owned += list(result[3:])
        gathered = lax.all_gather(part, "tok", axis=0, tiled=False)

    return tuple(
        pl.pallas_call(
            functools.partial(last_kernel, cfg),
            out_shape=(
                shape((STEPS, 1, part_rows, channels), F32),
                shape((1, part_rows, channels), F32),
            ),
            in_specs=[vmem] * (3 + len(owned)),
            out_specs=(vmem, vmem),
            scratch_shapes=[pltpu.VMEM((tok, channels), F32)],
            name="last",
        )(gathered, hpart, xq, *owned)
    )


def solution(mesh):
    return jax.shard_map(
        body,
        mesh=mesh,
        in_specs=(
            P("queue", "tok", None),
            P(None, "tok", None),
            P(),
            P(),
            P(None, "tok"),
            P(None, "tok"),
            P(None, "tok", None),
            P(None, "tok"),
            P("tok", None),
            P("tok", None),
        ),
        out_specs=(P(None, "queue", "tok", None), P("queue", "tok", None)),
        check_vma=False,
    )
```

```python
import functools
import math

import jax
import jax.numpy as jnp
from jax import lax
from jax.experimental import pallas as pl
from jax.experimental.pallas import tpu as pltpu
from jax.sharding import PartitionSpec as P

HD = 64
STEPS = 3
HALO = 3
LANES = 128
EPS = 1e-06
F32, BF16 = jnp.float32, jnp.bfloat16


def round_up(value, unit):
    return -(-value // unit) * unit


def dot(a, b):
    return jnp.dot(a, b, preferred_element_type=F32)


def dot_nt(a, b):
    return lax.dot_general(a, b, (((1,), (1,)), ((), ())), preferred_element_type=F32)


def halves(value, axis):
    high = value.astype(BF16)
    low = (value - high.astype(F32)).astype(BF16)
    return jnp.concatenate([high, low], axis=axis)


def table_kernel(channels, embed_ref, level_ref, vel_ref, out_ref):
    count, base = level_ref.shape[0], out_ref.shape[0] - vel_ref.shape[0]
    out_ref[:channels] = embed_ref[...]
    filler = jnp.zeros((base - channels - count, out_ref.shape[1]), F32)
    out_ref[channels:base] = jnp.concatenate([level_ref[...].astype(F32), filler], axis=0).astype(BF16)
    out_ref[base:] = vel_ref[...]


def start_chunks(rows, parts, qkv_hbm, out_hbm, buf, sems):
    per = out_hbm.shape[0] // rows
    depth = buf.shape[-1]
    index, count = lax.axis_index("tok"), lax.axis_size("tok")
    copies = []
    for chunk in range(4 * per):
        source = qkv_hbm.at[chunk // per] if chunk < 3 * per else out_hbm
        for at, part in enumerate(parts):
            columns = pl.ds(pl.multiple_of(lax.rem(index + part, count) * depth, LANES), depth)
            copy = pltpu.make_async_copy(
                source.at[pl.ds((chunk % per) * rows, rows), columns],
                buf.at[at, chunk],
                sems.at[at, chunk],
            )
            copy.start()
            copies.append(copy)
    return copies


def turned(table):
    return table.astype(F32).T.astype(BF16)


def own_weights_kernel(rows, base, g_ref, qkv_hbm, out_hbm, acc_ref, wo_ref, gram_ref, buf, sems):
    copies = start_chunks(rows, (0,), qkv_hbm, out_hbm, buf, sems)
    per = out_hbm.shape[0] // rows
    right = turned(g_ref[...])
    gram_ref[...] = dot(g_ref[...], right[:, :base])
    for chunk in range(4 * per):
        copies[chunk].wait()
        if chunk < 3 * per:
            acc_ref[chunk * rows : (chunk + 1) * rows, :] = dot(buf[0, chunk], right[:, :base])
        else:
            at = (chunk - 3 * per) * rows
            wo_ref[at : at + rows, :] = dot(buf[0, chunk], right[:, base:])


def other_weights_kernel(rows, base, count, *refs):
    tables, refs = refs[: count - 1], refs[count - 1 :]
    acc_ref, wo_acc, gram_acc, qkv_hbm, out_hbm, mq_ref, mk_ref, mv_ref, wo_ref, gram_ref, buf, sems = refs
    copies = start_chunks(rows, range(1, count), qkv_hbm, out_hbm, buf, sems)
    per = out_hbm.shape[0] // rows
    rights = [turned(table[...]) for table in tables]
    gram = gram_acc[...]
    for table, right in zip(tables, rights):
        gram = gram + dot(table[...], right[:, :base])
    gram_ref[...] = halves(gram, 1)
    for chunk in range(4 * per):
        for at in range(count - 1):
            copies[chunk * (count - 1) + at].wait()
        kind = chunk // per
        where = pl.ds((chunk % per) * rows, rows)
        if kind < 3:
            total = acc_ref[chunk * rows : (chunk + 1) * rows, :]
        else:
            total = wo_acc[where, :]
        for at, right in enumerate(rights):
            total = total + dot(buf[at, chunk], right[:, :base] if kind < 3 else right[:, base:])
        if kind == 0:
            mq_ref[where, :] = halves(total, 1)
        elif kind == 1:
            mk_ref[:, where] = halves(total.T, 0)
        elif kind == 2:
            mv_ref[where, :] = halves(total, 1)
        else:
            wo_ref[:, where] = halves(total.T, 0)


def advance(level_count, tok, first, g_ref, hpart_ref, xq_ref):
    shared = g_ref[0]
    for t in range(1, g_ref.shape[0]):
        shared = shared + g_ref[t]
    velocity = shared + hpart_ref[...]
    moved = xq_ref[...] - velocity * (1.0 / level_count)
    if first is None:
        return velocity, moved
    lane_frame = lax.broadcasted_iota(jnp.int32, (1, shared.shape[1]), 1) // tok
    return velocity, jnp.where(lane_frame + first == -1, shared, moved)


def own_rows(block, tok, part_rows, index, scratch):
    scratch[...] = block.T
    return scratch[pl.ds(pl.multiple_of(index * part_rows, 8), part_rows), :]


def step_kernel(step, cfg, *refs):
    tok, frames, channels, base, depth, level_count, heads, part_rows = cfg
    query_block = max(1, LANES // tok)
    n_query = query_block + 2 * HALO * (STEPS - 1 - step)
    n_key = n_query + 2 * HALO
    key_lanes, query_lanes = n_key * tok, n_query * tok
    width = heads * HD
    window = (2 * HALO + query_block) * tok
    position, tok_index = lax.axis_index("queue"), lax.axis_index("tok")
    first_key = position - HALO - (HALO + 1) * (STEPS - 1 - step)
    refs = list(refs)
    slot_ref, reach_ref = refs[0], refs[1]
    if step == 0:
        lat_ref = refs[2]
        refs = refs[3:]
    else:
        g_ref, hprev_ref, xprev_ref = refs[2:5]
        refs = refs[5:]
    fresh_ref = None
    if step < STEPS - 1:
        fresh_ref = refs.pop(0)
    gain_ref, mq_ref, mk_ref, mv_ref, wo_ref, gram_ref = refs[:6]
    refs = refs[6:]
    part_ref, hpart_ref, xq_ref = refs[:3]
    refs = refs[3:]
    own_ref = None
    if step > 0:
        own_ref = refs.pop(0)
    kbuf, vbuf, qbuf, att, tbuf = refs

    if step == 0:
        pieces = []
        for w in range(n_key):
            source = lax.rem(first_key - 1 + w + 2 * frames, frames)
            pieces += [lat_ref[source, t, 0] for t in range(tok // part_rows)]
        state = jnp.concatenate(pieces, axis=0).T
    else:
        velocity, state = advance(level_count, tok, first_key - 1, g_ref, hprev_ref, xprev_ref)
        mine = (HALO + 1) * (STEPS - step)
        own_ref[...] = own_rows(velocity[:, mine * tok : (mine + 1) * tok], tok, part_rows, tok_index, tbuf)

    key_frame = lax.broadcasted_iota(jnp.int32, (1, key_lanes), 1) // tok
    level_row = jnp.full((1, key_lanes), -1, jnp.int32)
    for w in range(n_key):
        frame = first_key + w
        known = slot_ref[jnp.clip(frame - step - 1, 0, frames - 1)] + step
        level_row = jnp.where(key_frame == w, jnp.where(frame >= step + 1, known, frame), level_row)
    row = lax.broadcasted_iota(jnp.int32, (base - channels, key_lanes), 0)
    aug_t = jnp.concatenate([state, jnp.where(row == level_row, 1.0, 0.0)], axis=0)
    aug_t = aug_t.astype(BF16).astype(F32)
    aug = aug_t.T
    aug_b, aug_tb = aug.astype(BF16), aug_t.astype(BF16)
    aug_q = aug_t[:, HALO * tok : HALO * tok + query_lanes]
    aug_qb = aug_q.astype(BF16)
    both = jnp.concatenate([aug_b, aug_b], axis=1)
    both_t = jnp.concatenate([aug_tb, aug_tb], axis=0)
    both_q = jnp.concatenate([aug_qb, aug_qb], axis=0)
    gram = gram_ref[:base, :]
    mean_t = jnp.sum(dot(gram, both_t) * aug_t, axis=0, keepdims=True) * (1.0 / depth)
    mean_q = jnp.sum(dot(gram, both_q) * aug_q, axis=0, keepdims=True) * (1.0 / depth)
    mean_c = jnp.sum(dot_nt(both, gram) * aug, axis=1, keepdims=True) * (1.0 / depth)
    mean_t, mean_q, mean_c = (jnp.maximum(m, 0.0) + EPS for m in (mean_t, mean_q, mean_c))

    hpart_ref[...] = dot(gram_ref[base:, :], both_q)
    xq_ref[...] = state[:, HALO * tok : HALO * tok + query_lanes]

    gain = gain_ref[0:1, :] * gain_ref[1:2, :] * (HD ** -0.5 * math.log2(math.e))
    span = 256 if width % 256 == 0 else 128
    head_of = lambda axis: lax.broadcasted_iota(jnp.int32, (span, span), axis) // HD
    average = jnp.where(head_of(0) == head_of(1), 1.0 / HD, 0.0).astype(BF16)
    for at in range(0, width, span):
        raw = dot(both, mk_ref[:, at : at + span])
        spread = dot((raw * raw).astype(BF16), average)
        kbuf[:, at : at + span] = (raw * lax.rsqrt(spread + EPS * mean_c) * gain[:, at : at + span]).astype(BF16)
    vbuf[...] = (dot(mv_ref[...], both_t) * lax.rsqrt(mean_t)).astype(BF16)
    raw = dot(mq_ref[...], both_q).reshape(heads, HD, query_lanes)
    spread = jnp.sum(raw * raw, axis=1, keepdims=True) * (1.0 / HD)
    qbuf[...] = (raw * lax.rsqrt(spread + EPS * mean_q)[:, :, :]).reshape(width, query_lanes).astype(BF16)

    def block(b, carry):
        lead = (b * LANES) // tok
        keys = pl.ds(pl.multiple_of(lead * tok, LANES), window)
        lanes = pl.ds(pl.multiple_of(b * LANES, LANES), LANES)
        lane = lax.broadcasted_iota(jnp.int32, (1, 2 * LANES), 1)
        within = lax.rem(lane, LANES) // tok
        bias_rows = []
        reach = []
        for j in range(query_block):
            frame = first_key + HALO + lead + j
            reach.append(reach_ref[jnp.clip(frame, 0, frames - 1)])
        for k in range(2 * HALO + query_block):
            target = first_key + lead + k
            inside = (target >= 0) & (target < frames)
            bias = jnp.zeros((1, 2 * LANES), F32)
            for j in range(query_block):
                counted = inside & (abs(k - HALO - j) <= reach[j])
                value = jnp.where(counted, 0.0, -1e30)
                bias = jnp.where(within == j, value, bias) if query_block > 1 else bias + value
            bias_rows.append(bias)
        ones = jnp.ones((16, window), BF16)
        upper = lax.broadcasted_iota(jnp.int32, (2 * HD, LANES), 0) < HD
        for pair in range(heads // 2):
            cols = slice(pair * 2 * HD, (pair + 1) * 2 * HD)
            query = qbuf[cols, lanes]
            zero = jnp.zeros_like(query)
            query = jnp.concatenate([jnp.where(upper, query, zero), jnp.where(upper, zero, query)], axis=1)
            score = dot(kbuf[keys, cols], query)
            score = jnp.concatenate(
                [score[k * tok : (k + 1) * tok] + bias_rows[k] for k in range(len(bias_rows))], axis=0
            )
            weight = jnp.exp2(score - jnp.max(score, axis=0, keepdims=True)).astype(BF16)
            mixed = dot(jnp.concatenate([vbuf[cols, keys], ones], axis=0), weight)
            total = 1.0 / mixed[2 * HD : 2 * HD + 1, :]
            top = mixed[:HD, :LANES] * total[:, :LANES]
            bottom = mixed[HD : 2 * HD, LANES:] * total[:, LANES:]
            att[cols, lanes] = jnp.concatenate([top, bottom], axis=0).astype(BF16)
        return carry

    blocks = query_lanes // LANES
    if blocks == 1:
        block(0, 0)
    else:
        lax.fori_loop(0, blocks, block, 0)
    mixed = dot(wo_ref[...], att[...])
    partial = mixed[:channels] + mixed[channels:]
    if step < STEPS - 1:
        tbuf[...] = jnp.zeros_like(tbuf)
        tbuf[pl.ds(pl.multiple_of(tok_index * part_rows, 8), part_rows), :] = fresh_ref[step + 1]
        fresh_t = tbuf[...].T
        fresh_t = jnp.concatenate([fresh_t] * n_query, axis=1)
        slot = lax.broadcasted_iota(jnp.int32, (1, query_lanes), 1) // tok + first_key + HALO
        partial = jnp.where(slot == -1, fresh_t, partial)
    part_ref[...] = partial[:, : part_ref.shape[1]]


def last_kernel(cfg, *refs):
    tok, frames, channels, base, depth, level_count, heads, part_rows = cfg
    g_ref, hpart_ref, xq_ref = refs[:3]
    own = refs[3 : 3 + STEPS - 1]
    velocity_ref, queue_ref, tbuf = refs[3 + STEPS - 1 :]
    tok_index = lax.axis_index("tok")
    velocity, moved = advance(level_count, tok, None, g_ref, hpart_ref, xq_ref)
    for s in range(STEPS - 1):
        velocity_ref[s, 0] = own[s][...]
    velocity_ref[STEPS - 1, 0] = own_rows(velocity[:, :tok], tok, part_rows, tok_index, tbuf)
    queue_ref[0] = own_rows(moved[:, :tok], tok, part_rows, tok_index, tbuf)


def body(
    latent,
    fresh_noise,
    frame_slot,
    frame_reach,
    level_embed,
    embed_weight,
    qkv_weight,
    qk_gain,
    out_weight,
    vel_weight,
):
    frames, parts = lax.axis_size("queue"), lax.axis_size("tok")
    position = lax.axis_index("queue")
    part_rows, channels = latent.shape[1], latent.shape[2]
    tok = part_rows * parts
    level_count = level_embed.shape[0]
    depth = qkv_weight.shape[2]
    width = qkv_weight.shape[1]
    spare = round_up(width, 2 * LANES) - width
    if spare:
        qkv_weight = jnp.pad(qkv_weight, ((0, 0), (0, spare), (0, 0)))
        qk_gain = jnp.pad(qk_gain, ((0, 0), (0, spare)))
        out_weight = jnp.pad(out_weight, ((0, spare), (0, 0)))
        width += spare
    heads = width // HD
    base = round_up(channels + level_count, LANES)
    cfg = (tok, frames, channels, base, depth, level_count, heads, part_rows)
    vmem, smem, hbm = (
        pl.BlockSpec(memory_space=pltpu.VMEM),
        pl.BlockSpec(memory_space=pltpu.SMEM),
        pl.BlockSpec(memory_space=pltpu.HBM),
    )
    shape = jax.ShapeDtypeStruct

    sent = jnp.where(position == frames - 1, fresh_noise[0], latent[0])[None]
    if frames * tok * channels < 2**18 + 1:
        sent = jnp.concatenate([sent, fresh_noise], axis=0)
    latents = lax.all_gather(sent.reshape(-1, channels), ("queue", "tok"), axis=0, tiled=True)
    latents = latents.reshape(frames, parts, -1, part_rows, channels)

    share = depth // parts
    table = pl.pallas_call(
        functools.partial(table_kernel, channels),
        out_shape=shape((base + channels, share), BF16),
        in_specs=[vmem] * 3,
        out_specs=vmem,
        name="table",
    )(embed_weight, level_embed, vel_weight.T)
    tables = [
        lax.ppermute(table, "tok", [(source, (source - k) % parts) for source in range(parts)])
        for k in range(1, parts)
    ]

    rows = 384 if width % 384 == 0 else 256
    chunks = 4 * width // rows
    limit = pltpu.CompilerParams(vmem_limit_bytes=40 * 2**20)

    def estimate(share_count):
        return pl.CostEstimate(
            flops=8 * base * width * share * share_count,
            bytes_accessed=8 * width * share * share_count,
            transcendentals=0,
        )

    sums = pl.pallas_call(
        functools.partial(own_weights_kernel, rows, base),
        out_shape=(
            shape((3 * width, base), F32),
            shape((width, channels), F32),
            shape((base + channels, base), F32),
        ),
        in_specs=[vmem, hbm, hbm],
        out_specs=(vmem,) * 3,
        scratch_shapes=[
            pltpu.VMEM((1, chunks, rows, share), BF16),
            pltpu.SemaphoreType.DMA((1, chunks)),
        ],
        compiler_params=limit,
        cost_estimate=estimate(1),
        name="own_weights",
    )(table, qkv_weight, out_weight)
    mq, mk, mv, wo, gram = pl.pallas_call(
        functools.partial(other_weights_kernel, rows, base, parts),
        out_shape=(
            shape((width, 2 * base), BF16),
            shape((2 * base, width), BF16),
            shape((width, 2 * base), BF16),
            shape((2 * channels, width), BF16),
            shape((base + channels, 2 * base), BF16),
        ),
        in_specs=[vmem] * (parts + 2) + [hbm, hbm],
        out_specs=(vmem,) * 5,
        scratch_shapes=[
            pltpu.VMEM((parts - 1, chunks, rows, share), BF16),
            pltpu.SemaphoreType.DMA((parts - 1, chunks)),
        ],
        compiler_params=limit,
        cost_estimate=estimate(parts - 1),
        name="other_weights",
    )(*tables, *sums, qkv_weight, out_weight)

    query_block = max(1, LANES // tok)
    owned = []
    for step in range(STEPS):
        n_query = query_block + 2 * HALO * (STEPS - 1 - step)
        query_lanes, key_lanes = n_query * tok, (n_query + 2 * HALO) * tok
        args = [frame_slot, frame_reach]
        specs = [smem, smem]
        if step == 0:
            args += [latents]
            specs += [vmem]
        else:
            args += [gathered, hpart, xq]
            specs += [vmem] * 3
        if step < STEPS - 1:
            args += [fresh_noise]
            specs += [vmem]
        args += [qk_gain, mq, mk, mv, wo, gram]
        specs += [vmem] * 6
        outs = [shape((channels, query_lanes), F32)] * 3
        if step > 0:
            outs += [shape((part_rows, channels), F32)]
        window = (2 * HALO + query_block) * tok
        result = pl.pallas_call(
            functools.partial(step_kernel, step, cfg),
            out_shape=tuple(outs),
            in_specs=specs,
            out_specs=(vmem,) * len(outs),
            scratch_shapes=[
                pltpu.VMEM((key_lanes, width), BF16),
                pltpu.VMEM((width, key_lanes), BF16),
                pltpu.VMEM((width, query_lanes), BF16),
                pltpu.VMEM((width, query_lanes), BF16),
                pltpu.VMEM((tok, channels), F32),
            ],
            compiler_params=pltpu.CompilerParams(vmem_limit_bytes=48 * 2**20),
            cost_estimate=pl.CostEstimate(
                flops=4 * query_lanes * window * width + 12 * key_lanes * base * width,
                bytes_accessed=8 * width * base,
                transcendentals=query_lanes * window * heads,
            ),
            name="step%d" % step,
        )(*args)
        part, hpart, xq = result[:3]
        owned += list(result[3:])
        gathered = lax.all_gather(part, "tok", axis=0, tiled=False)

    return tuple(
        pl.pallas_call(
            functools.partial(last_kernel, cfg),
            out_shape=(
                shape((STEPS, 1, part_rows, channels), F32),
                shape((1, part_rows, channels), F32),
            ),
            in_specs=[vmem] * (3 + len(owned)),
            out_specs=(vmem, vmem),
            scratch_shapes=[pltpu.VMEM((tok, channels), F32)],
            name="last",
        )(gathered, hpart, xq, *owned)
    )


def solution(mesh):
    return jax.shard_map(
        body,
        mesh=mesh,
        in_specs=(
            P("queue", "tok", None),
            P(None, "tok", None),
            P(),
            P(),
            P(None, "tok"),
            P(None, "tok"),
            P(None, "tok", None),
            P(None, "tok"),
            P("tok", None),
            P("tok", None),
        ),
        out_specs=(P(None, "queue", "tok", None), P("queue", "tok", None)),
        check_vma=False,
    )
```

```python
import functools
import math

import jax
import jax.numpy as jnp
from jax import lax
from jax.experimental import pallas as pl
from jax.experimental.pallas import tpu as pltpu
from jax.sharding import PartitionSpec as P

HD = 64
STEPS = 3
HALO = 3
LANES = 128
EPS = 1e-06
F32, BF16 = jnp.float32, jnp.bfloat16


def round_up(value, unit):
    return -(-value // unit) * unit


def dot(a, b):
    return jnp.dot(a, b, preferred_element_type=F32)


def dot_nt(a, b):
    return lax.dot_general(a, b, (((1,), (1,)), ((), ())), preferred_element_type=F32)


def halves(value, axis):
    high = value.astype(BF16)
    low = (value - high.astype(F32)).astype(BF16)
    return jnp.concatenate([high, low], axis=axis)


def start_chunks(rows, chunks, parts, qkv_hbm, out_hbm, buf, sems):
    per = out_hbm.shape[0] // rows
    depth = buf.shape[-1]
    index, count = lax.axis_index("tok"), lax.axis_size("tok")
    copies = []
    for place, chunk in enumerate(chunks):
        source = qkv_hbm.at[chunk // per] if chunk < 3 * per else out_hbm
        for at, part in enumerate(parts):
            columns = pl.ds(pl.multiple_of(lax.rem(index + part, count) * depth, LANES), depth)
            copy = pltpu.make_async_copy(
                source.at[pl.ds((chunk % per) * rows, rows), columns],
                buf.at[at, place],
                sems.at[at, place],
            )
            copy.start()
            copies.append(copy)
    return copies


def stack_rows(base, embed_ref, level_ref):
    filler = base - embed_ref.shape[0] - level_ref.shape[0]
    rows = [embed_ref[...].astype(F32), level_ref[...].astype(F32)]
    return jnp.concatenate(rows + [jnp.zeros((filler, embed_ref.shape[1]), F32)], axis=0)


def turned(base, embed_ref, level_ref, vel_ref):
    left = stack_rows(base, embed_ref, level_ref)
    return left.astype(BF16), left.T.astype(BF16), vel_ref[...].astype(F32).T.astype(BF16)


def own_weights_kernel(rows, base, *refs):
    qkv_hbm, out_hbm, acc_ref, wo_ref, gram_ref, gv_ref, buf, sems = refs[3:]
    per = out_hbm.shape[0] // rows
    copies = start_chunks(rows, range(4 * per), (0,), qkv_hbm, out_hbm, buf, sems)
    left, right, vel = turned(base, *refs[:3])
    gram_ref[...] = dot(left, right)
    gv_ref[...] = dot(refs[2][...], right)
    for chunk in range(4 * per):
        copies[chunk].wait()
        if chunk < 3 * per:
            acc_ref[chunk * rows : (chunk + 1) * rows, :] = dot(buf[0, chunk], right)
        else:
            at = (chunk - 3 * per) * rows
            wo_ref[at : at + rows, :] = dot(buf[0, chunk], vel)


def other_weights_kernel(rows, base, count, second, *refs):
    tables, refs = refs[: 3 * (count - 1)], refs[3 * (count - 1) :]
    acc_ref, wo_acc, gram_acc, gv_acc, qkv_hbm, out_hbm, _ = refs[:7]
    outs, buf, sems = refs[7:-2], refs[-2], refs[-1]
    per = out_hbm.shape[0] // rows
    chunks = range(2 * per, 4 * per) if second else range(2 * per)
    copies = start_chunks(rows, chunks, range(1, count), qkv_hbm, out_hbm, buf, sems)
    rights = [turned(base, *tables[3 * at : 3 * at + 3]) for at in range(count - 1)]
    if second:
        gram, gv = gram_acc[...], gv_acc[...]
        for at, (left, right, _) in enumerate(rights):
            gram = gram + dot(left, right)
            gv = gv + dot(tables[3 * at + 2][...], right)
        outs[2][:base] = halves(gram, 1)
        outs[2][base:] = halves(gv, 1)
    for place, chunk in enumerate(chunks):
        for at in range(count - 1):
            copies[place * (count - 1) + at].wait()
        kind = chunk // per
        where = pl.ds((chunk % per) * rows, rows)
        if kind < 3:
            total = acc_ref[chunk * rows : (chunk + 1) * rows, :]
        else:
            total = wo_acc[where, :]
        for at, (_, right, vel) in enumerate(rights):
            total = total + dot(buf[at, place], right if kind < 3 else vel)
        if kind % 2:
            outs[1][:, where] = halves(total.T, 0)
        else:
            outs[0][where, :] = halves(total, 1)


def advance(level_count, tok, first, g_ref, hpart_ref, xq_ref):
    shared = g_ref[0]
    for t in range(1, g_ref.shape[0]):
        shared = shared + g_ref[t]
    velocity = shared + hpart_ref[...]
    moved = xq_ref[...] - velocity * (1.0 / level_count)
    if first is None:
        return velocity, moved
    lane_frame = lax.broadcasted_iota(jnp.int32, (1, shared.shape[1]), 1) // tok
    return velocity, jnp.where(lane_frame + first == -1, shared, moved)


def own_rows(block, tok, part_rows, index, scratch):
    scratch[...] = block.T
    return scratch[pl.ds(pl.multiple_of(index * part_rows, 8), part_rows), :]


def step_kernel(step, cfg, *refs):
    tok, frames, channels, base, depth, level_count, heads, part_rows = cfg
    query_block = max(1, LANES // tok)
    n_query = query_block + 2 * HALO * (STEPS - 1 - step)
    n_key = n_query + 2 * HALO
    key_lanes, query_lanes = n_key * tok, n_query * tok
    width = heads * HD
    window = (2 * HALO + query_block) * tok
    position, tok_index = lax.axis_index("queue"), lax.axis_index("tok")
    first_key = position - HALO - (HALO + 1) * (STEPS - 1 - step)
    refs = list(refs)
    slot_ref, reach_ref = refs[0], refs[1]
    if step == 0:
        count = tok // part_rows
        lat_refs = refs[2 : 2 + count]
        refs = refs[2 + count :]
    else:
        g_ref, hprev_ref, xprev_ref = refs[2:5]
        refs = refs[5:]
    fresh_ref = None
    if step < STEPS - 1:
        fresh_ref = refs.pop(0)
    gain_ref, mq_ref, mk_ref, mv_ref, wo_ref, gram_ref = refs[:6]
    refs = refs[6:]
    part_ref, hpart_ref, xq_ref = refs[:3]
    refs = refs[3:]
    own_ref = None
    if step > 0:
        own_ref = refs.pop(0)
    kbuf, vbuf, qbuf, att, tbuf, xbuf = refs

    if step == 0:
        for w in range(n_key):
            source = lax.rem(first_key - 1 + w + 2 * frames, frames)
            for t in range(count):
                at = lax.rem(tok_index + t, count) * part_rows + w * tok
                xbuf[pl.ds(pl.multiple_of(at, 8), part_rows), :] = lat_refs[t][position ^ source]
        state = xbuf[...].T
    else:
        velocity, state = advance(level_count, tok, first_key - 1, g_ref, hprev_ref, xprev_ref)
        mine = (HALO + 1) * (STEPS - step)
        own_ref[...] = own_rows(velocity[:, mine * tok : (mine + 1) * tok], tok, part_rows, tok_index, tbuf)

    key_frame = lax.broadcasted_iota(jnp.int32, (1, key_lanes), 1) // tok
    level_row = jnp.full((1, key_lanes), -1, jnp.int32)
    for w in range(n_key):
        frame = first_key + w
        known = slot_ref[jnp.clip(frame - step - 1, 0, frames - 1)] + step
        level_row = jnp.where(key_frame == w, jnp.where(frame >= step + 1, known, frame), level_row)
    row = lax.broadcasted_iota(jnp.int32, (base - channels, key_lanes), 0)
    aug_t = jnp.concatenate([state, jnp.where(row == level_row, 1.0, 0.0)], axis=0)
    aug_t = aug_t.astype(BF16).astype(F32)
    aug = aug_t.T
    aug_b, aug_tb = aug.astype(BF16), aug_t.astype(BF16)
    aug_q = aug_t[:, HALO * tok : HALO * tok + query_lanes]
    aug_qb = aug_q.astype(BF16)
    both = jnp.concatenate([aug_b, aug_b], axis=1)
    both_t = jnp.concatenate([aug_tb, aug_tb], axis=0)
    both_q = jnp.concatenate([aug_qb, aug_qb], axis=0)
    gram = gram_ref[:base, :]
    mean_t = jnp.sum(dot(gram, both_t) * aug_t, axis=0, keepdims=True) * (1.0 / depth)
    mean_q = jnp.sum(dot(gram, both_q) * aug_q, axis=0, keepdims=True) * (1.0 / depth)
    mean_c = jnp.sum(dot_nt(both, gram) * aug, axis=1, keepdims=True) * (1.0 / depth)
    mean_t, mean_q, mean_c = (jnp.maximum(m, 0.0) + EPS for m in (mean_t, mean_q, mean_c))

    hpart_ref[...] = dot(gram_ref[base:, :], both_q)
    xq_ref[...] = state[:, HALO * tok : HALO * tok + query_lanes]

    gain = gain_ref[0:1, :] * gain_ref[1:2, :] * (HD ** -0.5 * math.log2(math.e))
    span = 256 if width % 256 == 0 else 128
    head_of = lambda axis: lax.broadcasted_iota(jnp.int32, (span, span), axis) // HD
    average = jnp.where(head_of(0) == head_of(1), 1.0 / HD, 0.0).astype(BF16)
    for at in range(0, width, span):
        raw = dot(both, mk_ref[:, at : at + span])
        spread = dot((raw * raw).astype(BF16), average)
        kbuf[:, at : at + span] = (raw * lax.rsqrt(spread + EPS * mean_c) * gain[:, at : at + span]).astype(BF16)
    vbuf[...] = (dot(mv_ref[...], both_t) * lax.rsqrt(mean_t)).astype(BF16)
    raw = dot(mq_ref[...], both_q).reshape(heads, HD, query_lanes)
    spread = jnp.sum(raw * raw, axis=1, keepdims=True) * (1.0 / HD)
    qbuf[...] = (raw * lax.rsqrt(spread + EPS * mean_q)[:, :, :]).reshape(width, query_lanes).astype(BF16)

    def block(b, carry):
        lead = (b * LANES) // tok
        keys = pl.ds(pl.multiple_of(lead * tok, LANES), window)
        lanes = pl.ds(pl.multiple_of(b * LANES, LANES), LANES)
        lane = lax.broadcasted_iota(jnp.int32, (1, 2 * LANES), 1)
        within = lax.rem(lane, LANES) // tok
        bias_rows = []
        reach = []
        for j in range(query_block):
            frame = first_key + HALO + lead + j
            reach.append(reach_ref[jnp.clip(frame, 0, frames - 1)])
        for k in range(2 * HALO + query_block):
            target = first_key + lead + k
            inside = (target >= 0) & (target < frames)
            bias = jnp.zeros((1, 2 * LANES), F32)
            for j in range(query_block):
                counted = inside & (abs(k - HALO - j) <= reach[j])
                value = jnp.where(counted, 0.0, -1e30)
                bias = jnp.where(within == j, value, bias) if query_block > 1 else bias + value
            bias_rows.append(bias)
        ones = jnp.ones((16, window), BF16)
        upper = lax.broadcasted_iota(jnp.int32, (2 * HD, LANES), 0) < HD
        for pair in range(heads // 2):
            cols = slice(pair * 2 * HD, (pair + 1) * 2 * HD)
            query = qbuf[cols, lanes]
            zero = jnp.zeros_like(query)
            query = jnp.concatenate([jnp.where(upper, query, zero), jnp.where(upper, zero, query)], axis=1)
            score = dot(kbuf[keys, cols], query)
            score = jnp.concatenate(
                [score[k * tok : (k + 1) * tok] + bias_rows[k] for k in range(len(bias_rows))], axis=0
            )
            weight = jnp.exp2(score - jnp.max(score, axis=0, keepdims=True)).astype(BF16)
            mixed = dot(jnp.concatenate([vbuf[cols, keys], ones], axis=0), weight)
            total = 1.0 / mixed[2 * HD : 2 * HD + 1, :]
            top = mixed[:HD, :LANES] * total[:, :LANES]
            bottom = mixed[HD : 2 * HD, LANES:] * total[:, LANES:]
            att[cols, lanes] = jnp.concatenate([top, bottom], axis=0).astype(BF16)
        return carry

    blocks = query_lanes // LANES
    if blocks == 1:
        block(0, 0)
    else:
        lax.fori_loop(0, blocks, block, 0)
    mixed = dot(wo_ref[...], att[...])
    partial = mixed[:channels] + mixed[channels:]
    if step < STEPS - 1:
        tbuf[...] = jnp.zeros_like(tbuf)
        tbuf[pl.ds(pl.multiple_of(tok_index * part_rows, 8), part_rows), :] = fresh_ref[step + 1]
        fresh_t = tbuf[...].T
        fresh_t = jnp.concatenate([fresh_t] * n_query, axis=1)
        slot = lax.broadcasted_iota(jnp.int32, (1, query_lanes), 1) // tok + first_key + HALO
        partial = jnp.where(slot == -1, fresh_t, partial)
    part_ref[...] = partial[:, : part_ref.shape[1]]


def last_kernel(cfg, *refs):
    tok, frames, channels, base, depth, level_count, heads, part_rows = cfg
    g_ref, hpart_ref, xq_ref = refs[:3]
    own = refs[3 : 3 + STEPS - 1]
    velocity_ref, queue_ref, tbuf = refs[3 + STEPS - 1 :]
    tok_index = lax.axis_index("tok")
    velocity, moved = advance(level_count, tok, None, g_ref, hpart_ref, xq_ref)
    for s in range(STEPS - 1):
        velocity_ref[s, 0] = own[s][...]
    velocity_ref[STEPS - 1, 0] = own_rows(velocity[:, :tok], tok, part_rows, tok_index, tbuf)
    queue_ref[0] = own_rows(moved[:, :tok], tok, part_rows, tok_index, tbuf)


def body(
    latent,
    fresh_noise,
    frame_slot,
    frame_reach,
    level_embed,
    embed_weight,
    qkv_weight,
    qk_gain,
    out_weight,
    vel_weight,
):
    frames, parts = lax.axis_size("queue"), lax.axis_size("tok")
    position = lax.axis_index("queue")
    part_rows, channels = latent.shape[1], latent.shape[2]
    tok = part_rows * parts
    level_count = level_embed.shape[0]
    depth = qkv_weight.shape[2]
    width = qkv_weight.shape[1]
    spare = round_up(width, 2 * LANES) - width
    if spare:
        qkv_weight = jnp.pad(qkv_weight, ((0, 0), (0, spare), (0, 0)))
        qk_gain = jnp.pad(qk_gain, ((0, 0), (0, spare)))
        out_weight = jnp.pad(out_weight, ((0, spare), (0, 0)))
        width += spare
    heads = width // HD
    base = round_up(channels + level_count, LANES)
    cfg = (tok, frames, channels, base, depth, level_count, heads, part_rows)
    vmem, smem, hbm = (
        pl.BlockSpec(memory_space=pltpu.VMEM),
        pl.BlockSpec(memory_space=pltpu.SMEM),
        pl.BlockSpec(memory_space=pltpu.HBM),
    )
    shape = jax.ShapeDtypeStruct

    def swapped(value, axis, distance):
        count = lax.axis_size(axis)
        return lax.ppermute(value, axis, [(source, source ^ distance) for source in range(count)])

    def from_ahead(value, distance):
        return lax.ppermute(value, "tok", [(source, (source - distance) % parts) for source in range(parts)])

    state = jnp.where(position == frames - 1, fresh_noise[0], latent[0])[None]
    rounds = []
    reached = 1
    while reached < frames:
        group = min(4, frames // reached)
        moved = [swapped(state, "queue", reached * d) for d in range(1, group)]
        state = jnp.concatenate([state] + moved, axis=0)
        rounds.append(state)
        reached *= group
    latents = [state] + [from_ahead(state, d) for d in range(1, parts)]

    share = depth // parts
    table = (embed_weight, level_embed, vel_weight.T)
    tables = [from_ahead(piece, d) for d in range(1, parts) for piece in table]

    rows = 384 if width % 384 == 0 else 256
    chunks = 4 * width // rows
    limit = pltpu.CompilerParams(vmem_limit_bytes=60 * 2**20)

    def estimate(share_count):
        return pl.CostEstimate(
            flops=int(8 * base * width * share * share_count),
            bytes_accessed=int(8 * width * share * share_count),
            transcendentals=0,
        )

    sums = pl.pallas_call(
        functools.partial(own_weights_kernel, rows, base),
        out_shape=(
            shape((3 * width, base), F32),
            shape((width, channels), F32),
            shape((base, base), F32),
            shape((channels, base), F32),
        ),
        in_specs=[vmem] * 3 + [hbm] * 2,
        out_specs=(vmem,) * 4,
        scratch_shapes=[
            pltpu.VMEM((1, chunks, rows, share), BF16),
            pltpu.SemaphoreType.DMA((1, chunks)),
        ],
        compiler_params=limit,
        cost_estimate=estimate(1),
        name="own_weights",
    )(*table, qkv_weight, out_weight)

    def other_weights(second, after):
        outs = [shape((width, 2 * base), BF16)]
        if second:
            outs += [shape((2 * channels, width), BF16), shape((base + channels, 2 * base), BF16)]
        else:
            outs += [shape((2 * base, width), BF16)]
        return pl.pallas_call(
            functools.partial(other_weights_kernel, rows, base, parts, second),
            out_shape=tuple(outs),
            in_specs=[vmem] * (3 * (parts - 1) + 4) + [hbm] * 2 + [pl.BlockSpec(memory_space=pl.ANY)],
            out_specs=(vmem,) * len(outs),
            scratch_shapes=[
                pltpu.VMEM((parts - 1, chunks // 2, rows, share), BF16),
                pltpu.SemaphoreType.DMA((parts - 1, chunks // 2)),
            ],
            compiler_params=limit,
            cost_estimate=estimate(0.5 * (parts - 1)),
            name="other_weights",
        )(*tables, *sums, qkv_weight, out_weight, after)

    mq, mk = other_weights(False, rounds[0])
    mv, wo, gram = other_weights(True, rounds[-1])

    query_block = max(1, LANES // tok)
    owned = []
    for step in range(STEPS):
        n_query = query_block + 2 * HALO * (STEPS - 1 - step)
        query_lanes, key_lanes = n_query * tok, (n_query + 2 * HALO) * tok
        args = [frame_slot, frame_reach]
        specs = [smem, smem]
        if step == 0:
            args += latents
            specs += [vmem] * parts
        else:
            args += [gathered, hpart, xq]
            specs += [vmem] * 3
        if step < STEPS - 1:
            args += [fresh_noise]
            specs += [vmem]
        args += [qk_gain, mq, mk, mv, wo, gram]
        specs += [vmem] * 6
        outs = [shape((channels, query_lanes), F32)] * 3
        if step > 0:
            outs += [shape((part_rows, channels), F32)]
        window = (2 * HALO + query_block) * tok
        result = pl.pallas_call(
            functools.partial(step_kernel, step, cfg),
            out_shape=tuple(outs),
            in_specs=specs,
            out_specs=(vmem,) * len(outs),
            scratch_shapes=[
                pltpu.VMEM((key_lanes, width), BF16),
                pltpu.VMEM((width, key_lanes), BF16),
                pltpu.VMEM((width, query_lanes), BF16),
                pltpu.VMEM((width, query_lanes), BF16),
                pltpu.VMEM((tok, channels), F32),
                pltpu.VMEM((key_lanes if step == 0 else tok, channels), F32),
            ],
            compiler_params=pltpu.CompilerParams(vmem_limit_bytes=48 * 2**20),
            cost_estimate=pl.CostEstimate(
                flops=4 * query_lanes * window * width + 12 * key_lanes * base * width,
                bytes_accessed=8 * width * base,
                transcendentals=query_lanes * window * heads,
            ),
            name="step%d" % step,
        )(*args)
        part, hpart, xq = result[:3]
        owned += list(result[3:])
        gathered = lax.all_gather(part, "tok", axis=0, tiled=False)

    return tuple(
        pl.pallas_call(
            functools.partial(last_kernel, cfg),
            out_shape=(
                shape((STEPS, 1, part_rows, channels), F32),
                shape((1, part_rows, channels), F32),
            ),
            in_specs=[vmem] * (3 + len(owned)),
            out_specs=(vmem, vmem),
            scratch_shapes=[pltpu.VMEM((tok, channels), F32)],
            compiler_params=pltpu.CompilerParams(vmem_limit_bytes=8 * 2**20),
            name="last",
        )(gathered, hpart, xq, *owned)
    )


def solution(mesh):
    return jax.shard_map(
        body,
        mesh=mesh,
        in_specs=(
            P("queue", "tok", None),
            P(None, "tok", None),
            P(),
            P(),
            P(None, "tok"),
            P(None, "tok"),
            P(None, "tok", None),
            P(None, "tok"),
            P("tok", None),
            P("tok", None),
        ),
        out_specs=(P(None, "queue", "tok", None), P("queue", "tok", None)),
        check_vma=False,
    )
```

```python
import functools
import math

import jax
import jax.numpy as jnp
from jax import lax
from jax.experimental import pallas as pl
from jax.experimental.pallas import tpu as pltpu
from jax.sharding import PartitionSpec as P

HD = 64
STEPS = 3
HALO = 3
LANES = 128
EPS = 1e-06
F32, BF16 = jnp.float32, jnp.bfloat16


def round_up(value, unit):
    return -(-value // unit) * unit


def dot(a, b):
    return jnp.dot(a, b, preferred_element_type=F32)


def dot_nt(a, b):
    return lax.dot_general(a, b, (((1,), (1,)), ((), ())), preferred_element_type=F32)


def halves(value, axis):
    high = value.astype(BF16)
    low = (value - high.astype(F32)).astype(BF16)
    return jnp.concatenate([high, low], axis=axis)


def start_chunks(rows, chunks, parts, qkv_hbm, out_hbm, buf, sems):
    per = out_hbm.shape[0] // rows
    depth = buf.shape[-1]
    index, count = lax.axis_index("tok"), lax.axis_size("tok")
    copies = []
    for place, chunk in enumerate(chunks):
        source = qkv_hbm.at[chunk // per] if chunk < 3 * per else out_hbm
        for at, part in enumerate(parts):
            columns = pl.ds(pl.multiple_of(lax.rem(index + part, count) * depth, LANES), depth)
            copy = pltpu.make_async_copy(
                source.at[pl.ds((chunk % per) * rows, rows), columns],
                buf.at[at, place],
                sems.at[at, place],
            )
            copy.start()
            copies.append(copy)
    return copies


def stack_rows(base, embed_ref, level_ref):
    filler = base - embed_ref.shape[0] - level_ref.shape[0]
    rows = [embed_ref[...].astype(F32), level_ref[...].astype(F32)]
    rows = jnp.concatenate(rows + [jnp.zeros((filler, embed_ref.shape[1]), F32)], axis=0)
    return rows.astype(BF16)


def weights_kernel(rows, base, count, second, *refs):
    shares = (0,) if count == 0 else tuple(range(1, count))
    tables, refs = refs[: 3 * len(shares)], refs[3 * len(shares) :]
    sums = ()
    if count:
        sums, refs = refs[: 3 if second else 1], refs[3 if second else 1 :]
    qkv_hbm, out_hbm = refs[:2]
    outs, buf, sems = refs[2:-2], refs[-2], refs[-1]
    width = out_hbm.shape[0]
    per = width // rows
    chunks = range(2 * per, 4 * per) if second else range(2 * per)
    copies = start_chunks(rows, chunks, shares, qkv_hbm, out_hbm, buf, sems)
    lefts = [stack_rows(base, *tables[3 * at : 3 * at + 2]) for at in range(len(shares))]
    vels = [tables[3 * at + 2][...] for at in range(len(shares))]
    if second:
        gram = sum(dot_nt(jnp.concatenate([left, vel], axis=0), left) for left, vel in zip(lefts, vels))
        outs[2][...] = halves(sums[2][...] + gram, 1) if count else gram
    for place, chunk in enumerate(chunks):
        for at in range(len(shares)):
            copies[place * len(shares) + at].wait()
        last = chunk // per == 3
        total = sum(dot_nt(buf[at, place], vels[at] if last else lefts[at]) for at in range(len(shares)))
        spot = slice(place * rows, (place + 1) * rows)
        if last:
            spot = slice((place - per) * rows, (place - per + 1) * rows)
        if count == 0:
            outs[1 if last else 0][spot, :] = total
            continue
        total = total + sums[1 if last else 0][spot, :]
        where = slice((chunk % per) * rows, (chunk % per + 1) * rows)
        if chunk // per % 2:
            outs[1][:, where] = halves(total.T, 0)
        else:
            outs[0][where, :] = halves(total, 1)


def advance(level_count, tok, first, g_ref, hpart_ref, xq_ref):
    shared = g_ref[0]
    for t in range(1, g_ref.shape[0]):
        shared = shared + g_ref[t]
    velocity = shared + hpart_ref[...]
    moved = xq_ref[...] - velocity * (1.0 / level_count)
    if first is None:
        return velocity, moved
    lane_frame = lax.broadcasted_iota(jnp.int32, (1, shared.shape[1]), 1) // tok
    return velocity, jnp.where(lane_frame + first == -1, shared, moved)


def own_rows(block, tok, part_rows, index, scratch):
    scratch[...] = block.T
    return scratch[pl.ds(pl.multiple_of(index * part_rows, 8), part_rows), :]


def step_kernel(step, cfg, *refs):
    tok, frames, channels, base, depth, level_count, heads, part_rows = cfg
    query_block = max(1, LANES // tok)
    n_query = query_block + 2 * HALO * (STEPS - 1 - step)
    n_key = n_query + 2 * HALO
    key_lanes, query_lanes = n_key * tok, n_query * tok
    width = heads * HD
    window = (2 * HALO + query_block) * tok
    position, tok_index = lax.axis_index("queue"), lax.axis_index("tok")
    first_key = position - HALO - (HALO + 1) * (STEPS - 1 - step)
    refs = list(refs)
    slot_ref, reach_ref = refs[0], refs[1]
    if step == 0:
        count = tok // part_rows
        lat_refs = refs[2 : 2 + count]
        refs = refs[2 + count :]
    else:
        g_ref, hprev_ref, xprev_ref = refs[2:5]
        refs = refs[5:]
    fresh_ref = None
    if step < STEPS - 1:
        fresh_ref = refs.pop(0)
    gain_ref, mq_ref, mk_ref, mv_ref, wo_ref, gram_ref = refs[:6]
    refs = refs[6:]
    part_ref, hpart_ref, xq_ref = refs[:3]
    refs = refs[3:]
    own_ref = None
    if step > 0:
        own_ref = refs.pop(0)
    kbuf, vbuf, qbuf, att, tbuf, xbuf = refs

    if step == 0:
        for w in range(n_key):
            source = lax.rem(first_key - 1 + w + 2 * frames, frames)
            for t in range(count):
                at = lax.rem(tok_index + t, count) * part_rows + w * tok
                xbuf[pl.ds(pl.multiple_of(at, 8), part_rows), :] = lat_refs[t][position ^ source]
        state = xbuf[...].T
    else:
        velocity, state = advance(level_count, tok, first_key - 1, g_ref, hprev_ref, xprev_ref)
        mine = (HALO + 1) * (STEPS - step)
        own_ref[...] = own_rows(velocity[:, mine * tok : (mine + 1) * tok], tok, part_rows, tok_index, tbuf)

    key_frame = lax.broadcasted_iota(jnp.int32, (1, key_lanes), 1) // tok
    level_row = jnp.full((1, key_lanes), -1, jnp.int32)
    for w in range(n_key):
        frame = first_key + w
        known = slot_ref[jnp.clip(frame - step - 1, 0, frames - 1)] + step
        level_row = jnp.where(key_frame == w, jnp.where(frame >= step + 1, known, frame), level_row)
    row = lax.broadcasted_iota(jnp.int32, (base - channels, key_lanes), 0)
    aug_t = jnp.concatenate([state, jnp.where(row == level_row, 1.0, 0.0)], axis=0)
    aug_t = aug_t.astype(BF16).astype(F32)
    aug = aug_t.T
    aug_b, aug_tb = aug.astype(BF16), aug_t.astype(BF16)
    aug_q = aug_t[:, HALO * tok : HALO * tok + query_lanes]
    aug_qb = aug_q.astype(BF16)
    both = jnp.concatenate([aug_b, aug_b], axis=1)
    both_t = jnp.concatenate([aug_tb, aug_tb], axis=0)
    both_q = jnp.concatenate([aug_qb, aug_qb], axis=0)
    gram = gram_ref[:base, :]
    mean_t = jnp.sum(dot(gram, both_t) * aug_t, axis=0, keepdims=True) * (1.0 / depth)
    mean_q = jnp.sum(dot(gram, both_q) * aug_q, axis=0, keepdims=True) * (1.0 / depth)
    mean_c = jnp.sum(dot_nt(both, gram) * aug, axis=1, keepdims=True) * (1.0 / depth)
    mean_t, mean_q, mean_c = (jnp.maximum(m, 0.0) + EPS for m in (mean_t, mean_q, mean_c))

    hpart_ref[...] = dot(gram_ref[base:, :], both_q)
    xq_ref[...] = state[:, HALO * tok : HALO * tok + query_lanes]

    gain = gain_ref[0:1, :] * gain_ref[1:2, :] * (HD ** -0.5 * math.log2(math.e))
    span = 256 if width % 256 == 0 else 128
    head_of = lambda axis: lax.broadcasted_iota(jnp.int32, (span, span), axis) // HD
    average = jnp.where(head_of(0) == head_of(1), 1.0 / HD, 0.0).astype(BF16)
    for at in range(0, width, span):
        raw = dot(both, mk_ref[:, at : at + span])
        spread = dot((raw * raw).astype(BF16), average)
        kbuf[:, at : at + span] = (raw * lax.rsqrt(spread + EPS * mean_c) * gain[:, at : at + span]).astype(BF16)
    vbuf[...] = (dot(mv_ref[...], both_t) * lax.rsqrt(mean_t)).astype(BF16)
    raw = dot(mq_ref[...], both_q).reshape(heads, HD, query_lanes)
    spread = jnp.sum(raw * raw, axis=1, keepdims=True) * (1.0 / HD)
    qbuf[...] = (raw * lax.rsqrt(spread + EPS * mean_q)[:, :, :]).reshape(width, query_lanes).astype(BF16)

    bound = HD * jnp.max(gain, axis=1, keepdims=True)
    upper = lax.broadcasted_iota(jnp.int32, (2 * HD, LANES), 0) < HD
    lane = lax.broadcasted_iota(jnp.int32, (1, 2 * LANES), 1)
    within = lax.rem(lane, LANES) // tok

    def place(b):
        lead = (b * LANES) // tok
        keys = pl.ds(pl.multiple_of(lead * tok, LANES), window)
        return lead, keys, pl.ds(pl.multiple_of(b * LANES, LANES), LANES)

    def biases(lead, shift):
        rows = []
        for k in range(2 * HALO + query_block):
            target = first_key + lead + k
            inside = (target >= 0) & (target < frames)
            row = jnp.zeros((1, 2 * LANES), F32)
            for j in range(query_block):
                frame = first_key + HALO + lead + j
                reach = reach_ref[jnp.clip(frame, 0, frames - 1)]
                unused = (frame < 0) | (frame >= frames)
                counted = (inside & (abs(k - HALO - j) <= reach)) | unused
                row = jnp.where(within == j, jnp.where(counted, 0.0, -1e30), row)
            rows.append(row - shift)
        return rows

    def scores(keys, lanes, cols, rows):
        query = qbuf[cols, lanes]
        zero = jnp.zeros_like(query)
        query = jnp.concatenate([jnp.where(upper, query, zero), jnp.where(upper, zero, query)], axis=1)
        score = dot(kbuf[keys, cols], query)
        return jnp.concatenate([score[k * tok : (k + 1) * tok] + rows[k] for k in range(len(rows))], axis=0)

    def mix(keys, lanes, cols, weight):
        ones = jnp.ones((16, window), BF16)
        mixed = dot(jnp.concatenate([vbuf[cols, keys], ones], axis=0), weight.astype(BF16))
        total = mixed[2 * HD : 2 * HD + 1, :]
        scale = 1.0 / total
        top = mixed[:HD, :LANES] * scale[:, :LANES]
        bottom = mixed[HD : 2 * HD, LANES:] * scale[:, LANES:]
        att[cols, lanes] = jnp.concatenate([top, bottom], axis=0).astype(BF16)
        return total

    def block(b, least):
        lead, keys, lanes = place(b)
        rows = biases(lead, bound)
        held = None
        for pair in range(heads // 2):
            cols = slice(pair * 2 * HD, (pair + 1) * 2 * HD)
            weight = jnp.exp2(scores(keys, lanes, cols, rows)).astype(BF16)
            if held is not None:
                least = jnp.minimum(least, mix(keys, lanes, *held))
            held = (cols, weight)
        return jnp.minimum(least, mix(keys, lanes, *held))

    def exact_block(at, carry):
        lead, keys, lanes = place(at // (heads // 2))
        cols = pl.ds(pl.multiple_of(lax.rem(at, heads // 2) * 2 * HD, 2 * HD), 2 * HD)
        score = scores(keys, lanes, cols, biases(lead, 0.0))
        mix(keys, lanes, cols, jnp.exp2(score - jnp.max(score, axis=0, keepdims=True)))
        return carry

    blocks = query_lanes // LANES
    least = jnp.ones((1, 2 * LANES), F32)
    least = block(0, least) if blocks == 1 else lax.fori_loop(0, blocks, block, least)

    @pl.when(jnp.min(least) < 1e-25)
    def _():
        lax.fori_loop(0, blocks * (heads // 2), exact_block, 0)

    mixed = dot(wo_ref[...], att[...])
    partial = mixed[:channels] + mixed[channels:]
    if step < STEPS - 1:
        tbuf[...] = jnp.zeros_like(tbuf)
        tbuf[pl.ds(pl.multiple_of(tok_index * part_rows, 8), part_rows), :] = fresh_ref[step + 1]
        fresh_t = tbuf[...].T
        fresh_t = jnp.concatenate([fresh_t] * n_query, axis=1)
        slot = lax.broadcasted_iota(jnp.int32, (1, query_lanes), 1) // tok + first_key + HALO
        partial = jnp.where(slot == -1, fresh_t, partial)
    part_ref[...] = partial[:, : part_ref.shape[1]]


def last_kernel(cfg, *refs):
    tok, frames, channels, base, depth, level_count, heads, part_rows = cfg
    g_ref, hpart_ref, xq_ref = refs[:3]
    own = refs[3 : 3 + STEPS - 1]
    velocity_ref, queue_ref, tbuf = refs[3 + STEPS - 1 :]
    tok_index = lax.axis_index("tok")
    velocity, moved = advance(level_count, tok, None, g_ref, hpart_ref, xq_ref)
    for s in range(STEPS - 1):
        velocity_ref[s, 0] = own[s][...]
    velocity_ref[STEPS - 1, 0] = own_rows(velocity[:, :tok], tok, part_rows, tok_index, tbuf)
    queue_ref[0] = own_rows(moved[:, :tok], tok, part_rows, tok_index, tbuf)


def body(
    latent,
    fresh_noise,
    frame_slot,
    frame_reach,
    level_embed,
    embed_weight,
    qkv_weight,
    qk_gain,
    out_weight,
    vel_weight,
):
    frames, parts = lax.axis_size("queue"), lax.axis_size("tok")
    position = lax.axis_index("queue")
    part_rows, channels = latent.shape[1], latent.shape[2]
    tok = part_rows * parts
    level_count = level_embed.shape[0]
    depth = qkv_weight.shape[2]
    width = qkv_weight.shape[1]
    spare = round_up(width, 2 * LANES) - width
    if spare:
        qkv_weight = jnp.pad(qkv_weight, ((0, 0), (0, spare), (0, 0)))
        qk_gain = jnp.pad(qk_gain, ((0, 0), (0, spare)))
        out_weight = jnp.pad(out_weight, ((0, spare), (0, 0)))
        width += spare
    heads = width // HD
    base = round_up(channels + level_count, LANES)
    cfg = (tok, frames, channels, base, depth, level_count, heads, part_rows)
    vmem, smem, hbm = (
        pl.BlockSpec(memory_space=pltpu.VMEM),
        pl.BlockSpec(memory_space=pltpu.SMEM),
        pl.BlockSpec(memory_space=pltpu.HBM),
    )
    shape = jax.ShapeDtypeStruct

    def swapped(value, axis, distance):
        count = lax.axis_size(axis)
        return lax.ppermute(value, axis, [(source, source ^ distance) for source in range(count)])

    def from_ahead(value, distance):
        return lax.ppermute(value, "tok", [(source, (source - distance) % parts) for source in range(parts)])

    share = depth // parts
    table = (embed_weight, level_embed, vel_weight.T)
    tables = [from_ahead(piece, d) for d in range(1, parts) for piece in table]
    rows = 384 if width % 384 == 0 else 256
    chunks = 2 * width // rows
    qkv_weight = pltpu.with_memory_space_constraint(qkv_weight, pltpu.HBM)
    out_weight = pltpu.with_memory_space_constraint(out_weight, pltpu.HBM)

    def weights(count, second, *operands):
        shares = max(1, count - 1)
        if count == 0 and second:
            outs = [shape((width, base), F32), shape((width, channels), F32), shape((base + channels, base), F32)]
        elif count == 0:
            outs = [shape((2 * width, base), F32)]
        elif second:
            outs = [
                shape((width, 2 * base), BF16),
                shape((2 * channels, width), BF16),
                shape((base + channels, 2 * base), BF16),
            ]
        else:
            outs = [shape((width, 2 * base), BF16), shape((2 * base, width), BF16)]
        return pl.pallas_call(
            functools.partial(weights_kernel, rows, base, count, second),
            out_shape=tuple(outs),
            in_specs=[vmem] * len(operands) + [hbm] * 2,
            out_specs=(vmem,) * len(outs),
            scratch_shapes=[
                pltpu.VMEM((shares, chunks, rows, share), BF16),
                pltpu.SemaphoreType.DMA((shares, chunks)),
            ],
            compiler_params=pltpu.CompilerParams(vmem_limit_bytes=24 * 2**20),
            cost_estimate=pl.CostEstimate(
                flops=4 * base * width * share * shares,
                bytes_accessed=4 * width * share * shares,
                transcendentals=0,
            ),
            name="weights",
        )(*operands, qkv_weight, out_weight)

    state = jnp.where(position == frames - 1, fresh_noise[0], latent[0])[None]
    work = [
        lambda: weights(0, False, *table),
        lambda: weights(0, True, *table),
        lambda: weights(parts, False, *tables, *done[0]),
        lambda: weights(parts, True, *tables, *done[1]),
    ]
    done = []
    reached = 1
    while reached < frames:
        moved = swapped(state, "queue", reached)
        if len(done) < len(work):
            moved, result = lax.optimization_barrier((moved, work[len(done)]()))
            done.append(result)
        state = jnp.concatenate([state, moved], axis=0)
        reached *= 2
    while len(done) < len(work):
        done.append(work[len(done)]())
    latents = [state] + [from_ahead(state, d) for d in range(1, parts)]
    mq, mk = done[2]
    mv, wo, gram = done[3]

    query_block = max(1, LANES // tok)
    owned = []
    for step in range(STEPS):
        n_query = query_block + 2 * HALO * (STEPS - 1 - step)
        query_lanes, key_lanes = n_query * tok, (n_query + 2 * HALO) * tok
        args = [frame_slot, frame_reach]
        specs = [smem, smem]
        if step == 0:
            args += latents
            specs += [vmem] * parts
        else:
            args += [gathered, hpart, xq]
            specs += [vmem] * 3
        if step < STEPS - 1:
            args += [fresh_noise]
            specs += [vmem]
        args += [qk_gain, mq, mk, mv, wo, gram]
        specs += [vmem] * 6
        outs = [shape((channels, query_lanes), F32)] * 3
        if step > 0:
            outs += [shape((part_rows, channels), F32)]
        window = (2 * HALO + query_block) * tok
        result = pl.pallas_call(
            functools.partial(step_kernel, step, cfg),
            out_shape=tuple(outs),
            in_specs=specs,
            out_specs=(vmem,) * len(outs),
            scratch_shapes=[
                pltpu.VMEM((key_lanes, width), BF16),
                pltpu.VMEM((width, key_lanes), BF16),
                pltpu.VMEM((width, query_lanes), BF16),
                pltpu.VMEM((width, query_lanes), BF16),
                pltpu.VMEM((tok, channels), F32),
                pltpu.VMEM((key_lanes if step == 0 else tok, channels), F32),
            ],
            compiler_params=pltpu.CompilerParams(vmem_limit_bytes=48 * 2**20),
            cost_estimate=pl.CostEstimate(
                flops=4 * query_lanes * window * width + 12 * key_lanes * base * width,
                bytes_accessed=8 * width * base,
                transcendentals=query_lanes * window * heads,
            ),
            name="step%d" % step,
        )(*args)
        part, hpart, xq = result[:3]
        owned += list(result[3:])
        gathered = lax.all_gather(part, "tok", axis=0, tiled=False)

    return tuple(
        pl.pallas_call(
            functools.partial(last_kernel, cfg),
            out_shape=(
                shape((STEPS, 1, part_rows, channels), F32),
                shape((1, part_rows, channels), F32),
            ),
            in_specs=[vmem] * (3 + len(owned)),
            out_specs=(vmem, vmem),
            scratch_shapes=[pltpu.VMEM((tok, channels), F32)],
            compiler_params=pltpu.CompilerParams(vmem_limit_bytes=8 * 2**20),
            name="last",
        )(gathered, hpart, xq, *owned)
    )


def solution(mesh):
    return jax.shard_map(
        body,
        mesh=mesh,
        in_specs=(
            P("queue", "tok", None),
            P(None, "tok", None),
            P(),
            P(),
            P(None, "tok"),
            P(None, "tok"),
            P(None, "tok", None),
            P(None, "tok"),
            P("tok", None),
            P("tok", None),
        ),
        out_specs=(P(None, "queue", "tok", None), P("queue", "tok", None)),
        check_vma=False,
    )
```

```python
import functools
import math

import jax
import jax.numpy as jnp
from jax import lax
from jax.experimental import pallas as pl
from jax.experimental.pallas import tpu as pltpu
from jax.sharding import PartitionSpec as P

HD = 64
STEPS = 3
HALO = 3
LANES = 128
EPS = 1e-06
F32, BF16 = jnp.float32, jnp.bfloat16


def round_up(value, unit):
    return -(-value // unit) * unit


def dot(a, b):
    return jnp.dot(a, b, preferred_element_type=F32)


def dot_nt(a, b):
    return lax.dot_general(a, b, (((1,), (1,)), ((), ())), preferred_element_type=F32)


def halves(value, axis):
    high = value.astype(BF16)
    low = (value - high.astype(F32)).astype(BF16)
    return jnp.concatenate([high, low], axis=axis)


def start_chunks(rows, chunks, parts, qkv_hbm, out_hbm, buf, sems):
    per = out_hbm.shape[0] // rows
    depth = buf.shape[-1]
    index, count = lax.axis_index("tok"), lax.axis_size("tok")
    copies = []
    for place, chunk in enumerate(chunks):
        source = qkv_hbm.at[chunk // per] if chunk < 3 * per else out_hbm
        for at, part in enumerate(parts):
            columns = pl.ds(pl.multiple_of(lax.rem(index + part, count) * depth, LANES), depth)
            copy = pltpu.make_async_copy(
                source.at[pl.ds((chunk % per) * rows, rows), columns],
                buf.at[at, place],
                sems.at[at, place],
            )
            copy.start()
            copies.append(copy)
    return copies


def stack_rows(base, embed, level):
    rows = [embed.astype(F32), level.astype(F32)]
    rows.append(jnp.zeros((base - embed.shape[0] - level.shape[0], embed.shape[1]), F32))
    return jnp.concatenate(rows, axis=0).astype(BF16)


def halved_dot(a, b):
    half = round_up(a.shape[1] // 2, LANES)
    return dot_nt(a[:, :half], b[:, :half]) + dot_nt(a[:, half:], b[:, half:])


def weights_kernel(rows, base, count, second, *refs):
    shares = (0,) if count == 0 else tuple(range(1, count))
    tables, refs = refs[: 3 * len(shares)], refs[3 * len(shares) :]
    sums = ()
    if count:
        sums, refs = refs[: 3 if second else 1], refs[3 if second else 1 :]
    qkv_hbm, out_hbm = refs[:2]
    scratch = 5 + 1 if count == 0 else 2
    outs, buf, sems = refs[-scratch - (3 if second else 1 + (count > 0)) : -scratch], refs[-2], refs[-1]
    width = out_hbm.shape[0]
    per = width // rows
    chunks = range(2 * per, 4 * per) if second else range(2 * per)
    if count == 0:
        held, small = refs[-6:-3], refs[-3]
        brought = [pltpu.make_async_copy(tables[at], held[at], small.at[at]) for at in range(3)]
        for copy in brought:
            copy.start()
    copies = start_chunks(rows, chunks, shares, qkv_hbm, out_hbm, buf, sems)
    if count == 0:
        for copy in brought:
            copy.wait()
        tables = held
    lefts = [stack_rows(base, tables[3 * at][...], tables[3 * at + 1][...]) for at in range(len(shares))]
    vels = [tables[3 * at + 2][...] for at in range(len(shares))]
    if second:
        gram = sum(dot_nt(jnp.concatenate([left, vel], axis=0), left) for left, vel in zip(lefts, vels))
        outs[2][...] = halves(sums[2][...] + gram, 1) if count else gram
    for place, chunk in enumerate(chunks):
        for at in range(len(shares)):
            copies[place * len(shares) + at].wait()
        last = chunk // per == 3
        total = sum(halved_dot(vels[at] if last else lefts[at], buf[at, place]) for at in range(len(shares)))
        spot = slice(place * rows, (place + 1) * rows)
        if last:
            spot = slice((place - per) * rows, (place - per + 1) * rows)
        if count == 0:
            outs[1 if last else 0][:, spot] = total
            continue
        total = total + sums[1 if last else 0][:, spot]
        where = slice((chunk % per) * rows, (chunk % per + 1) * rows)
        if chunk // per % 2:
            outs[1][:, where] = halves(total, 0)
        else:
            outs[0][where, :] = halves(total.T, 1)


def advance(level_count, tok, first, g_ref, hpart_ref, xq_ref):
    shared = g_ref[0]
    for t in range(1, g_ref.shape[0]):
        shared = shared + g_ref[t]
    velocity = shared + hpart_ref[...]
    moved = xq_ref[...] - velocity * (1.0 / level_count)
    if first is None:
        return velocity, moved
    lane_frame = lax.broadcasted_iota(jnp.int32, (1, shared.shape[1]), 1) // tok
    return velocity, jnp.where(lane_frame + first == -1, shared, moved)


def own_rows(block, tok, part_rows, index, scratch):
    scratch[...] = block.T
    return scratch[pl.ds(pl.multiple_of(index * part_rows, 8), part_rows), :]


def step_kernel(step, cfg, *refs):
    tok, frames, channels, base, depth, level_count, heads, part_rows = cfg
    query_block = max(1, LANES // tok)
    n_query = query_block + 2 * HALO * (STEPS - 1 - step)
    n_key = n_query + 2 * HALO
    key_lanes, query_lanes = n_key * tok, n_query * tok
    width = heads * HD
    window = (2 * HALO + query_block) * tok
    position, tok_index = lax.axis_index("queue"), lax.axis_index("tok")
    first_key = position - HALO - (HALO + 1) * (STEPS - 1 - step)
    refs = list(refs)
    slot_ref, reach_ref = refs[0], refs[1]
    if step == 0:
        count = tok // part_rows
        lat_refs, noise_refs = refs[2 : 2 + count], refs[2 + count : 1 + 2 * count]
        refs = refs[1 + 2 * count :]
    else:
        g_ref, hprev_ref, xprev_ref = refs[2:5]
        refs = refs[5:]
    fresh_ref = None
    if step < STEPS - 1:
        fresh_ref = refs.pop(0)
    gain_ref, mq_ref, mk_ref, mv_ref, wo_ref, gram_ref = refs[:6]
    refs = refs[6:]
    part_ref, hpart_ref, xq_ref = refs[:3]
    refs = refs[3:]
    own_ref = None
    if step > 0:
        own_ref = refs.pop(0)
    kbuf, vbuf, qbuf, att, tbuf, xbuf = refs

    if step == 0:
        noise = [fresh_ref[0]] + [ref[...] for ref in noise_refs]
        for w in range(n_key):
            source = lax.rem(first_key - 1 + w + 2 * frames, frames)
            for t in range(count):
                at = lax.rem(tok_index + t, count) * part_rows + w * tok
                rows = jnp.where(source == frames - 1, noise[t], lat_refs[t][position ^ source])
                xbuf[pl.ds(pl.multiple_of(at, 8), part_rows), :] = rows
        state = xbuf[...].T
    else:
        velocity, state = advance(level_count, tok, first_key - 1, g_ref, hprev_ref, xprev_ref)
        mine = (HALO + 1) * (STEPS - step)
        own_ref[...] = own_rows(velocity[:, mine * tok : (mine + 1) * tok], tok, part_rows, tok_index, tbuf)

    key_frame = lax.broadcasted_iota(jnp.int32, (1, key_lanes), 1) // tok
    level_row = jnp.full((1, key_lanes), -1, jnp.int32)
    for w in range(n_key):
        frame = first_key + w
        known = slot_ref[jnp.clip(frame - step - 1, 0, frames - 1)] + step
        level_row = jnp.where(key_frame == w, jnp.where(frame >= step + 1, known, frame), level_row)
    row = lax.broadcasted_iota(jnp.int32, (base - channels, key_lanes), 0)
    aug_t = jnp.concatenate([state, jnp.where(row == level_row, 1.0, 0.0)], axis=0)
    aug_t = aug_t.astype(BF16).astype(F32)
    aug_tb = aug_t.astype(BF16)
    both_t = jnp.concatenate([aug_tb, aug_tb], axis=0)
    mean_t = jnp.sum(dot(gram_ref[:base, :], both_t) * aug_t, axis=0, keepdims=True) * (1.0 / depth)
    mean_t = jnp.maximum(mean_t, 0.0) + EPS
    queries = slice(HALO * tok, HALO * tok + query_lanes)
    mean_q = mean_t[:, queries]
    aug_qb = aug_t[:, queries].astype(BF16)
    both_q = jnp.concatenate([aug_qb, aug_qb], axis=0)
    last_row = lax.broadcasted_iota(jnp.int32, (base, key_lanes), 0) == base - 1
    aug = jnp.where(last_row, EPS * mean_t, aug_t).T
    eps_c = aug[:, base - 1 : base]
    aug_b = aug.astype(BF16)
    both = jnp.concatenate([aug_b, aug_b], axis=1)

    hpart_ref[...] = dot(gram_ref[base:, :], both_q)
    xq_ref[...] = state[:, queries]

    gain = gain_ref[0:1, :] * gain_ref[1:2, :] * (HD ** -0.5 * math.log2(math.e))
    span = 256 if width % 256 == 0 else 128
    head_of = lambda axis: lax.broadcasted_iota(jnp.int32, (span, span), axis) // HD
    average = jnp.where(head_of(0) == head_of(1), 1.0 / HD, 0.0).astype(BF16)
    for at in range(0, width, span):
        raw = dot(both, mk_ref[:, at : at + span])
        spread = dot((raw * raw).astype(BF16), average)
        kbuf[:, at : at + span] = (raw * lax.rsqrt(spread + eps_c) * gain[:, at : at + span]).astype(BF16)
    vbuf[...] = (dot(mv_ref[...], both_t) * lax.rsqrt(mean_t)).astype(BF16)
    raw = dot(mq_ref[...], both_q).reshape(heads, HD, query_lanes)
    spread = jnp.sum(raw * raw, axis=1, keepdims=True) * (1.0 / HD)
    qbuf[...] = (raw * lax.rsqrt(spread + EPS * mean_q)[:, :, :]).reshape(width, query_lanes).astype(BF16)

    bound = HD * jnp.max(gain, axis=1, keepdims=True)
    upper = lax.broadcasted_iota(jnp.int32, (2 * HD, LANES), 0) < HD
    lane = lax.broadcasted_iota(jnp.int32, (1, 2 * LANES), 1)
    within = lax.rem(lane, LANES) // tok

    def place(b):
        lead = (b * LANES) // tok
        keys = pl.ds(pl.multiple_of(lead * tok, LANES), window)
        return lead, keys, pl.ds(pl.multiple_of(b * LANES, LANES), LANES)

    def biases(lead, shift):
        rows = []
        for k in range(2 * HALO + query_block):
            target = first_key + lead + k
            inside = (target >= 0) & (target < frames)
            row = jnp.zeros((1, 2 * LANES), F32)
            for j in range(query_block):
                frame = first_key + HALO + lead + j
                reach = reach_ref[jnp.clip(frame, 0, frames - 1)]
                unused = (frame < 0) | (frame >= frames)
                counted = (inside & (abs(k - HALO - j) <= reach)) | unused
                row = jnp.where(within == j, jnp.where(counted, 0.0, -1e30), row)
            rows.append(row - shift)
        return rows

    def scores(keys, lanes, cols, rows):
        query = qbuf[cols, lanes]
        zero = jnp.zeros_like(query)
        query = jnp.concatenate([jnp.where(upper, query, zero), jnp.where(upper, zero, query)], axis=1)
        score = dot(kbuf[keys, cols], query)
        return jnp.concatenate([score[k * tok : (k + 1) * tok] + rows[k] for k in range(len(rows))], axis=0)

    def mix(keys, lanes, cols, weight):
        ones = jnp.ones((16, window), BF16)
        mixed = dot(jnp.concatenate([vbuf[cols, keys], ones], axis=0), weight.astype(BF16))
        total = mixed[2 * HD : 2 * HD + 1, :]
        scale = 1.0 / total
        top = mixed[:HD, :LANES] * scale[:, :LANES]
        bottom = mixed[HD : 2 * HD, LANES:] * scale[:, LANES:]
        att[cols, lanes] = jnp.concatenate([top, bottom], axis=0).astype(BF16)
        return total

    def block(b, least):
        lead, keys, lanes = place(b)
        rows = biases(lead, bound)
        held = None
        for pair in range(heads // 2):
            cols = slice(pair * 2 * HD, (pair + 1) * 2 * HD)
            weight = jnp.exp2(scores(keys, lanes, cols, rows)).astype(BF16)
            if held is not None:
                least = jnp.minimum(least, mix(keys, lanes, *held))
            held = (cols, weight)
        return jnp.minimum(least, mix(keys, lanes, *held))

    def exact_block(at, carry):
        lead, keys, lanes = place(at // (heads // 2))
        cols = pl.ds(pl.multiple_of(lax.rem(at, heads // 2) * 2 * HD, 2 * HD), 2 * HD)
        score = scores(keys, lanes, cols, biases(lead, 0.0))
        mix(keys, lanes, cols, jnp.exp2(score - jnp.max(score, axis=0, keepdims=True)))
        return carry

    blocks = query_lanes // LANES
    least = jnp.ones((1, 2 * LANES), F32)
    least = block(0, least) if blocks == 1 else lax.fori_loop(0, blocks, block, least)

    @pl.when(jnp.min(least) < 1e-25)
    def _():
        lax.fori_loop(0, blocks * (heads // 2), exact_block, 0)

    mixed = dot(wo_ref[...], att[...])
    partial = mixed[:channels] + mixed[channels:]
    if step < STEPS - 1:
        tbuf[...] = jnp.zeros_like(tbuf)
        tbuf[pl.ds(pl.multiple_of(tok_index * part_rows, 8), part_rows), :] = fresh_ref[step + 1]
        fresh_t = tbuf[...].T
        fresh_t = jnp.concatenate([fresh_t] * n_query, axis=1)
        slot = lax.broadcasted_iota(jnp.int32, (1, query_lanes), 1) // tok + first_key + HALO
        partial = jnp.where(slot == -1, fresh_t, partial)
    part_ref[...] = partial[:, : part_ref.shape[1]]


def last_kernel(cfg, *refs):
    tok, frames, channels, base, depth, level_count, heads, part_rows = cfg
    g_ref, hpart_ref, xq_ref = refs[:3]
    own = refs[3 : 3 + STEPS - 1]
    velocity_ref, queue_ref, tbuf = refs[3 + STEPS - 1 :]
    tok_index = lax.axis_index("tok")
    velocity, moved = advance(level_count, tok, None, g_ref, hpart_ref, xq_ref)
    for s in range(STEPS - 1):
        velocity_ref[s, 0] = own[s][...]
    velocity_ref[STEPS - 1, 0] = own_rows(velocity[:, :tok], tok, part_rows, tok_index, tbuf)
    queue_ref[0] = own_rows(moved[:, :tok], tok, part_rows, tok_index, tbuf)


def body(
    latent,
    fresh_noise,
    frame_slot,
    frame_reach,
    level_embed,
    embed_weight,
    qkv_weight,
    qk_gain,
    out_weight,
    vel_weight,
):
    frames, parts = lax.axis_size("queue"), lax.axis_size("tok")
    position = lax.axis_index("queue")
    part_rows, channels = latent.shape[1], latent.shape[2]
    tok = part_rows * parts
    level_count = level_embed.shape[0]
    depth = qkv_weight.shape[2]
    width = qkv_weight.shape[1]
    spare = round_up(width, 2 * LANES) - width
    if spare:
        qkv_weight = jnp.pad(qkv_weight, ((0, 0), (0, spare), (0, 0)))
        qk_gain = jnp.pad(qk_gain, ((0, 0), (0, spare)))
        out_weight = jnp.pad(out_weight, ((0, spare), (0, 0)))
        width += spare
    heads = width // HD
    base = round_up(channels + level_count + 1, LANES)
    cfg = (tok, frames, channels, base, depth, level_count, heads, part_rows)
    vmem, smem, hbm, anywhere = (
        pl.BlockSpec(memory_space=pltpu.VMEM),
        pl.BlockSpec(memory_space=pltpu.SMEM),
        pl.BlockSpec(memory_space=pltpu.HBM),
        pl.BlockSpec(memory_space=pl.ANY),
    )
    shape = jax.ShapeDtypeStruct

    def swapped(value, axis, distance):
        count = lax.axis_size(axis)
        return lax.ppermute(value, axis, [(source, source ^ distance) for source in range(count)])

    def from_ahead(value, distance):
        return lax.ppermute(value, "tok", [(source, (source - distance) % parts) for source in range(parts)])

    share = depth // parts
    table = (embed_weight, level_embed, vel_weight.T)
    tables = [from_ahead(piece, d) for d in range(1, parts) for piece in table]
    noise = [from_ahead(fresh_noise[0], d) for d in range(1, parts)]
    in_hbm = lambda array: pltpu.with_memory_space_constraint(array, pltpu.HBM)
    table = tuple(in_hbm(piece) for piece in table)
    qkv_weight, out_weight = in_hbm(qkv_weight), in_hbm(out_weight)
    rows = 384 if width % 384 == 0 else 256
    chunks = 2 * width // rows

    def weights(count, second, after, *operands):
        shares = max(1, count - 1)
        if count == 0 and second:
            outs = [shape((base, width), F32), shape((channels, width), F32), shape((base + channels, base), F32)]
        elif count == 0:
            outs = [shape((base, 2 * width), F32)]
        elif second:
            outs = [
                shape((width, 2 * base), BF16),
                shape((2 * channels, width), BF16),
                shape((base + channels, 2 * base), BF16),
            ]
        else:
            outs = [shape((width, 2 * base), BF16), shape((2 * base, width), BF16)]
        scratch = [pltpu.VMEM((shares, chunks, rows, share), BF16), pltpu.SemaphoreType.DMA((shares, chunks))]
        if count == 0:
            held = [pltpu.VMEM(piece.shape, BF16) for piece in table]
            scratch = held + [pltpu.SemaphoreType.DMA((3,))] + scratch
        return pl.pallas_call(
            functools.partial(weights_kernel, rows, base, count, second),
            out_shape=tuple(outs),
            in_specs=[hbm if count == 0 else vmem] * len(operands) + [hbm] * 2 + [anywhere] * len(after),
            out_specs=(vmem,) * len(outs),
            scratch_shapes=scratch,
            compiler_params=pltpu.CompilerParams(vmem_limit_bytes=24 * 2**20),
            cost_estimate=pl.CostEstimate(
                flops=4 * base * width * share * shares,
                bytes_accessed=4 * width * share * shares,
                transcendentals=0,
            ),
            name="weights",
        )(*operands, qkv_weight, out_weight, *after)

    state = latent
    work = [
        lambda *after: weights(0, False, after, *table),
        lambda *after: weights(0, True, after, *table),
        lambda *after: weights(parts, False, after, *tables, *done[0]),
        lambda *after: weights(parts, True, after, *tables, *done[1]),
    ]
    done, after = [], ()
    reached = 1
    while reached < frames:
        moved = swapped(state, "queue", reached)
        if len(done) < len(work):
            moved, noise, result = lax.optimization_barrier((moved, noise, work[len(done)](*after)))
            done.append(result)
            after = (moved,)
        state = jnp.concatenate([state, moved], axis=0)
        reached *= 2
    while len(done) < len(work):
        done.append(work[len(done)]())
    latents = [state] + [from_ahead(state, d) for d in range(1, parts)] + noise
    mq, mk = done[2]
    mv, wo, gram = done[3]

    query_block = max(1, LANES // tok)
    owned = []
    for step in range(STEPS):
        n_query = query_block + 2 * HALO * (STEPS - 1 - step)
        query_lanes, key_lanes = n_query * tok, (n_query + 2 * HALO) * tok
        args = [frame_slot, frame_reach]
        specs = [smem, smem]
        if step == 0:
            args += latents
            specs += [vmem] * len(latents)
        else:
            args += [gathered, hpart, xq]
            specs += [vmem] * 3
        if step < STEPS - 1:
            args += [fresh_noise]
            specs += [vmem]
        args += [qk_gain, mq, mk, mv, wo, gram]
        specs += [vmem] * 6
        outs = [shape((channels, query_lanes), F32)] * 3
        if step > 0:
            outs += [shape((part_rows, channels), F32)]
        window = (2 * HALO + query_block) * tok
        result = pl.pallas_call(
            functools.partial(step_kernel, step, cfg),
            out_shape=tuple(outs),
            in_specs=specs,
            out_specs=(vmem,) * len(outs),
            scratch_shapes=[
                pltpu.VMEM((key_lanes, width), BF16),
                pltpu.VMEM((width, key_lanes), BF16),
                pltpu.VMEM((width, query_lanes), BF16),
                pltpu.VMEM((width, query_lanes), BF16),
                pltpu.VMEM((tok, channels), F32),
                pltpu.VMEM((key_lanes if step == 0 else tok, channels), F32),
            ],
            compiler_params=pltpu.CompilerParams(vmem_limit_bytes=48 * 2**20),
            cost_estimate=pl.CostEstimate(
                flops=4 * query_lanes * window * width + 12 * key_lanes * base * width,
                bytes_accessed=8 * width * base,
                transcendentals=query_lanes * window * heads,
            ),
            name="step%d" % step,
        )(*args)
        part, hpart, xq = result[:3]
        owned += list(result[3:])
        gathered = lax.all_gather(part, "tok", axis=0, tiled=False)

    return tuple(
        pl.pallas_call(
            functools.partial(last_kernel, cfg),
            out_shape=(
                shape((STEPS, 1, part_rows, channels), F32),
                shape((1, part_rows, channels), F32),
            ),
            in_specs=[vmem] * (3 + len(owned)),
            out_specs=(vmem, vmem),
            scratch_shapes=[pltpu.VMEM((tok, channels), F32)],
            compiler_params=pltpu.CompilerParams(vmem_limit_bytes=8 * 2**20),
            name="last",
        )(gathered, hpart, xq, *owned)
    )


def solution(mesh):
    return jax.shard_map(
        body,
        mesh=mesh,
        in_specs=(
            P("queue", "tok", None),
            P(None, "tok", None),
            P(),
            P(),
            P(None, "tok"),
            P(None, "tok"),
            P(None, "tok", None),
            P(None, "tok"),
            P("tok", None),
            P("tok", None),
        ),
        out_specs=(P(None, "queue", "tok", None), P("queue", "tok", None)),
        check_vma=False,
    )
```

```python
import functools
import math

import jax
import jax.numpy as jnp
from jax import lax
from jax.experimental import pallas as pl
from jax.experimental.pallas import tpu as pltpu
from jax.sharding import PartitionSpec as P

HD = 64
STEPS = 3
HALO = 3
LANES = 128
AHEAD = 3
EPS = 1e-06
F32, BF16 = jnp.float32, jnp.bfloat16


def round_up(value, unit):
    return -(-value // unit) * unit


def dot(a, b):
    return jnp.dot(a, b, preferred_element_type=F32)


def dot_nt(a, b):
    return lax.dot_general(a, b, (((1,), (1,)), ((), ())), preferred_element_type=F32)


def halves(value, axis):
    high = value.astype(BF16)
    low = (value - high.astype(F32)).astype(BF16)
    return jnp.concatenate([high, low], axis=axis)


def chunk_copies(rows, chunks, parts, qkv_hbm, out_hbm, buf, sems):
    per = out_hbm.shape[0] // rows
    depth = buf.shape[-1]
    index, count = lax.axis_index("tok"), lax.axis_size("tok")
    copies = {}
    for place, chunk in enumerate(chunks):
        source = qkv_hbm.at[chunk // per] if chunk < 3 * per else out_hbm
        for at, part in enumerate(parts):
            columns = pl.ds(pl.multiple_of(lax.rem(index + part, count) * depth, LANES), depth)
            copies[place, at] = pltpu.make_async_copy(
                source.at[pl.ds((chunk % per) * rows, rows), columns],
                buf.at[at, place],
                sems.at[at, place],
            )
    return copies


def stack_rows(base, embed, level):
    rows = [embed.astype(F32), level.astype(F32)]
    rows.append(jnp.zeros((base - embed.shape[0] - level.shape[0], embed.shape[1]), F32))
    return jnp.concatenate(rows, axis=0).astype(BF16)


def halved_dot(a, b):
    half = round_up(a.shape[1] // 2, LANES)
    return dot_nt(a[:, :half], b[:, :half]) + dot_nt(a[:, half:], b[:, half:])


def weights_kernel(rows, base, count, second, *refs):
    shares = (0,) if count == 0 else tuple(range(1, count))
    tables, refs = refs[: 3 * len(shares)], refs[3 * len(shares) :]
    sums = ()
    if count:
        sums, refs = refs[: 3 if second else 1], refs[3 if second else 1 :]
    qkv_hbm, out_hbm = refs[:2]
    scratch = 5 + 1 if count == 0 else 2
    outs, buf, sems = refs[-scratch - (3 if second else 1 + (count > 0)) : -scratch], refs[-2], refs[-1]
    width = out_hbm.shape[0]
    per = width // rows
    chunks = range(2 * per, 4 * per) if second else range(2 * per)
    if count == 0:
        held, small = refs[-6:-3], refs[-3]
        brought = [pltpu.make_async_copy(tables[at], held[at], small.at[at]) for at in range(3)]
        for copy in brought:
            copy.start()
    copies = chunk_copies(rows, chunks, shares, qkv_hbm, out_hbm, buf, sems)
    for key in copies:
        if key[0] < AHEAD:
            copies[key].start()
    if count == 0:
        for copy in brought:
            copy.wait()
        tables = held
    lefts = [stack_rows(base, tables[3 * at][...], tables[3 * at + 1][...]) for at in range(len(shares))]
    vels = [tables[3 * at + 2][...] for at in range(len(shares))]
    if second:
        gram = sum(dot_nt(jnp.concatenate([left, vel], axis=0), left) for left, vel in zip(lefts, vels))
        outs[2][...] = halves(sums[2][...] + gram, 1) if count else gram
    for place, chunk in enumerate(chunks):
        for at in range(len(shares)):
            copies[place, at].wait()
            if place + AHEAD < len(chunks):
                copies[place + AHEAD, at].start()
        last = chunk // per == 3
        total = sum(halved_dot(vels[at] if last else lefts[at], buf[at, place]) for at in range(len(shares)))
        spot = slice(place * rows, (place + 1) * rows)
        if last:
            spot = slice((place - per) * rows, (place - per + 1) * rows)
        if count == 0:
            outs[1 if last else 0][:, spot] = total
            continue
        total = total + sums[1 if last else 0][:, spot]
        where = slice((chunk % per) * rows, (chunk % per + 1) * rows)
        if chunk // per % 2:
            outs[1][:, where] = halves(total, 0)
        else:
            outs[0][where, :] = halves(total.T, 1)


def advance(level_count, tok, first, g_ref, hpart_ref, xq_ref):
    shared = g_ref[0]
    for t in range(1, g_ref.shape[0]):
        shared = shared + g_ref[t]
    velocity = shared + hpart_ref[...]
    moved = xq_ref[...] - velocity * (1.0 / level_count)
    if first is None:
        return velocity, moved
    lane_frame = lax.broadcasted_iota(jnp.int32, (1, shared.shape[1]), 1) // tok
    return velocity, jnp.where(lane_frame + first == -1, shared, moved)


def own_rows(block, tok, part_rows, index, scratch):
    scratch[...] = block.T
    return scratch[pl.ds(pl.multiple_of(index * part_rows, 8), part_rows), :]


def step_kernel(step, cfg, *refs):
    tok, frames, channels, base, depth, level_count, heads, part_rows = cfg
    query_block = max(1, LANES // tok)
    n_query = query_block + 2 * HALO * (STEPS - 1 - step)
    n_key = n_query + 2 * HALO
    key_lanes, query_lanes = n_key * tok, n_query * tok
    width = heads * HD
    window = (2 * HALO + query_block) * tok
    position, tok_index = lax.axis_index("queue"), lax.axis_index("tok")
    first_key = position - HALO - (HALO + 1) * (STEPS - 1 - step)
    refs = list(refs)
    slot_ref, reach_ref = refs[0], refs[1]
    if step == 0:
        count = tok // part_rows
        lat_refs, noise_refs = refs[2 : 2 + count], refs[2 + count : 1 + 2 * count]
        refs = refs[1 + 2 * count :]
    else:
        g_ref, hprev_ref, xprev_ref = refs[2:5]
        refs = refs[5:]
    fresh_ref = None
    if step < STEPS - 1:
        fresh_ref = refs.pop(0)
    gain_ref, mq_ref, mk_ref, mv_ref, wo_ref, gram_ref = refs[:6]
    refs = refs[6:]
    part_ref, hpart_ref, xq_ref = refs[:3]
    refs = refs[3:]
    own_ref = None
    if step > 0:
        own_ref = refs.pop(0)
    kbuf, vbuf, qbuf, att, tbuf, xbuf = refs

    if step == 0:
        noise = [fresh_ref[0]] + [ref[0] for ref in noise_refs]
        for w in range(n_key):
            source = lax.rem(first_key - 1 + w + 2 * frames, frames)
            apart, bits = position ^ source, frames.bit_length() - 2
            second = ((apart >> bits) & 1) == 1
            entry = sum(((apart >> bit) & 1) << (bits - 1 - bit) for bit in range(bits))
            for t in range(count):
                at = lax.rem(tok_index + t, count) * part_rows + w * tok
                beside = lat_refs[t][entry]
                rows = jnp.where(second, beside[:, channels:], beside[:, :channels])
                rows = jnp.where(source == frames - 1, noise[t], rows)
                xbuf[pl.ds(pl.multiple_of(at, 8), part_rows), :] = rows
        state = xbuf[...].T
    else:
        velocity, state = advance(level_count, tok, first_key - 1, g_ref, hprev_ref, xprev_ref)
        mine = (HALO + 1) * (STEPS - step)
        own_ref[...] = own_rows(velocity[:, mine * tok : (mine + 1) * tok], tok, part_rows, tok_index, tbuf)

    key_frame = lax.broadcasted_iota(jnp.int32, (1, key_lanes), 1) // tok
    level_row = jnp.full((1, key_lanes), -1, jnp.int32)
    for w in range(n_key):
        frame = first_key + w
        known = slot_ref[jnp.clip(frame - step - 1, 0, frames - 1)] + step
        level_row = jnp.where(key_frame == w, jnp.where(frame >= step + 1, known, frame), level_row)
    row = lax.broadcasted_iota(jnp.int32, (base - channels, key_lanes), 0)
    aug_t = jnp.concatenate([state, jnp.where(row == level_row, 1.0, 0.0)], axis=0)
    aug_t = aug_t.astype(BF16).astype(F32)
    aug_tb = aug_t.astype(BF16)
    both_t = jnp.concatenate([aug_tb, aug_tb], axis=0)
    mean_t = jnp.sum(dot(gram_ref[:base, :], both_t) * aug_t, axis=0, keepdims=True) * (1.0 / depth)
    mean_t = jnp.maximum(mean_t, 0.0) + EPS
    queries = slice(HALO * tok, HALO * tok + query_lanes)
    mean_q = mean_t[:, queries]
    aug_qb = aug_t[:, queries].astype(BF16)
    both_q = jnp.concatenate([aug_qb, aug_qb], axis=0)
    last_row = lax.broadcasted_iota(jnp.int32, (base, key_lanes), 0) == base - 1
    aug = jnp.where(last_row, EPS * mean_t, aug_t).T
    eps_c = aug[:, base - 1 : base]
    aug_b = aug.astype(BF16)
    both = jnp.concatenate([aug_b, aug_b], axis=1)

    hpart_ref[...] = dot(gram_ref[base:, :], both_q)
    xq_ref[...] = state[:, queries]

    gain = gain_ref[0:1, :] * gain_ref[1:2, :] * (HD ** -0.5 * math.log2(math.e))
    span = 256 if width % 256 == 0 else 128
    head_of = lambda axis: lax.broadcasted_iota(jnp.int32, (span, span), axis) // HD
    average = jnp.where(head_of(0) == head_of(1), 1.0 / HD, 0.0).astype(BF16)
    for at in range(0, width, span):
        raw = dot(both, mk_ref[:, at : at + span])
        spread = dot((raw * raw).astype(BF16), average)
        kbuf[:, at : at + span] = (raw * lax.rsqrt(spread + eps_c) * gain[:, at : at + span]).astype(BF16)
    vbuf[...] = (dot(mv_ref[...], both_t) * lax.rsqrt(mean_t)).astype(BF16)
    raw = dot(mq_ref[...], both_q).reshape(heads, HD, query_lanes)
    spread = jnp.sum(raw * raw, axis=1, keepdims=True) * (1.0 / HD)
    qbuf[...] = (raw * lax.rsqrt(spread + EPS * mean_q)[:, :, :]).reshape(width, query_lanes).astype(BF16)

    bound = HD * jnp.max(gain, axis=1, keepdims=True)
    upper = lax.broadcasted_iota(jnp.int32, (2 * HD, LANES), 0) < HD
    lane = lax.broadcasted_iota(jnp.int32, (1, 2 * LANES), 1)
    within = lax.rem(lane, LANES) // tok

    def place(b):
        lead = (b * LANES) // tok
        keys = pl.ds(pl.multiple_of(lead * tok, LANES), window)
        return lead, keys, pl.ds(pl.multiple_of(b * LANES, LANES), LANES)

    def biases(lead, shift):
        rows = []
        for k in range(2 * HALO + query_block):
            target = first_key + lead + k
            inside = (target >= 0) & (target < frames)
            row = jnp.zeros((1, 2 * LANES), F32)
            for j in range(query_block):
                frame = first_key + HALO + lead + j
                reach = reach_ref[jnp.clip(frame, 0, frames - 1)]
                unused = (frame < 0) | (frame >= frames)
                counted = (inside & (abs(k - HALO - j) <= reach)) | unused
                row = jnp.where(within == j, jnp.where(counted, 0.0, -1e30), row)
            rows.append(row - shift)
        return rows

    def scores(keys, lanes, cols, rows):
        query = qbuf[cols, lanes]
        zero = jnp.zeros_like(query)
        query = jnp.concatenate([jnp.where(upper, query, zero), jnp.where(upper, zero, query)], axis=1)
        score = dot(kbuf[keys, cols], query)
        return jnp.concatenate([score[k * tok : (k + 1) * tok] + rows[k] for k in range(len(rows))], axis=0)

    def mix(keys, lanes, cols, weight):
        ones = jnp.ones((16, window), BF16)
        mixed = dot(jnp.concatenate([vbuf[cols, keys], ones], axis=0), weight.astype(BF16))
        total = mixed[2 * HD : 2 * HD + 1, :]
        scale = 1.0 / total
        top = mixed[:HD, :LANES] * scale[:, :LANES]
        bottom = mixed[HD : 2 * HD, LANES:] * scale[:, LANES:]
        att[cols, lanes] = jnp.concatenate([top, bottom], axis=0).astype(BF16)
        return total

    def block(b, least):
        lead, keys, lanes = place(b)
        rows = biases(lead, bound)
        held = None
        for pair in range(heads // 2):
            cols = slice(pair * 2 * HD, (pair + 1) * 2 * HD)
            weight = jnp.exp2(scores(keys, lanes, cols, rows)).astype(BF16)
            if held is not None:
                least = jnp.minimum(least, mix(keys, lanes, *held))
            held = (cols, weight)
        return jnp.minimum(least, mix(keys, lanes, *held))

    def exact_block(at, carry):
        lead, keys, lanes = place(at // (heads // 2))
        cols = pl.ds(pl.multiple_of(lax.rem(at, heads // 2) * 2 * HD, 2 * HD), 2 * HD)
        score = scores(keys, lanes, cols, biases(lead, 0.0))
        mix(keys, lanes, cols, jnp.exp2(score - jnp.max(score, axis=0, keepdims=True)))
        return carry

    blocks = query_lanes // LANES
    least = jnp.ones((1, 2 * LANES), F32)
    least = block(0, least) if blocks == 1 else lax.fori_loop(0, blocks, block, least)

    @pl.when(jnp.min(least) < 1e-25)
    def _():
        lax.fori_loop(0, blocks * (heads // 2), exact_block, 0)

    mixed = dot(wo_ref[...], att[...])
    partial = mixed[:channels] + mixed[channels:]
    if step < STEPS - 1:
        tbuf[...] = jnp.zeros_like(tbuf)
        tbuf[pl.ds(pl.multiple_of(tok_index * part_rows, 8), part_rows), :] = fresh_ref[step + 1]
        fresh_t = tbuf[...].T
        fresh_t = jnp.concatenate([fresh_t] * n_query, axis=1)
        slot = lax.broadcasted_iota(jnp.int32, (1, query_lanes), 1) // tok + first_key + HALO
        partial = jnp.where(slot == -1, fresh_t, partial)
    part_ref[...] = partial[:, : part_ref.shape[1]]


def last_kernel(cfg, *refs):
    tok, frames, channels, base, depth, level_count, heads, part_rows = cfg
    g_ref, hpart_ref, xq_ref = refs[:3]
    own = refs[3 : 3 + STEPS - 1]
    velocity_ref, queue_ref, tbuf = refs[3 + STEPS - 1 :]
    tok_index = lax.axis_index("tok")
    velocity, moved = advance(level_count, tok, None, g_ref, hpart_ref, xq_ref)
    for s in range(STEPS - 1):
        velocity_ref[s, 0] = own[s][...]
    velocity_ref[STEPS - 1, 0] = own_rows(velocity[:, :tok], tok, part_rows, tok_index, tbuf)
    queue_ref[0] = own_rows(moved[:, :tok], tok, part_rows, tok_index, tbuf)


def body(
    latent,
    fresh_noise,
    frame_slot,
    frame_reach,
    level_embed,
    embed_weight,
    qkv_weight,
    qk_gain,
    out_weight,
    vel_weight,
):
    frames, parts = lax.axis_size("queue"), lax.axis_size("tok")
    position = lax.axis_index("queue")
    part_rows, channels = latent.shape[1], latent.shape[2]
    tok = part_rows * parts
    level_count = level_embed.shape[0]
    depth = qkv_weight.shape[2]
    width = qkv_weight.shape[1]
    spare = round_up(width, 2 * LANES) - width
    if spare:
        qkv_weight = jnp.pad(qkv_weight, ((0, 0), (0, spare), (0, 0)))
        qk_gain = jnp.pad(qk_gain, ((0, 0), (0, spare)))
        out_weight = jnp.pad(out_weight, ((0, spare), (0, 0)))
        width += spare
    heads = width // HD
    base = round_up(channels + level_count + 1, LANES)
    cfg = (tok, frames, channels, base, depth, level_count, heads, part_rows)
    vmem, smem, hbm, anywhere = (
        pl.BlockSpec(memory_space=pltpu.VMEM),
        pl.BlockSpec(memory_space=pltpu.SMEM),
        pl.BlockSpec(memory_space=pltpu.HBM),
        pl.BlockSpec(memory_space=pl.ANY),
    )
    shape = jax.ShapeDtypeStruct

    def swapped(value, axis, distance):
        count = lax.axis_size(axis)
        return lax.ppermute(value, axis, [(source, source ^ distance) for source in range(count)])

    def from_ahead(value, distance):
        return lax.ppermute(value, "tok", [(source, (source - distance) % parts) for source in range(parts)])

    share = depth // parts
    table = (embed_weight, level_embed, vel_weight.T)
    tables = [from_ahead(piece, d) for d in range(1, parts) for piece in table]
    noise = [from_ahead(fresh_noise, d) for d in range(1, parts)]
    in_hbm = lambda array: pltpu.with_memory_space_constraint(array, pltpu.HBM)
    table = tuple(in_hbm(piece) for piece in table)
    qkv_weight, out_weight = in_hbm(qkv_weight), in_hbm(out_weight)
    rows = 256
    chunks = 2 * width // rows

    def weights(count, second, after, *operands):
        shares = max(1, count - 1)
        if count == 0 and second:
            outs = [shape((base, width), F32), shape((channels, width), F32), shape((base + channels, base), F32)]
        elif count == 0:
            outs = [shape((base, 2 * width), F32)]
        elif second:
            outs = [
                shape((width, 2 * base), BF16),
                shape((2 * channels, width), BF16),
                shape((base + channels, 2 * base), BF16),
            ]
        else:
            outs = [shape((width, 2 * base), BF16), shape((2 * base, width), BF16)]
        scratch = [pltpu.VMEM((shares, chunks, rows, share), BF16), pltpu.SemaphoreType.DMA((shares, chunks))]
        if count == 0:
            held = [pltpu.VMEM(piece.shape, BF16) for piece in table]
            scratch = held + [pltpu.SemaphoreType.DMA((3,))] + scratch
        return pl.pallas_call(
            functools.partial(weights_kernel, rows, base, count, second),
            out_shape=tuple(outs),
            in_specs=[hbm if count == 0 else vmem] * len(operands) + [hbm] * 2 + [anywhere] * len(after),
            out_specs=(vmem,) * len(outs),
            scratch_shapes=scratch,
            compiler_params=pltpu.CompilerParams(vmem_limit_bytes=24 * 2**20),
            cost_estimate=pl.CostEstimate(
                flops=4 * base * width * share * shares,
                bytes_accessed=4 * width * share * shares,
                transcendentals=0,
            ),
            name="weights",
        )(*operands, qkv_weight, out_weight, *after)

    state = latent
    work = [
        lambda *after: weights(0, False, after, *table),
        lambda *after: weights(0, True, after, *table),
        lambda *after: weights(parts, False, after, *tables, *done[0]),
        lambda *after: weights(parts, True, after, *tables, *done[1]),
    ]
    done, after = [], ()
    distance = frames // 2
    while distance:
        moved = swapped(state, "queue", distance)
        if len(done) < len(work):
            moved, noise, result = lax.optimization_barrier((moved, noise, work[len(done)](*after)))
            done.append(result)
            after = (moved,)
        axis = 2 if distance == frames // 2 else 0
        state = lax.optimization_barrier(jnp.concatenate([state, moved], axis=axis))
        distance //= 2
    while len(done) < len(work):
        done.append(work[len(done)]())
    latents = [state] + [from_ahead(state, d) for d in range(1, parts)] + noise
    mq, mk = done[2]
    mv, wo, gram = done[3]

    query_block = max(1, LANES // tok)
    owned = []
    for step in range(STEPS):
        n_query = query_block + 2 * HALO * (STEPS - 1 - step)
        query_lanes, key_lanes = n_query * tok, (n_query + 2 * HALO) * tok
        args = [frame_slot, frame_reach]
        specs = [smem, smem]
        if step == 0:
            args += latents
            specs += [vmem] * len(latents)
        else:
            args += [gathered, hpart, xq]
            specs += [vmem] * 3
        if step < STEPS - 1:
            args += [fresh_noise]
            specs += [vmem]
        args += [qk_gain, mq, mk, mv, wo, gram]
        specs += [vmem] * 6
        outs = [shape((channels, query_lanes), F32)] * 3
        if step > 0:
            outs += [shape((part_rows, channels), F32)]
        window = (2 * HALO + query_block) * tok
        result = pl.pallas_call(
            functools.partial(step_kernel, step, cfg),
            out_shape=tuple(outs),
            in_specs=specs,
            out_specs=(vmem,) * len(outs),
            scratch_shapes=[
                pltpu.VMEM((key_lanes, width), BF16),
                pltpu.VMEM((width, key_lanes), BF16),
                pltpu.VMEM((width, query_lanes), BF16),
                pltpu.VMEM((width, query_lanes), BF16),
                pltpu.VMEM((tok, channels), F32),
                pltpu.VMEM((key_lanes if step == 0 else tok, channels), F32),
            ],
            compiler_params=pltpu.CompilerParams(vmem_limit_bytes=48 * 2**20),
            cost_estimate=pl.CostEstimate(
                flops=4 * query_lanes * window * width + 12 * key_lanes * base * width,
                bytes_accessed=8 * width * base,
                transcendentals=query_lanes * window * heads,
            ),
            name="step%d" % step,
        )(*args)
        part, hpart, xq = result[:3]
        owned += list(result[3:])
        gathered = lax.all_gather(part, "tok", axis=0, tiled=False)

    return tuple(
        pl.pallas_call(
            functools.partial(last_kernel, cfg),
            out_shape=(
                shape((STEPS, 1, part_rows, channels), F32),
                shape((1, part_rows, channels), F32),
            ),
            in_specs=[vmem] * (3 + len(owned)),
            out_specs=(vmem, vmem),
            scratch_shapes=[pltpu.VMEM((tok, channels), F32)],
            compiler_params=pltpu.CompilerParams(vmem_limit_bytes=8 * 2**20),
            name="last",
        )(gathered, hpart, xq, *owned)
    )


def solution(mesh):
    return jax.shard_map(
        body,
        mesh=mesh,
        in_specs=(
            P("queue", "tok", None),
            P(None, "tok", None),
            P(),
            P(),
            P(None, "tok"),
            P(None, "tok"),
            P(None, "tok", None),
            P(None, "tok"),
            P("tok", None),
            P("tok", None),
        ),
        out_specs=(P(None, "queue", "tok", None), P("queue", "tok", None)),
        check_vma=False,
    )
```

```python
import functools
import math

import jax
import jax.numpy as jnp
from jax import lax
from jax.experimental import pallas as pl
from jax.experimental.pallas import tpu as pltpu
from jax.sharding import PartitionSpec as P

HD = 64
STEPS = 3
HALO = 3
LANES = 128
EPS = 1e-06
F32, BF16 = jnp.float32, jnp.bfloat16


def round_up(value, unit):
    return -(-value // unit) * unit


def dot(a, b):
    return jnp.dot(a, b, preferred_element_type=F32)


def dot_nt(a, b):
    return lax.dot_general(a, b, (((1,), (1,)), ((), ())), preferred_element_type=F32)


def halves(value, axis):
    high = value.astype(BF16)
    low = (value - high.astype(F32)).astype(BF16)
    return jnp.concatenate([high, low], axis=axis)


def chunk_copies(rows, chunks, parts, qkv_hbm, out_hbm, buf, sems):
    per = out_hbm.shape[0] // rows
    depth = buf.shape[-1]
    index, count = lax.axis_index("tok"), lax.axis_size("tok")
    copies = {}
    for place, chunk in enumerate(chunks):
        source = qkv_hbm.at[chunk // per] if chunk < 3 * per else out_hbm
        for at, part in enumerate(parts):
            columns = pl.ds(pl.multiple_of(lax.rem(index + part, count) * depth, LANES), depth)
            copies[place, at] = pltpu.make_async_copy(
                source.at[pl.ds((chunk % per) * rows, rows), columns],
                buf.at[at, place],
                sems.at[place, at],
            )
    return copies


def started(sources, targets, sems):
    copies = [pltpu.make_async_copy(a, b, sems.at[i]) for i, (a, b) in enumerate(zip(sources, targets))]
    for copy in copies:
        copy.start()
    return copies


def turned(value):
    return value.astype(F32).T.astype(BF16)


def keys_kernel(rows, base, shares, *refs):
    own, count = shares == (0,), len(shares)
    tables, refs = refs[: 2 * count], refs[2 * count :]
    if own:
        qkv_hbm, out_hbm = refs[:2]
        total_ref, gram_ref, right_ref, embed, level, small, buf, sems = refs[-8:]
        brought = started(tables, (embed, level), small)
    else:
        sum_ref, gram_sum, qkv_hbm, out_hbm = refs[:4]
        mq_ref, mk_ref, gram_ref, right_ref, buf, sems = refs[-6:]
    per = out_hbm.shape[0] // rows
    depth = buf.shape[-1]
    copies = chunk_copies(rows, range(2 * per), shares, qkv_hbm, out_hbm, buf, sems)
    for copy in copies.values():
        copy.start()
    if own:
        for copy in brought:
            copy.wait()
        tables = (embed, level)
    gram = jnp.zeros((base, base), F32) if own else gram_sum[...]
    for at in range(count):
        left = [tables[2 * at][...].astype(F32), tables[2 * at + 1][...].astype(F32)]
        left.append(jnp.zeros((base - left[0].shape[0] - left[1].shape[0], depth), F32))
        left = jnp.concatenate(left, axis=0)
        right_ref[at * depth : (at + 1) * depth, :] = left.T.astype(BF16)
        gram = gram + dot(left.astype(BF16), right_ref[at * depth : (at + 1) * depth, :])
    gram_ref[...] = gram if own else halves(gram, 1)
    for chunk in range(2 * per):
        spot = slice(chunk * rows, (chunk + 1) * rows)
        total = None if own else sum_ref[spot, :]
        for at in range(count):
            copies[chunk, at].wait()
            product = dot(buf[at, chunk], right_ref[at * depth : (at + 1) * depth, :])
            total = product if total is None else total + product
        where = slice((chunk % per) * rows, (chunk % per + 1) * rows)
        if own:
            total_ref[spot, :] = total
        elif chunk < per:
            mq_ref[where, :] = halves(total, 1)
        else:
            mk_ref[:, where] = halves(total.T, 0)


def values_kernel(rows, shares, *refs):
    own, count = shares == (0,), len(shares)
    tables, right_ref, refs = refs[:count], refs[count], refs[count + 1 :]
    if own:
        qkv_hbm, out_hbm = refs[:2]
        mv_ref, wo_ref, gv_ref, held, small, buf, sems = refs[-7:]
        brought = started(tables, (held,), small)
    else:
        mv_sum, wo_sum, gv_sum, qkv_hbm, out_hbm = refs[:5]
        mv_ref, wo_ref, gv_ref, buf, sems = refs[-5:]
    per = out_hbm.shape[0] // rows
    depth = buf.shape[-1]
    copies = chunk_copies(rows, range(2 * per, 4 * per), shares, qkv_hbm, out_hbm, buf, sems)
    for copy in copies.values():
        copy.start()
    if own:
        brought[0].wait()
        tables = (held,)
    vels = [table[...] for table in tables]
    gv = sum(dot(vel, right_ref[at * depth : (at + 1) * depth, :]) for at, vel in enumerate(vels))
    gv_ref[...] = gv if own else halves(gv_sum[...] + gv, 1)
    downs = [turned(vel) for vel in vels]
    for place in range(2 * per):
        where = slice((place % per) * rows, (place % per + 1) * rows)
        total = None if own else (mv_sum if place < per else wo_sum)[where, :]
        for at in range(count):
            copies[place, at].wait()
            right = right_ref[at * depth : (at + 1) * depth, :] if place < per else downs[at]
            product = dot(buf[at, place], right)
            total = product if total is None else total + product
        if own:
            (mv_ref if place < per else wo_ref)[where, :] = total
        elif place < per:
            mv_ref[where, :] = halves(total, 1)
        else:
            wo_ref[:, where] = halves(total.T, 0)


def advance(level_count, tok, first, g_ref, hpart_ref, xq_ref):
    shared = g_ref[0]
    for t in range(1, g_ref.shape[0]):
        shared = shared + g_ref[t]
    velocity = shared + hpart_ref[...]
    moved = xq_ref[...] - velocity * (1.0 / level_count)
    if first is None:
        return velocity, moved
    lane_frame = lax.broadcasted_iota(jnp.int32, (1, shared.shape[1]), 1) // tok
    return velocity, jnp.where(lane_frame + first == -1, shared, moved)


def own_rows(block, tok, part_rows, index, scratch):
    scratch[...] = block.T
    return scratch[pl.ds(pl.multiple_of(index * part_rows, 8), part_rows), :]


def step_kernel(step, cfg, *refs):
    tok, frames, channels, base, depth, level_count, heads, part_rows = cfg
    query_block = max(1, LANES // tok)
    n_query = query_block + 2 * HALO * (STEPS - 1 - step)
    n_key = n_query + 2 * HALO
    key_lanes, query_lanes = n_key * tok, n_query * tok
    width = heads * HD
    window = (2 * HALO + query_block) * tok
    position, tok_index = lax.axis_index("queue"), lax.axis_index("tok")
    first_key = position - HALO - (HALO + 1) * (STEPS - 1 - step)
    refs = list(refs)
    slot_ref, reach_ref = refs[0], refs[1]
    if step == 0:
        count = tok // part_rows
        lat_refs, noise_refs = refs[2 : 2 + count], refs[2 + count : 1 + 2 * count]
        refs = refs[1 + 2 * count :]
    else:
        g_ref, hprev_ref, xprev_ref = refs[2:5]
        refs = refs[5:]
    fresh_ref = None
    if step < STEPS - 1:
        fresh_ref = refs.pop(0)
    gain_ref, mq_ref, mk_ref, mv_ref, wo_ref, gram_ref, gv_ref = refs[:7]
    refs = refs[7:]
    part_ref, hpart_ref, xq_ref = refs[:3]
    refs = refs[3:]
    own_ref = None
    if step > 0:
        own_ref = refs.pop(0)
    kbuf, vbuf, qbuf, att, tbuf, xbuf = refs

    if step == 0:
        noise = [fresh_ref[0]] + [ref[0] for ref in noise_refs]
        for w in range(n_key):
            source = lax.rem(first_key - 1 + w + 2 * frames, frames)
            apart, bits = position ^ source, frames.bit_length() - 2
            second = ((apart >> bits) & 1) == 1
            entry = sum(((apart >> bit) & 1) << (bits - 1 - bit) for bit in range(bits))
            for t in range(count):
                at = lax.rem(tok_index + t, count) * part_rows + w * tok
                beside = lat_refs[t][entry]
                rows = jnp.where(second, beside[:, channels:], beside[:, :channels])
                rows = jnp.where(source == frames - 1, noise[t], rows)
                xbuf[pl.ds(pl.multiple_of(at, 8), part_rows), :] = rows
        state = xbuf[...].T
    else:
        velocity, state = advance(level_count, tok, first_key - 1, g_ref, hprev_ref, xprev_ref)
        mine = (HALO + 1) * (STEPS - step)
        own_ref[...] = own_rows(velocity[:, mine * tok : (mine + 1) * tok], tok, part_rows, tok_index, tbuf)

    key_frame = lax.broadcasted_iota(jnp.int32, (1, key_lanes), 1) // tok
    level_row = jnp.full((1, key_lanes), -1, jnp.int32)
    for w in range(n_key):
        frame = first_key + w
        known = slot_ref[jnp.clip(frame - step - 1, 0, frames - 1)] + step
        level_row = jnp.where(key_frame == w, jnp.where(frame >= step + 1, known, frame), level_row)
    row = lax.broadcasted_iota(jnp.int32, (base - channels, key_lanes), 0)
    aug_t = jnp.concatenate([state, jnp.where(row == level_row, 1.0, 0.0)], axis=0)
    aug_t = aug_t.astype(BF16).astype(F32)
    aug_tb = aug_t.astype(BF16)
    both_t = jnp.concatenate([aug_tb, aug_tb], axis=0)
    mean_t = jnp.sum(dot(gram_ref[...], both_t) * aug_t, axis=0, keepdims=True) * (1.0 / depth)
    mean_t = jnp.maximum(mean_t, 0.0) + EPS
    queries = slice(HALO * tok, HALO * tok + query_lanes)
    mean_q = mean_t[:, queries]
    aug_qb = aug_t[:, queries].astype(BF16)
    both_q = jnp.concatenate([aug_qb, aug_qb], axis=0)
    last_row = lax.broadcasted_iota(jnp.int32, (base, key_lanes), 0) == base - 1
    aug = jnp.where(last_row, EPS * mean_t, aug_t).T
    eps_c = aug[:, base - 1 : base]
    aug_b = aug.astype(BF16)
    both = jnp.concatenate([aug_b, aug_b], axis=1)

    hpart_ref[...] = dot(gv_ref[...], both_q)
    xq_ref[...] = state[:, queries]

    gain = gain_ref[0:1, :] * gain_ref[1:2, :] * (HD ** -0.5 * math.log2(math.e))
    span = 256 if width % 256 == 0 else 128
    head_of = lambda axis: lax.broadcasted_iota(jnp.int32, (span, span), axis) // HD
    average = jnp.where(head_of(0) == head_of(1), 1.0 / HD, 0.0).astype(BF16)
    for at in range(0, width, span):
        raw = dot(both, mk_ref[:, at : at + span])
        spread = dot((raw * raw).astype(BF16), average)
        kbuf[:, at : at + span] = (raw * lax.rsqrt(spread + eps_c) * gain[:, at : at + span]).astype(BF16)
    vbuf[...] = (dot(mv_ref[...], both_t) * lax.rsqrt(mean_t)).astype(BF16)
    raw = dot(mq_ref[...], both_q).reshape(heads, HD, query_lanes)
    spread = jnp.sum(raw * raw, axis=1, keepdims=True) * (1.0 / HD)
    qbuf[...] = (raw * lax.rsqrt(spread + EPS * mean_q)[:, :, :]).reshape(width, query_lanes).astype(BF16)

    bound = HD * jnp.max(gain, axis=1, keepdims=True)
    upper = lax.broadcasted_iota(jnp.int32, (2 * HD, LANES), 0) < HD
    lane = lax.broadcasted_iota(jnp.int32, (1, 2 * LANES), 1)
    within = lax.rem(lane, LANES) // tok

    def place(b):
        lead = (b * LANES) // tok
        keys = pl.ds(pl.multiple_of(lead * tok, LANES), window)
        return lead, keys, pl.ds(pl.multiple_of(b * LANES, LANES), LANES)

    def biases(lead, shift):
        rows = []
        for k in range(2 * HALO + query_block):
            target = first_key + lead + k
            inside = (target >= 0) & (target < frames)
            row = jnp.zeros((1, 2 * LANES), F32)
            for j in range(query_block):
                frame = first_key + HALO + lead + j
                reach = reach_ref[jnp.clip(frame, 0, frames - 1)]
                unused = (frame < 0) | (frame >= frames)
                counted = (inside & (abs(k - HALO - j) <= reach)) | unused
                row = jnp.where(within == j, jnp.where(counted, 0.0, -1e30), row)
            rows.append(row - shift)
        return rows

    def scores(keys, lanes, cols, rows):
        query = qbuf[cols, lanes]
        zero = jnp.zeros_like(query)
        query = jnp.concatenate([jnp.where(upper, query, zero), jnp.where(upper, zero, query)], axis=1)
        score = dot(kbuf[keys, cols], query)
        return jnp.concatenate([score[k * tok : (k + 1) * tok] + rows[k] for k in range(len(rows))], axis=0)

    def mix(keys, lanes, cols, weight):
        ones = jnp.ones((16, window), BF16)
        mixed = dot(jnp.concatenate([vbuf[cols, keys], ones], axis=0), weight.astype(BF16))
        total = mixed[2 * HD : 2 * HD + 1, :]
        scale = 1.0 / total
        top = mixed[:HD, :LANES] * scale[:, :LANES]
        bottom = mixed[HD : 2 * HD, LANES:] * scale[:, LANES:]
        att[cols, lanes] = jnp.concatenate([top, bottom], axis=0).astype(BF16)
        return total

    def block(b, least):
        lead, keys, lanes = place(b)
        rows = biases(lead, bound)
        held = None
        for pair in range(heads // 2):
            cols = slice(pair * 2 * HD, (pair + 1) * 2 * HD)
            weight = jnp.exp2(scores(keys, lanes, cols, rows)).astype(BF16)
            if held is not None:
                least = jnp.minimum(least, mix(keys, lanes, *held))
            held = (cols, weight)
        return jnp.minimum(least, mix(keys, lanes, *held))

    def exact_block(at, carry):
        lead, keys, lanes = place(at // (heads // 2))
        cols = pl.ds(pl.multiple_of(lax.rem(at, heads // 2) * 2 * HD, 2 * HD), 2 * HD)
        score = scores(keys, lanes, cols, biases(lead, 0.0))
        mix(keys, lanes, cols, jnp.exp2(score - jnp.max(score, axis=0, keepdims=True)))
        return carry

    blocks = query_lanes // LANES
    least = jnp.ones((1, 2 * LANES), F32)
    least = block(0, least) if blocks == 1 else lax.fori_loop(0, blocks, block, least)

    @pl.when(jnp.min(least) < 1e-25)
    def _():
        lax.fori_loop(0, blocks * (heads // 2), exact_block, 0)

    mixed = dot(wo_ref[...], att[...])
    partial = mixed[:channels] + mixed[channels:]
    if step < STEPS - 1:
        tbuf[...] = jnp.zeros_like(tbuf)
        tbuf[pl.ds(pl.multiple_of(tok_index * part_rows, 8), part_rows), :] = fresh_ref[step + 1]
        fresh_t = tbuf[...].T
        fresh_t = jnp.concatenate([fresh_t] * n_query, axis=1)
        slot = lax.broadcasted_iota(jnp.int32, (1, query_lanes), 1) // tok + first_key + HALO
        partial = jnp.where(slot == -1, fresh_t, partial)
    part_ref[...] = partial[:, : part_ref.shape[1]]


def last_kernel(cfg, *refs):
    tok, frames, channels, base, depth, level_count, heads, part_rows = cfg
    g_ref, hpart_ref, xq_ref = refs[:3]
    own = refs[3 : 3 + STEPS - 1]
    velocity_ref, queue_ref, tbuf = refs[3 + STEPS - 1 :]
    tok_index = lax.axis_index("tok")
    velocity, moved = advance(level_count, tok, None, g_ref, hpart_ref, xq_ref)
    for s in range(STEPS - 1):
        velocity_ref[s, 0] = own[s][...]
    velocity_ref[STEPS - 1, 0] = own_rows(velocity[:, :tok], tok, part_rows, tok_index, tbuf)
    queue_ref[0] = own_rows(moved[:, :tok], tok, part_rows, tok_index, tbuf)


def body(
    latent,
    fresh_noise,
    frame_slot,
    frame_reach,
    level_embed,
    embed_weight,
    qkv_weight,
    qk_gain,
    out_weight,
    vel_weight,
):
    frames, parts = lax.axis_size("queue"), lax.axis_size("tok")
    position = lax.axis_index("queue")
    part_rows, channels = latent.shape[1], latent.shape[2]
    tok = part_rows * parts
    level_count = level_embed.shape[0]
    depth = qkv_weight.shape[2]
    width = qkv_weight.shape[1]
    spare = round_up(width, 2 * LANES) - width
    if spare:
        qkv_weight = jnp.pad(qkv_weight, ((0, 0), (0, spare), (0, 0)))
        qk_gain = jnp.pad(qk_gain, ((0, 0), (0, spare)))
        out_weight = jnp.pad(out_weight, ((0, spare), (0, 0)))
        width += spare
    heads = width // HD
    base = round_up(channels + level_count + 1, LANES)
    cfg = (tok, frames, channels, base, depth, level_count, heads, part_rows)
    vmem, smem, hbm, anywhere = (
        pl.BlockSpec(memory_space=pltpu.VMEM),
        pl.BlockSpec(memory_space=pltpu.SMEM),
        pl.BlockSpec(memory_space=pltpu.HBM),
        pl.BlockSpec(memory_space=pl.ANY),
    )
    shape = jax.ShapeDtypeStruct

    def swapped(value, axis, distance):
        count = lax.axis_size(axis)
        return lax.ppermute(value, axis, [(source, source ^ distance) for source in range(count)])

    def from_ahead(value, distance):
        return lax.ppermute(value, "tok", [(source, (source - distance) % parts) for source in range(parts)])

    share = depth // parts
    table = (embed_weight, level_embed, vel_weight.T)
    around = range(1, parts)
    tables = [from_ahead(piece, d) for d in around for piece in table[:2]]
    vel_tables = [from_ahead(table[2], d) for d in around]
    noise = [from_ahead(fresh_noise, d) for d in around]
    in_hbm = lambda array: pltpu.with_memory_space_constraint(array, pltpu.HBM)
    table = tuple(in_hbm(piece) for piece in table)
    qkv_weight, out_weight = in_hbm(qkv_weight), in_hbm(out_weight)
    rows = 384 if width % 384 == 0 else 256
    chunks = 2 * width // rows

    def weights(kernel, shares, outs, held, after, *operands):
        count = len(shares)
        scratch = [pltpu.VMEM(piece.shape, BF16) for piece in held]
        if held:
            scratch.append(pltpu.SemaphoreType.DMA((len(held),)))
        scratch += [pltpu.VMEM((count, chunks, rows, share), BF16), pltpu.SemaphoreType.DMA((chunks, count))]
        return pl.pallas_call(
            functools.partial(kernel, shares),
            out_shape=tuple(outs),
            in_specs=[hbm] * len(held)
            + [vmem] * (len(operands) - len(held))
            + [hbm] * 2
            + [anywhere] * len(after),
            out_specs=(vmem,) * len(outs),
            scratch_shapes=scratch,
            compiler_params=pltpu.CompilerParams(vmem_limit_bytes=24 * 2**20),
            cost_estimate=pl.CostEstimate(
                flops=4 * base * width * share * count,
                bytes_accessed=4 * width * share * count,
                transcendentals=0,
            ),
            name="weights",
        )(*operands, qkv_weight, out_weight, *after)

    keys_part = lambda shares, *refs: keys_kernel(rows, base, shares, *refs)
    values_part = lambda shares, *refs: values_kernel(rows, shares, *refs)
    right = lambda count: shape((count * share, base), BF16)
    others = tuple(around)

    def own_keys(*after):
        outs = [shape((2 * width, base), F32), shape((base, base), F32), right(1)]
        return weights(keys_part, (0,), outs, table[:2], after, *table[:2])

    def own_values(*after):
        outs = [shape((width, base), F32), shape((width, channels), F32), shape((channels, base), F32)]
        return weights(values_part, (0,), outs, table[2:], after, table[2], done[0][2])

    def other_keys(*after):
        outs = [
            shape((width, 2 * base), BF16),
            shape((2 * base, width), BF16),
            shape((base, 2 * base), BF16),
            right(parts - 1),
        ]
        return weights(keys_part, others, outs, (), after, *tables, *done[0][:2])

    def other_values(*after):
        outs = [
            shape((width, 2 * base), BF16),
            shape((2 * channels, width), BF16),
            shape((channels, 2 * base), BF16),
        ]
        return weights(values_part, others, outs, (), after, *vel_tables, done[2][3], *done[1])

    state = latent
    work = [own_keys, own_values, other_keys, other_values]
    done, after = [], ()
    distance = frames // 2
    while distance:
        moved = swapped(state, "queue", distance)
        if len(done) < len(work):
            moved, noise, result = lax.optimization_barrier((moved, noise, work[len(done)](*after)))
            done.append(result)
            after = (moved,)
        axis = 2 if distance == frames // 2 else 0
        state = lax.optimization_barrier(jnp.concatenate([state, moved], axis=axis))
        distance //= 2
    while len(done) < len(work):
        done.append(work[len(done)]())
    latents = [state] + [from_ahead(state, d) for d in range(1, parts)] + noise
    mq, mk, gram = done[2][:3]
    mv, wo, gv = done[3]

    query_block = max(1, LANES // tok)
    owned = []
    for step in range(STEPS):
        n_query = query_block + 2 * HALO * (STEPS - 1 - step)
        query_lanes, key_lanes = n_query * tok, (n_query + 2 * HALO) * tok
        args = [frame_slot, frame_reach]
        specs = [smem, smem]
        if step == 0:
            args += latents
            specs += [vmem] * len(latents)
        else:
            args += [gathered, hpart, xq]
            specs += [vmem] * 3
        if step < STEPS - 1:
            args += [fresh_noise]
            specs += [vmem]
        args += [qk_gain, mq, mk, mv, wo, gram, gv]
        specs += [vmem] * 7
        outs = [shape((channels, query_lanes), F32)] * 3
        if step > 0:
            outs += [shape((part_rows, channels), F32)]
        window = (2 * HALO + query_block) * tok
        result = pl.pallas_call(
            functools.partial(step_kernel, step, cfg),
            out_shape=tuple(outs),
            in_specs=specs,
            out_specs=(vmem,) * len(outs),
            scratch_shapes=[
                pltpu.VMEM((key_lanes, width), BF16),
                pltpu.VMEM((width, key_lanes), BF16),
                pltpu.VMEM((width, query_lanes), BF16),
                pltpu.VMEM((width, query_lanes), BF16),
                pltpu.VMEM((tok, channels), F32),
                pltpu.VMEM((key_lanes if step == 0 else tok, channels), F32),
            ],
            compiler_params=pltpu.CompilerParams(vmem_limit_bytes=48 * 2**20),
            cost_estimate=pl.CostEstimate(
                flops=4 * query_lanes * window * width + 12 * key_lanes * base * width,
                bytes_accessed=8 * width * base,
                transcendentals=query_lanes * window * heads,
            ),
            name="step%d" % step,
        )(*args)
        part, hpart, xq = result[:3]
        owned += list(result[3:])
        gathered = lax.all_gather(part, "tok", axis=0, tiled=False)

    return tuple(
        pl.pallas_call(
            functools.partial(last_kernel, cfg),
            out_shape=(
                shape((STEPS, 1, part_rows, channels), F32),
                shape((1, part_rows, channels), F32),
            ),
            in_specs=[vmem] * (3 + len(owned)),
            out_specs=(vmem, vmem),
            scratch_shapes=[pltpu.VMEM((tok, channels), F32)],
            compiler_params=pltpu.CompilerParams(vmem_limit_bytes=8 * 2**20),
            name="last",
        )(gathered, hpart, xq, *owned)
    )


def solution(mesh):
    return jax.shard_map(
        body,
        mesh=mesh,
        in_specs=(
            P("queue", "tok", None),
            P(None, "tok", None),
            P(),
            P(),
            P(None, "tok"),
            P(None, "tok"),
            P(None, "tok", None),
            P(None, "tok"),
            P("tok", None),
            P("tok", None),
        ),
        out_specs=(P(None, "queue", "tok", None), P("queue", "tok", None)),
        check_vma=False,
    )
```

```python
import functools
import math

import jax
import jax.numpy as jnp
from jax import lax
from jax.experimental import pallas as pl
from jax.experimental.pallas import tpu as pltpu
from jax.sharding import PartitionSpec as P

HD = 64
STEPS = 3
HALO = 3
LANES = 128
EPS = 1e-06
F32, BF16 = jnp.float32, jnp.bfloat16


def round_up(value, unit):
    return -(-value // unit) * unit


def dot(a, b):
    return jnp.dot(a, b, preferred_element_type=F32)


def dot_nt(a, b):
    return lax.dot_general(a, b, (((1,), (1,)), ((), ())), preferred_element_type=F32)


def halves(value, axis):
    high = value.astype(BF16)
    low = (value - high.astype(F32)).astype(BF16)
    return jnp.concatenate([high, low], axis=axis)


def started(sources, targets, sems):
    copies = [pltpu.make_async_copy(a, b, sems.at[i]) for i, (a, b) in enumerate(zip(sources, targets))]
    for copy in copies:
        copy.start()
    return copies


def fetched(rows, weight, buf, sems):
    half = buf.shape[-1]
    return {
        (at, side): pltpu.make_async_copy(
            weight.at[pl.ds(at * rows, rows), pl.ds(side * half, half)], buf.at[at, side], sems.at[at, side]
        )
        for at in range(buf.shape[0])
        for side in range(2)
    }


def weigh(rows, across, copies, buf, table_ref, out_ref):
    half = buf.shape[-1]
    for at in range(buf.shape[0]):
        total = 0.0
        for side in range(2):
            copies[at, side].wait()
            total = total + dot(buf[at, side], table_ref[side * half : (side + 1) * half, :])
        if across:
            out_ref[:, at * rows : (at + 1) * rows] = halves(total.T, 0)
        else:
            out_ref[at * rows : (at + 1) * rows, :] = halves(total, 1)


def first_weights_kernel(rows, base, parts, *refs):
    tables, weight = refs[: 3 * parts], refs[3 * parts].at[0]
    out_ref, right_ref, down_ref, gram_ref, gv_ref = refs[3 * parts + 1 : 3 * parts + 6]
    held, small, buf, sems = refs[-6:-3], refs[-3], refs[-2], refs[-1]
    brought = started(tables[:3], held, small)
    copies = fetched(rows, weight, buf, sems)
    for copy in copies.values():
        copy.start()
    for copy in brought:
        copy.wait()
    tables = tuple(held) + tables[3:]
    share = tables[0].shape[1]
    index = lax.axis_index("tok")
    gram = gv = 0.0
    for at in range(parts):
        spot = pl.ds(pl.multiple_of(lax.rem(index + at, parts) * share, LANES), share)
        left = [tables[3 * at][...].astype(F32), tables[3 * at + 1][...].astype(F32)]
        left.append(jnp.zeros((base - left[0].shape[0] - left[1].shape[0], share), F32))
        left = jnp.concatenate(left, axis=0)
        right = left.T.astype(BF16)
        vel = tables[3 * at + 2][...]
        right_ref[spot, :] = right
        down_ref[spot, :] = vel.astype(F32).T.astype(BF16)
        gram = gram + dot(left.astype(BF16), right)
        gv = gv + dot(vel, right)
    gram_ref[...] = halves(gram, 1)
    gv_ref[...] = halves(gv, 1)
    weigh(rows, False, copies, buf, right_ref, out_ref)


def weights_kernel(rows, across, kind, weight, table_ref, *refs):
    out_ref, buf, sems = refs[-3:]
    copies = fetched(rows, weight if kind is None else weight.at[kind], buf, sems)
    for copy in copies.values():
        copy.start()
    weigh(rows, across, copies, buf, table_ref, out_ref)


def advance(level_count, tok, first, g_ref, hpart_ref, xq_ref):
    shared = g_ref[0]
    for t in range(1, g_ref.shape[0]):
        shared = shared + g_ref[t]
    velocity = shared + hpart_ref[...]
    moved = xq_ref[...] - velocity * (1.0 / level_count)
    if first is None:
        return velocity, moved
    lane_frame = lax.broadcasted_iota(jnp.int32, (1, shared.shape[1]), 1) // tok
    return velocity, jnp.where(lane_frame + first == -1, shared, moved)


def own_rows(block, tok, part_rows, index, scratch):
    scratch[...] = block.T
    return scratch[pl.ds(pl.multiple_of(index * part_rows, 8), part_rows), :]


def step_kernel(step, cfg, *refs):
    tok, frames, channels, base, depth, level_count, heads, part_rows = cfg
    query_block = max(1, LANES // tok)
    n_query = query_block + 2 * HALO * (STEPS - 1 - step)
    n_key = n_query + 2 * HALO
    key_lanes, query_lanes = n_key * tok, n_query * tok
    width = heads * HD
    window = (2 * HALO + query_block) * tok
    position, tok_index = lax.axis_index("queue"), lax.axis_index("tok")
    first_key = position - HALO - (HALO + 1) * (STEPS - 1 - step)
    refs = list(refs)
    slot_ref, reach_ref = refs[0], refs[1]
    if step == 0:
        count = tok // part_rows
        lat_refs, noise_refs = refs[2 : 2 + count], refs[2 + count : 1 + 2 * count]
        refs = refs[1 + 2 * count :]
    else:
        g_ref, hprev_ref, xprev_ref = refs[2:5]
        refs = refs[5:]
    fresh_ref = None
    if step < STEPS - 1:
        fresh_ref = refs.pop(0)
    gain_ref, mq_ref, mk_ref, mv_ref, wo_ref, gram_ref, gv_ref = refs[:7]
    refs = refs[7:]
    part_ref, hpart_ref, xq_ref = refs[:3]
    refs = refs[3:]
    own_ref = None
    if step > 0:
        own_ref = refs.pop(0)
    kbuf, vbuf, qbuf, att, tbuf, xbuf = refs

    if step == 0:
        noise = [fresh_ref[0]] + [ref[0] for ref in noise_refs]
        for w in range(n_key):
            source = lax.rem(first_key - 1 + w + 2 * frames, frames)
            apart, bits = position ^ source, frames.bit_length() - 2
            second = ((apart >> bits) & 1) == 1
            entry = sum(((apart >> bit) & 1) << (bits - 1 - bit) for bit in range(bits))
            for t in range(count):
                at = lax.rem(tok_index + t, count) * part_rows + w * tok
                beside = lat_refs[t][entry]
                rows = jnp.where(second, beside[:, channels:], beside[:, :channels])
                rows = jnp.where(source == frames - 1, noise[t], rows)
                xbuf[pl.ds(pl.multiple_of(at, 8), part_rows), :] = rows
        state = xbuf[...].T
    else:
        velocity, state = advance(level_count, tok, first_key - 1, g_ref, hprev_ref, xprev_ref)
        mine = (HALO + 1) * (STEPS - step)
        own_ref[...] = own_rows(velocity[:, mine * tok : (mine + 1) * tok], tok, part_rows, tok_index, tbuf)

    key_frame = lax.broadcasted_iota(jnp.int32, (1, key_lanes), 1) // tok
    level_row = jnp.full((1, key_lanes), -1, jnp.int32)
    for w in range(n_key):
        frame = first_key + w
        known = slot_ref[jnp.clip(frame - step - 1, 0, frames - 1)] + step
        level_row = jnp.where(key_frame == w, jnp.where(frame >= step + 1, known, frame), level_row)
    row = lax.broadcasted_iota(jnp.int32, (base - channels, key_lanes), 0)
    aug_t = jnp.concatenate([state, jnp.where(row == level_row, 1.0, 0.0)], axis=0)
    aug_t = aug_t.astype(BF16).astype(F32)
    aug_tb = aug_t.astype(BF16)
    both_t = jnp.concatenate([aug_tb, aug_tb], axis=0)
    mean_t = jnp.sum(dot(gram_ref[...], both_t) * aug_t, axis=0, keepdims=True) * (1.0 / depth)
    mean_t = jnp.maximum(mean_t, 0.0) + EPS
    queries = slice(HALO * tok, HALO * tok + query_lanes)
    mean_q = mean_t[:, queries]
    aug_qb = aug_t[:, queries].astype(BF16)
    both_q = jnp.concatenate([aug_qb, aug_qb], axis=0)
    last_row = lax.broadcasted_iota(jnp.int32, (base, key_lanes), 0) == base - 1
    aug = jnp.where(last_row, EPS * mean_t, aug_t).T
    eps_c = aug[:, base - 1 : base]
    aug_b = aug.astype(BF16)
    both = jnp.concatenate([aug_b, aug_b], axis=1)

    hpart_ref[...] = dot(gv_ref[...], both_q)
    xq_ref[...] = state[:, queries]

    gain = gain_ref[0:1, :] * gain_ref[1:2, :] * (HD ** -0.5 * math.log2(math.e))
    span = 256 if width % 256 == 0 else 128
    head_of = lambda axis: lax.broadcasted_iota(jnp.int32, (span, span), axis) // HD
    average = jnp.where(head_of(0) == head_of(1), 1.0 / HD, 0.0).astype(BF16)
    for at in range(0, width, span):
        raw = dot(both, mk_ref[:, at : at + span])
        spread = dot((raw * raw).astype(BF16), average)
        kbuf[:, at : at + span] = (raw * lax.rsqrt(spread + eps_c) * gain[:, at : at + span]).astype(BF16)
    vbuf[...] = (dot(mv_ref[...], both_t) * lax.rsqrt(mean_t)).astype(BF16)
    raw = dot(mq_ref[...], both_q).reshape(heads, HD, query_lanes)
    spread = jnp.sum(raw * raw, axis=1, keepdims=True) * (1.0 / HD)
    qbuf[...] = (raw * lax.rsqrt(spread + EPS * mean_q)[:, :, :]).reshape(width, query_lanes).astype(BF16)

    bound = HD * jnp.max(gain, axis=1, keepdims=True)
    upper = lax.broadcasted_iota(jnp.int32, (2 * HD, LANES), 0) < HD
    lane = lax.broadcasted_iota(jnp.int32, (1, 2 * LANES), 1)
    within = lax.rem(lane, LANES) // tok

    def place(b):
        lead = (b * LANES) // tok
        keys = pl.ds(pl.multiple_of(lead * tok, LANES), window)
        return lead, keys, pl.ds(pl.multiple_of(b * LANES, LANES), LANES)

    def biases(lead, shift):
        rows = []
        for k in range(2 * HALO + query_block):
            target = first_key + lead + k
            inside = (target >= 0) & (target < frames)
            row = jnp.zeros((1, 2 * LANES), F32)
            for j in range(query_block):
                frame = first_key + HALO + lead + j
                reach = reach_ref[jnp.clip(frame, 0, frames - 1)]
                unused = (frame < 0) | (frame >= frames)
                counted = (inside & (abs(k - HALO - j) <= reach)) | unused
                row = jnp.where(within == j, jnp.where(counted, 0.0, -1e30), row)
            rows.append(row - shift)
        return rows

    def scores(keys, lanes, cols, rows):
        query = qbuf[cols, lanes]
        zero = jnp.zeros_like(query)
        query = jnp.concatenate([jnp.where(upper, query, zero), jnp.where(upper, zero, query)], axis=1)
        score = dot(kbuf[keys, cols], query)
        return jnp.concatenate([score[k * tok : (k + 1) * tok] + rows[k] for k in range(len(rows))], axis=0)

    def mix(keys, lanes, cols, weight):
        ones = jnp.ones((16, window), BF16)
        mixed = dot(jnp.concatenate([vbuf[cols, keys], ones], axis=0), weight.astype(BF16))
        total = mixed[2 * HD : 2 * HD + 1, :]
        scale = 1.0 / total
        top = mixed[:HD, :LANES] * scale[:, :LANES]
        bottom = mixed[HD : 2 * HD, LANES:] * scale[:, LANES:]
        att[cols, lanes] = jnp.concatenate([top, bottom], axis=0).astype(BF16)
        return total

    def block(b, least):
        lead, keys, lanes = place(b)
        rows = biases(lead, bound)
        held = None
        for pair in range(heads // 2):
            cols = slice(pair * 2 * HD, (pair + 1) * 2 * HD)
            weight = jnp.exp2(scores(keys, lanes, cols, rows)).astype(BF16)
            if held is not None:
                least = jnp.minimum(least, mix(keys, lanes, *held))
            held = (cols, weight)
        return jnp.minimum(least, mix(keys, lanes, *held))

    def exact_block(at, carry):
        lead, keys, lanes = place(at // (heads // 2))
        cols = pl.ds(pl.multiple_of(lax.rem(at, heads // 2) * 2 * HD, 2 * HD), 2 * HD)
        score = scores(keys, lanes, cols, biases(lead, 0.0))
        mix(keys, lanes, cols, jnp.exp2(score - jnp.max(score, axis=0, keepdims=True)))
        return carry

    blocks = query_lanes // LANES
    least = jnp.ones((1, 2 * LANES), F32)
    least = block(0, least) if blocks == 1 else lax.fori_loop(0, blocks, block, least)

    @pl.when(jnp.min(least) < 1e-25)
    def _():
        lax.fori_loop(0, blocks * (heads // 2), exact_block, 0)

    mixed = dot(wo_ref[...], att[...])
    partial = mixed[:channels] + mixed[channels:]
    if step < STEPS - 1:
        tbuf[...] = jnp.zeros_like(tbuf)
        tbuf[pl.ds(pl.multiple_of(tok_index * part_rows, 8), part_rows), :] = fresh_ref[step + 1]
        fresh_t = tbuf[...].T
        fresh_t = jnp.concatenate([fresh_t] * n_query, axis=1)
        slot = lax.broadcasted_iota(jnp.int32, (1, query_lanes), 1) // tok + first_key + HALO
        partial = jnp.where(slot == -1, fresh_t, partial)
    part_ref[...] = partial[:, : part_ref.shape[1]]


def last_kernel(cfg, *refs):
    tok, frames, channels, base, depth, level_count, heads, part_rows = cfg
    g_ref, hpart_ref, xq_ref = refs[:3]
    own = refs[3 : 3 + STEPS - 1]
    velocity_ref, queue_ref, tbuf = refs[3 + STEPS - 1 :]
    tok_index = lax.axis_index("tok")
    velocity, moved = advance(level_count, tok, None, g_ref, hpart_ref, xq_ref)
    for s in range(STEPS - 1):
        velocity_ref[s, 0] = own[s][...]
    velocity_ref[STEPS - 1, 0] = own_rows(velocity[:, :tok], tok, part_rows, tok_index, tbuf)
    queue_ref[0] = own_rows(moved[:, :tok], tok, part_rows, tok_index, tbuf)


def body(
    latent,
    fresh_noise,
    frame_slot,
    frame_reach,
    level_embed,
    embed_weight,
    qkv_weight,
    qk_gain,
    out_weight,
    vel_weight,
):
    frames, parts = lax.axis_size("queue"), lax.axis_size("tok")
    position = lax.axis_index("queue")
    part_rows, channels = latent.shape[1], latent.shape[2]
    tok = part_rows * parts
    level_count = level_embed.shape[0]
    depth = qkv_weight.shape[2]
    width = qkv_weight.shape[1]
    spare = round_up(width, 2 * LANES) - width
    if spare:
        qkv_weight = jnp.pad(qkv_weight, ((0, 0), (0, spare), (0, 0)))
        qk_gain = jnp.pad(qk_gain, ((0, 0), (0, spare)))
        out_weight = jnp.pad(out_weight, ((0, spare), (0, 0)))
        width += spare
    heads = width // HD
    base = round_up(channels + level_count + 1, LANES)
    cfg = (tok, frames, channels, base, depth, level_count, heads, part_rows)
    vmem, smem, hbm, anywhere = (
        pl.BlockSpec(memory_space=pltpu.VMEM),
        pl.BlockSpec(memory_space=pltpu.SMEM),
        pl.BlockSpec(memory_space=pltpu.HBM),
        pl.BlockSpec(memory_space=pl.ANY),
    )
    shape = jax.ShapeDtypeStruct

    def swapped(value, axis, distance):
        count = lax.axis_size(axis)
        return lax.ppermute(value, axis, [(source, source ^ distance) for source in range(count)])

    def from_ahead(value, distance):
        return lax.ppermute(value, "tok", [(source, (source - distance) % parts) for source in range(parts)])

    share = depth // parts
    table = (embed_weight, level_embed, vel_weight.T)
    around = range(1, parts)
    tables = [from_ahead(piece, d) for d in around for piece in table]
    noise = [from_ahead(fresh_noise, d) for d in around]
    rows = 384 if width % 384 == 0 else 256

    in_hbm = lambda array: pltpu.with_memory_space_constraint(array, pltpu.HBM)
    qkv_weight, out_weight = in_hbm(qkv_weight), in_hbm(out_weight)
    fetching = [
        pltpu.VMEM((width // rows, 2, rows, depth // 2), BF16),
        pltpu.SemaphoreType.DMA((width // rows, 2)),
    ]
    price = pl.CostEstimate(flops=4 * base * width * depth, bytes_accessed=2 * width * depth, transcendentals=0)

    def first_weights():
        return pl.pallas_call(
            functools.partial(first_weights_kernel, rows, base, parts),
            out_shape=(
                shape((width, 2 * base), BF16),
                shape((depth, base), BF16),
                shape((depth, channels), BF16),
                shape((base, 2 * base), BF16),
                shape((channels, 2 * base), BF16),
            ),
            in_specs=[hbm] * 3 + [vmem] * len(tables) + [hbm],
            out_specs=(vmem,) * 5,
            scratch_shapes=[pltpu.VMEM(piece.shape, BF16) for piece in table]
            + [pltpu.SemaphoreType.DMA((3,))]
            + fetching,
            compiler_params=pltpu.CompilerParams(vmem_limit_bytes=24 * 2**20),
            cost_estimate=price,
            name="first_weights",
        )(*map(in_hbm, table), *tables, qkv_weight)

    def weights(weight, kind, at, across, *after):
        factor = done[0][at]
        wide = 2 * factor.shape[1]
        return pl.pallas_call(
            functools.partial(weights_kernel, rows, across, kind),
            out_shape=shape((wide, width) if across else (width, wide), BF16),
            in_specs=[hbm, vmem] + [anywhere] * len(after),
            out_specs=vmem,
            scratch_shapes=fetching,
            compiler_params=pltpu.CompilerParams(vmem_limit_bytes=24 * 2**20),
            cost_estimate=price,
            name="weights",
        )(weight, factor, *after)

    state = latent
    work = [
        first_weights,
        functools.partial(weights, qkv_weight, 1, 1, True),
        functools.partial(weights, qkv_weight, 2, 1, False),
        functools.partial(weights, out_weight, None, 2, True),
    ]
    done, after = [], ()
    distance = frames // 2
    while distance:
        moved = swapped(state, "queue", distance)
        if len(done) < len(work):
            moved, noise, result = lax.optimization_barrier((moved, noise, work[len(done)](*after)))
            done.append(result)
            after = (moved,)
        axis = 2 if distance == frames // 2 else 0
        state = lax.optimization_barrier(jnp.concatenate([state, moved], axis=axis))
        distance //= 2
    while len(done) < len(work):
        done.append(work[len(done)]())
    latents = [state] + [from_ahead(state, d) for d in range(1, parts)] + noise
    (mq, _, _, gram, gv), mk, mv, wo = done

    query_block = max(1, LANES // tok)
    owned = []
    for step in range(STEPS):
        n_query = query_block + 2 * HALO * (STEPS - 1 - step)
        query_lanes, key_lanes = n_query * tok, (n_query + 2 * HALO) * tok
        args = [frame_slot, frame_reach]
        specs = [smem, smem]
        if step == 0:
            args += latents
            specs += [vmem] * len(latents)
        else:
            args += [gathered, hpart, xq]
            specs += [vmem] * 3
        if step < STEPS - 1:
            args += [fresh_noise]
            specs += [vmem]
        args += [qk_gain, mq, mk, mv, wo, gram, gv]
        specs += [vmem] * 7
        outs = [shape((channels, query_lanes), F32)] * 3
        if step > 0:
            outs += [shape((part_rows, channels), F32)]
        window = (2 * HALO + query_block) * tok
        result = pl.pallas_call(
            functools.partial(step_kernel, step, cfg),
            out_shape=tuple(outs),
            in_specs=specs,
            out_specs=(vmem,) * len(outs),
            scratch_shapes=[
                pltpu.VMEM((key_lanes, width), BF16),
                pltpu.VMEM((width, key_lanes), BF16),
                pltpu.VMEM((width, query_lanes), BF16),
                pltpu.VMEM((width, query_lanes), BF16),
                pltpu.VMEM((tok, channels), F32),
                pltpu.VMEM((key_lanes if step == 0 else tok, channels), F32),
            ],
            compiler_params=pltpu.CompilerParams(vmem_limit_bytes=48 * 2**20),
            cost_estimate=pl.CostEstimate(
                flops=4 * query_lanes * window * width + 12 * key_lanes * base * width,
                bytes_accessed=8 * width * base,
                transcendentals=query_lanes * window * heads,
            ),
            name="step%d" % step,
        )(*args)
        part, hpart, xq = result[:3]
        owned += list(result[3:])
        gathered = lax.all_gather(part, "tok", axis=0, tiled=False)

    return tuple(
        pl.pallas_call(
            functools.partial(last_kernel, cfg),
            out_shape=(
                shape((STEPS, 1, part_rows, channels), F32),
                shape((1, part_rows, channels), F32),
            ),
            in_specs=[vmem] * (3 + len(owned)),
            out_specs=(vmem, vmem),
            scratch_shapes=[pltpu.VMEM((tok, channels), F32)],
            compiler_params=pltpu.CompilerParams(vmem_limit_bytes=8 * 2**20),
            name="last",
        )(gathered, hpart, xq, *owned)
    )


def solution(mesh):
    return jax.shard_map(
        body,
        mesh=mesh,
        in_specs=(
            P("queue", "tok", None),
            P(None, "tok", None),
            P(),
            P(),
            P(None, "tok"),
            P(None, "tok"),
            P(None, "tok", None),
            P(None, "tok"),
            P("tok", None),
            P("tok", None),
        ),
        out_specs=(P(None, "queue", "tok", None), P("queue", "tok", None)),
        check_vma=False,
    )
```

```python
import functools
import math

import jax
import jax.numpy as jnp
from jax import lax
from jax.experimental import pallas as pl
from jax.experimental.pallas import tpu as pltpu
from jax.sharding import PartitionSpec as P

HD = 64
STEPS = 3
HALO = 3
LANES = 128
EPS = 1e-06
F32, BF16 = jnp.float32, jnp.bfloat16


def round_up(value, unit):
    return -(-value // unit) * unit


def dot(a, b):
    return jnp.dot(a, b, preferred_element_type=F32)


def dot_nt(a, b):
    return lax.dot_general(a, b, (((1,), (1,)), ((), ())), preferred_element_type=F32)


def halves(value, axis):
    high = value.astype(BF16)
    low = (value - high.astype(F32)).astype(BF16)
    return jnp.concatenate([high, low], axis=axis)


def chunk_copies(rows, chunks, parts, qkv_hbm, out_hbm, buf, sems):
    per = out_hbm.shape[0] // rows
    depth = buf.shape[-1]
    index, count = lax.axis_index("tok"), lax.axis_size("tok")
    copies = {}
    for place, chunk in enumerate(chunks):
        source = qkv_hbm.at[chunk // per] if chunk < 3 * per else out_hbm
        for at, part in enumerate(parts):
            columns = pl.ds(pl.multiple_of(lax.rem(index + part, count) * depth, LANES), depth)
            copies[place, at] = pltpu.make_async_copy(
                source.at[pl.ds((chunk % per) * rows, rows), columns],
                buf.at[at, place],
                sems.at[place, at],
            )
    return copies


def started(sources, targets, sems):
    copies = [pltpu.make_async_copy(a, b, sems.at[i]) for i, (a, b) in enumerate(zip(sources, targets))]
    for copy in copies:
        copy.start()
    return copies


def turned(value):
    return value.astype(F32).T.astype(BF16)


def keys_kernel(rows, base, shares, *refs):
    own, count = shares == (0,), len(shares)
    tables, refs = refs[: 2 * count], refs[2 * count :]
    if own:
        qkv_hbm, out_hbm = refs[:2]
        total_ref, gram_ref, right_ref, embed, level, small, buf, sems = refs[-8:]
        brought = started(tables, (embed, level), small)
    else:
        sum_ref, gram_sum, qkv_hbm, out_hbm = refs[:4]
        mq_ref, mk_ref, gram_ref, right_ref, buf, sems = refs[-6:]
    per = out_hbm.shape[0] // rows
    depth = buf.shape[-1]
    copies = chunk_copies(rows, range(2 * per), shares, qkv_hbm, out_hbm, buf, sems)
    for copy in copies.values():
        copy.start()
    if own:
        for copy in brought:
            copy.wait()
        tables = (embed, level)
    gram = jnp.zeros((base, base), F32) if own else gram_sum[...]
    for at in range(count):
        left = [tables[2 * at][...].astype(F32), tables[2 * at + 1][...].astype(F32)]
        left.append(jnp.zeros((base - left[0].shape[0] - left[1].shape[0], depth), F32))
        left = jnp.concatenate(left, axis=0)
        right_ref[at * depth : (at + 1) * depth, :] = left.T.astype(BF16)
        gram = gram + dot(left.astype(BF16), right_ref[at * depth : (at + 1) * depth, :])
    gram_ref[...] = gram if own else halves(gram, 1)
    for chunk in range(2 * per):
        spot = slice(chunk * rows, (chunk + 1) * rows)
        total = None if own else sum_ref[spot, :]
        for at in range(count):
            copies[chunk, at].wait()
            product = dot(buf[at, chunk], right_ref[at * depth : (at + 1) * depth, :])
            total = product if total is None else total + product
        where = slice((chunk % per) * rows, (chunk % per + 1) * rows)
        if own:
            total_ref[spot, :] = total
        elif chunk < per:
            mq_ref[where, :] = halves(total, 1)
        else:
            mk_ref[:, where] = halves(total.T, 0)


def values_kernel(rows, shares, *refs):
    own, count = shares == (0,), len(shares)
    tables, right_ref, refs = refs[:count], refs[count], refs[count + 1 :]
    if own:
        qkv_hbm, out_hbm = refs[:2]
        mv_ref, wo_ref, gv_ref, held, small, buf, sems = refs[-7:]
        brought = started(tables, (held,), small)
    else:
        mv_sum, wo_sum, gv_sum, qkv_hbm, out_hbm = refs[:5]
        mv_ref, wo_ref, gv_ref, buf, sems = refs[-5:]
    per = out_hbm.shape[0] // rows
    depth = buf.shape[-1]
    copies = chunk_copies(rows, range(2 * per, 4 * per), shares, qkv_hbm, out_hbm, buf, sems)
    for copy in copies.values():
        copy.start()
    if own:
        brought[0].wait()
        tables = (held,)
    vels = [table[...] for table in tables]
    gv = sum(dot(vel, right_ref[at * depth : (at + 1) * depth, :]) for at, vel in enumerate(vels))
    gv_ref[...] = gv if own else halves(gv_sum[...] + gv, 1)
    downs = [turned(vel) for vel in vels]
    for place in range(2 * per):
        where = slice((place % per) * rows, (place % per + 1) * rows)
        total = None if own else (mv_sum if place < per else wo_sum)[where, :]
        for at in range(count):
            copies[place, at].wait()
            right = right_ref[at * depth : (at + 1) * depth, :] if place < per else downs[at]
            product = dot(buf[at, place], right)
            total = product if total is None else total + product
        if own:
            (mv_ref if place < per else wo_ref)[where, :] = total
        elif place < per:
            mv_ref[where, :] = halves(total, 1)
        else:
            wo_ref[:, where] = halves(total.T, 0)


def advance(level_count, tok, first, g_ref, hpart_ref, xq_ref):
    shared = g_ref[0]
    for t in range(1, g_ref.shape[0]):
        shared = shared + g_ref[t]
    velocity = shared + hpart_ref[...]
    moved = xq_ref[...] - velocity * (1.0 / level_count)
    if first is None:
        return velocity, moved
    lane_frame = lax.broadcasted_iota(jnp.int32, (1, shared.shape[1]), 1) // tok
    return velocity, jnp.where(lane_frame + first == -1, shared, moved)


def own_rows(block, tok, part_rows, index, scratch):
    scratch[...] = block.T
    return scratch[pl.ds(pl.multiple_of(index * part_rows, 8), part_rows), :]


def step_kernel(step, cfg, *refs):
    tok, frames, channels, base, depth, level_count, heads, part_rows = cfg
    query_block = max(1, LANES // tok)
    n_query = query_block + 2 * HALO * (STEPS - 1 - step)
    n_key = n_query + 2 * HALO
    key_lanes, query_lanes = n_key * tok, n_query * tok
    width = heads * HD
    position, tok_index = lax.axis_index("queue"), lax.axis_index("tok")
    first_key = position - HALO - (HALO + 1) * (STEPS - 1 - step)
    refs = list(refs)
    slot_ref, reach_ref = refs[0], refs[1]
    if step == 0:
        count = tok // part_rows
        lat_refs, noise_refs = refs[2 : 2 + count], refs[2 + count : 1 + 2 * count]
        refs = refs[1 + 2 * count :]
    else:
        g_ref, hprev_ref, xprev_ref = refs[2:5]
        refs = refs[5:]
    fresh_ref = None
    if step < STEPS - 1:
        fresh_ref = refs.pop(0)
    gain_ref, mq_ref, mk_ref, mv_ref, wo_ref, gram_ref, gv_ref = refs[:7]
    refs = refs[7:]
    part_ref, hpart_ref, xq_ref = refs[:3]
    refs = refs[3:]
    own_ref = None
    if step > 0:
        own_ref = refs.pop(0)
    kbuf, vbuf, qbuf, att, tbuf, xbuf = refs

    if step == 0:
        noise = [fresh_ref[0]] + [ref[0] for ref in noise_refs]
        for w in range(n_key):
            source = lax.rem(first_key - 1 + w + 2 * frames, frames)
            apart, bits = position ^ source, frames.bit_length() - 2
            second = ((apart >> bits) & 1) == 1
            entry = sum(((apart >> bit) & 1) << (bits - 1 - bit) for bit in range(bits))
            for t in range(count):
                at = lax.rem(tok_index + t, count) * part_rows + w * tok
                beside = lat_refs[t][entry]
                rows = jnp.where(second, beside[:, channels:], beside[:, :channels])
                rows = jnp.where(source == frames - 1, noise[t], rows)
                xbuf[pl.ds(pl.multiple_of(at, 8), part_rows), :] = rows
        state = xbuf[...].T
    else:
        velocity, state = advance(level_count, tok, first_key - 1, g_ref, hprev_ref, xprev_ref)
        mine = (HALO + 1) * (STEPS - step)
        own_ref[...] = own_rows(velocity[:, mine * tok : (mine + 1) * tok], tok, part_rows, tok_index, tbuf)

    key_frame = lax.broadcasted_iota(jnp.int32, (1, key_lanes), 1) // tok
    level_row = jnp.full((1, key_lanes), -1, jnp.int32)
    for w in range(n_key):
        frame = first_key + w
        known = slot_ref[jnp.clip(frame - step - 1, 0, frames - 1)] + step
        level_row = jnp.where(key_frame == w, jnp.where(frame >= step + 1, known, frame), level_row)
    row = lax.broadcasted_iota(jnp.int32, (base - channels, key_lanes), 0)
    aug_t = jnp.concatenate([state, jnp.where(row == level_row, 1.0, 0.0)], axis=0)
    aug_t = aug_t.astype(BF16).astype(F32)
    aug_tb = aug_t.astype(BF16)
    both_t = jnp.concatenate([aug_tb, aug_tb], axis=0)
    mean_t = jnp.sum(dot(gram_ref[...], both_t) * aug_t, axis=0, keepdims=True) * (1.0 / depth)
    mean_t = jnp.maximum(mean_t, 0.0) + EPS
    queries = slice(HALO * tok, HALO * tok + query_lanes)
    mean_q = mean_t[:, queries]
    aug_qb = aug_t[:, queries].astype(BF16)
    both_q = jnp.concatenate([aug_qb, aug_qb], axis=0)
    last_row = lax.broadcasted_iota(jnp.int32, (base, key_lanes), 0) == base - 1
    aug = jnp.where(last_row, EPS * mean_t, aug_t).T
    eps_c = aug[:, base - 1 : base]
    aug_b = aug.astype(BF16)
    both = jnp.concatenate([aug_b, aug_b], axis=1)

    hpart_ref[...] = dot(gv_ref[...], both_q)
    xq_ref[...] = state[:, queries]

    gain = gain_ref[0:1, :] * gain_ref[1:2, :] * (HD ** -0.5 * math.log2(math.e))
    span = 256 if width % 256 == 0 else 128
    head_of = lambda axis: lax.broadcasted_iota(jnp.int32, (span, span), axis) // HD
    average = jnp.where(head_of(0) == head_of(1), 1.0 / HD, 0.0).astype(BF16)
    for at in range(0, width, span):
        raw = dot(both, mk_ref[:, at : at + span])
        spread = dot((raw * raw).astype(BF16), average)
        kbuf[:, at : at + span] = (raw * lax.rsqrt(spread + eps_c) * gain[:, at : at + span]).astype(BF16)
    vbuf[...] = (dot(mv_ref[...], both_t) * lax.rsqrt(mean_t)).astype(BF16)
    raw = dot(mq_ref[...], both_q).reshape(heads, HD, query_lanes)
    spread = jnp.sum(raw * raw, axis=1, keepdims=True) * (1.0 / HD)
    qbuf[...] = (raw * lax.rsqrt(spread + EPS * mean_q)[:, :, :]).reshape(width, query_lanes).astype(BF16)

    bound = HD * jnp.max(gain, axis=1, keepdims=True)
    upper = lax.broadcasted_iota(jnp.int32, (2 * HD, LANES), 0) < HD
    lane = lax.broadcasted_iota(jnp.int32, (1, 2 * LANES), 1)
    within = lax.rem(lane, LANES) // tok

    full = 2 * HALO + query_block
    if query_block == 1:
        cuts = [(HALO - r, 2 * r + 1) for r in range(HALO + 1)]
    else:
        cuts = [(2, full - 4), (2, full - 2), (0, full - 2), (0, full)]

    def reaches(lead):
        widths = []
        for j in range(query_block):
            frame = first_key + HALO + lead + j
            needed = (frame >= 0) & (frame < frames) & (lead + j <= n_query - query_block)
            widths.append(jnp.where(needed, reach_ref[jnp.clip(frame, 0, frames - 1)], -1))
        return widths

    def biases(lead, shift):
        rows, widths = [], reaches(lead)
        for k in range(full):
            target = first_key + lead + k
            inside = (target >= 0) & (target < frames)
            row = jnp.zeros((1, 2 * LANES), F32)
            for j in range(query_block):
                counted = (inside & (abs(k - HALO - j) <= widths[j])) | (widths[j] < 0)
                row = jnp.where(within == j, jnp.where(counted, 0.0, -1e30), row)
            rows.append(row - shift)
        return rows

    def span_of(first, count):
        return pl.ds(pl.multiple_of(first * tok, LANES), count * tok)

    def scores(keys, lanes, cols, rows):
        query = qbuf[cols, lanes]
        zero = jnp.zeros_like(query)
        query = jnp.concatenate([jnp.where(upper, query, zero), jnp.where(upper, zero, query)], axis=1)
        score = dot(kbuf[keys, cols], query)
        return jnp.concatenate([score[k * tok : (k + 1) * tok] + rows[k] for k in range(len(rows))], axis=0)

    def mix(keys, lanes, cols, weight):
        ones = jnp.ones((16, weight.shape[0]), BF16)
        mixed = dot(jnp.concatenate([vbuf[cols, keys], ones], axis=0), weight.astype(BF16))
        total = mixed[2 * HD : 2 * HD + 1, :]
        scale = 1.0 / total
        top = mixed[:HD, :LANES] * scale[:, :LANES]
        bottom = mixed[HD : 2 * HD, LANES:] * scale[:, LANES:]
        att[cols, lanes] = jnp.concatenate([top, bottom], axis=0).astype(BF16)
        return total

    def block(b, least):
        lead = (b * LANES) // tok
        lanes = pl.ds(pl.multiple_of(b * LANES, LANES), LANES)
        rows, widths = biases(lead, bound), reaches(lead)

        def run(first, count, least):
            keys = span_of(lead + first, count)
            held = None
            for pair in range(heads // 2):
                cols = slice(pair * 2 * HD, (pair + 1) * 2 * HD)
                weight = jnp.exp2(scores(keys, lanes, cols, rows[first : first + count])).astype(BF16)
                if held is not None:
                    least = jnp.minimum(least, mix(keys, lanes, *held))
                held = (cols, weight)
            return jnp.minimum(least, mix(keys, lanes, *held))

        if query_block == 1:
            chosen = jnp.maximum(widths[0], 0)
        else:
            left, right = widths[0], widths[0] - query_block + 1
            for j in range(1, query_block):
                left = jnp.maximum(left, widths[j] - j)
                right = jnp.maximum(right, widths[j] + j - query_block + 1)
            chosen = jnp.where(left > 1, 2, 0) + jnp.where(right > 1, 1, 0)
        return lax.switch(chosen, [functools.partial(run, *cut) for cut in cuts], least)

    def exact_block(at, carry):
        lead = (at // (heads // 2) * LANES) // tok
        keys = span_of(lead, full)
        lanes = pl.ds(pl.multiple_of(at // (heads // 2) * LANES, LANES), LANES)
        cols = pl.ds(pl.multiple_of(lax.rem(at, heads // 2) * 2 * HD, 2 * HD), 2 * HD)
        score = scores(keys, lanes, cols, biases(lead, 0.0))
        mix(keys, lanes, cols, jnp.exp2(score - jnp.max(score, axis=0, keepdims=True)))
        return carry

    blocks = query_lanes // LANES
    least = jnp.ones((1, 2 * LANES), F32)
    least = block(0, least) if blocks == 1 else lax.fori_loop(0, blocks, block, least)

    @pl.when(jnp.min(least) < 1e-25)
    def _():
        lax.fori_loop(0, blocks * (heads // 2), exact_block, 0)

    mixed = dot(wo_ref[...], att[...])
    partial = mixed[:channels] + mixed[channels:]
    if step < STEPS - 1:
        tbuf[...] = jnp.zeros_like(tbuf)
        tbuf[pl.ds(pl.multiple_of(tok_index * part_rows, 8), part_rows), :] = fresh_ref[step + 1]
        fresh_t = tbuf[...].T
        fresh_t = jnp.concatenate([fresh_t] * n_query, axis=1)
        slot = lax.broadcasted_iota(jnp.int32, (1, query_lanes), 1) // tok + first_key + HALO
        partial = jnp.where(slot == -1, fresh_t, partial)
    part_ref[...] = partial[:, : part_ref.shape[1]]


def last_kernel(cfg, *refs):
    tok, frames, channels, base, depth, level_count, heads, part_rows = cfg
    g_ref, hpart_ref, xq_ref = refs[:3]
    own = refs[3 : 3 + STEPS - 1]
    velocity_ref, queue_ref, tbuf = refs[3 + STEPS - 1 :]
    tok_index = lax.axis_index("tok")
    velocity, moved = advance(level_count, tok, None, g_ref, hpart_ref, xq_ref)
    for s in range(STEPS - 1):
        velocity_ref[s, 0] = own[s][...]
    velocity_ref[STEPS - 1, 0] = own_rows(velocity[:, :tok], tok, part_rows, tok_index, tbuf)
    queue_ref[0] = own_rows(moved[:, :tok], tok, part_rows, tok_index, tbuf)


def body(
    latent,
    fresh_noise,
    frame_slot,
    frame_reach,
    level_embed,
    embed_weight,
    qkv_weight,
    qk_gain,
    out_weight,
    vel_weight,
):
    frames, parts = lax.axis_size("queue"), lax.axis_size("tok")
    position = lax.axis_index("queue")
    part_rows, channels = latent.shape[1], latent.shape[2]
    tok = part_rows * parts
    level_count = level_embed.shape[0]
    depth = qkv_weight.shape[2]
    width = qkv_weight.shape[1]
    spare = round_up(width, 2 * LANES) - width
    if spare:
        qkv_weight = jnp.pad(qkv_weight, ((0, 0), (0, spare), (0, 0)))
        qk_gain = jnp.pad(qk_gain, ((0, 0), (0, spare)))
        out_weight = jnp.pad(out_weight, ((0, spare), (0, 0)))
        width += spare
    heads = width // HD
    base = round_up(channels + level_count + 1, LANES)
    cfg = (tok, frames, channels, base, depth, level_count, heads, part_rows)
    vmem, smem, hbm, anywhere = (
        pl.BlockSpec(memory_space=pltpu.VMEM),
        pl.BlockSpec(memory_space=pltpu.SMEM),
        pl.BlockSpec(memory_space=pltpu.HBM),
        pl.BlockSpec(memory_space=pl.ANY),
    )
    shape = jax.ShapeDtypeStruct

    def swapped(value, axis, distance):
        count = lax.axis_size(axis)
        return lax.ppermute(value, axis, [(source, source ^ distance) for source in range(count)])

    def from_ahead(value, distance):
        return lax.ppermute(value, "tok", [(source, (source - distance) % parts) for source in range(parts)])

    share = depth // parts
    table = (embed_weight, level_embed, vel_weight.T)
    around = range(1, parts)
    tables = [from_ahead(piece, d) for d in around for piece in table[:2]]
    vel_tables = [from_ahead(table[2], d) for d in around]
    noise = [from_ahead(fresh_noise, d) for d in around]
    in_hbm = lambda array: pltpu.with_memory_space_constraint(array, pltpu.HBM)
    table = tuple(in_hbm(piece) for piece in table)
    qkv_weight, out_weight = in_hbm(qkv_weight), in_hbm(out_weight)
    rows = 384 if width % 384 == 0 else 256
    chunks = 2 * width // rows

    def weights(kernel, shares, outs, held, after, *operands):
        count = len(shares)
        scratch = [pltpu.VMEM(piece.shape, BF16) for piece in held]
        if held:
            scratch.append(pltpu.SemaphoreType.DMA((len(held),)))
        scratch += [pltpu.VMEM((count, chunks, rows, share), BF16), pltpu.SemaphoreType.DMA((chunks, count))]
        return pl.pallas_call(
            functools.partial(kernel, shares),
            out_shape=tuple(outs),
            in_specs=[hbm] * len(held)
            + [vmem] * (len(operands) - len(held))
            + [hbm] * 2
            + [anywhere] * len(after),
            out_specs=(vmem,) * len(outs),
            scratch_shapes=scratch,
            compiler_params=pltpu.CompilerParams(vmem_limit_bytes=24 * 2**20),
            cost_estimate=pl.CostEstimate(
                flops=4 * base * width * share * count,
                bytes_accessed=4 * width * share * count,
                transcendentals=0,
            ),
            name="weights",
        )(*operands, qkv_weight, out_weight, *after)

    keys_part = lambda shares, *refs: keys_kernel(rows, base, shares, *refs)
    values_part = lambda shares, *refs: values_kernel(rows, shares, *refs)
    right = lambda count: shape((count * share, base), BF16)
    others = tuple(around)

    def own_keys(*after):
        outs = [shape((2 * width, base), F32), shape((base, base), F32), right(1)]
        return weights(keys_part, (0,), outs, table[:2], after, *table[:2])

    def own_values(*after):
        outs = [shape((width, base), F32), shape((width, channels), F32), shape((channels, base), F32)]
        return weights(values_part, (0,), outs, table[2:], after, table[2], done[0][2])

    def other_keys(*after):
        outs = [
            shape((width, 2 * base), BF16),
            shape((2 * base, width), BF16),
            shape((base, 2 * base), BF16),
            right(parts - 1),
        ]
        return weights(keys_part, others, outs, (), after, *tables, *done[0][:2])

    def other_values(*after):
        outs = [
            shape((width, 2 * base), BF16),
            shape((2 * channels, width), BF16),
            shape((channels, 2 * base), BF16),
        ]
        return weights(values_part, others, outs, (), after, *vel_tables, done[2][3], *done[1])

    state = latent
    work = [own_keys, own_values, other_keys, other_values]
    done, after = [], ()
    distance = frames // 2
    while distance:
        moved = swapped(state, "queue", distance)
        if len(done) < len(work):
            moved, noise, result = lax.optimization_barrier((moved, noise, work[len(done)](*after)))
            done.append(result)
            after = (moved,)
        axis = 2 if distance == frames // 2 else 0
        state = lax.optimization_barrier(jnp.concatenate([state, moved], axis=axis))
        distance //= 2
    while len(done) < len(work):
        done.append(work[len(done)]())
    latents = [state] + [from_ahead(state, d) for d in range(1, parts)] + noise
    mq, mk, gram = done[2][:3]
    mv, wo, gv = done[3]

    query_block = max(1, LANES // tok)
    owned = []
    for step in range(STEPS):
        n_query = query_block + 2 * HALO * (STEPS - 1 - step)
        query_lanes, key_lanes = n_query * tok, (n_query + 2 * HALO) * tok
        args = [frame_slot, frame_reach]
        specs = [smem, smem]
        if step == 0:
            args += latents
            specs += [vmem] * len(latents)
        else:
            args += [gathered, hpart, xq]
            specs += [vmem] * 3
        if step < STEPS - 1:
            args += [fresh_noise]
            specs += [vmem]
        args += [qk_gain, mq, mk, mv, wo, gram, gv]
        specs += [vmem] * 7
        outs = [shape((channels, query_lanes), F32)] * 3
        if step > 0:
            outs += [shape((part_rows, channels), F32)]
        window = (2 * HALO + query_block) * tok
        result = pl.pallas_call(
            functools.partial(step_kernel, step, cfg),
            out_shape=tuple(outs),
            in_specs=specs,
            out_specs=(vmem,) * len(outs),
            scratch_shapes=[
                pltpu.VMEM((key_lanes, width), BF16),
                pltpu.VMEM((width, key_lanes), BF16),
                pltpu.VMEM((width, query_lanes), BF16),
                pltpu.VMEM((width, query_lanes), BF16),
                pltpu.VMEM((tok, channels), F32),
                pltpu.VMEM((key_lanes if step == 0 else tok, channels), F32),
            ],
            compiler_params=pltpu.CompilerParams(vmem_limit_bytes=48 * 2**20),
            cost_estimate=pl.CostEstimate(
                flops=4 * query_lanes * window * width + 12 * key_lanes * base * width,
                bytes_accessed=8 * width * base,
                transcendentals=query_lanes * window * heads,
            ),
            name="step%d" % step,
        )(*args)
        part, hpart, xq = result[:3]
        owned += list(result[3:])
        gathered = lax.all_gather(part, "tok", axis=0, tiled=False)

    return tuple(
        pl.pallas_call(
            functools.partial(last_kernel, cfg),
            out_shape=(
                shape((STEPS, 1, part_rows, channels), F32),
                shape((1, part_rows, channels), F32),
            ),
            in_specs=[vmem] * (3 + len(owned)),
            out_specs=(vmem, vmem),
            scratch_shapes=[pltpu.VMEM((tok, channels), F32)],
            compiler_params=pltpu.CompilerParams(vmem_limit_bytes=8 * 2**20),
            name="last",
        )(gathered, hpart, xq, *owned)
    )


def solution(mesh):
    return jax.shard_map(
        body,
        mesh=mesh,
        in_specs=(
            P("queue", "tok", None),
            P(None, "tok", None),
            P(),
            P(),
            P(None, "tok"),
            P(None, "tok"),
            P(None, "tok", None),
            P(None, "tok"),
            P("tok", None),
            P("tok", None),
        ),
        out_specs=(P(None, "queue", "tok", None), P("queue", "tok", None)),
        check_vma=False,
    )
```

```python
import functools
import math

import jax
import jax.numpy as jnp
from jax import lax
from jax.experimental import pallas as pl
from jax.experimental.pallas import tpu as pltpu
from jax.sharding import PartitionSpec as P

HD = 64
STEPS = 3
HALO = 3
LANES = 128
EPS = 1e-06
F32, BF16 = jnp.float32, jnp.bfloat16


def round_up(value, unit):
    return -(-value // unit) * unit


def dot(a, b):
    return jnp.dot(a, b, preferred_element_type=F32)


def dot_nt(a, b):
    return lax.dot_general(a, b, (((1,), (1,)), ((), ())), preferred_element_type=F32)


def halves(value, axis):
    high = value.astype(BF16)
    low = (value - high.astype(F32)).astype(BF16)
    return jnp.concatenate([high, low], axis=axis)


def chunk_copies(rows, chunks, parts, qkv_hbm, out_hbm, buf, sems):
    per = out_hbm.shape[0] // rows
    depth = buf.shape[-1]
    index, count = lax.axis_index("tok"), lax.axis_size("tok")
    copies = {}
    for place, chunk in enumerate(chunks):
        source = qkv_hbm.at[chunk // per] if chunk < 3 * per else out_hbm
        for at, part in enumerate(parts):
            columns = pl.ds(pl.multiple_of(lax.rem(index + part, count) * depth, LANES), depth)
            copies[place, at] = pltpu.make_async_copy(
                source.at[pl.ds((chunk % per) * rows, rows), columns],
                buf.at[at, place],
                sems.at[place, at],
            )
    return copies


def started(sources, targets, sems):
    copies = [pltpu.make_async_copy(a, b, sems.at[i]) for i, (a, b) in enumerate(zip(sources, targets))]
    for copy in copies:
        copy.start()
    return copies


def turned(value):
    return value.astype(F32).T.astype(BF16)


def keys_kernel(rows, base, shares, *refs):
    own, count = shares == (0,), len(shares)
    tables, refs = refs[: 3 * count], refs[3 * count :]
    if own:
        qkv_hbm, out_hbm = refs[:2]
        total_ref, gram_ref, gv_ref, right_ref, down_ref, *held, small, buf, sems = refs[-11:]
        brought = started(tables, held, small)
    else:
        sum_ref, gram_sum, gv_sum, qkv_hbm, out_hbm = refs[:5]
        mq_ref, mk_ref, gram_ref, gv_ref, right_ref, down_ref, buf, sems = refs[-8:]
    per = out_hbm.shape[0] // rows
    depth = buf.shape[-1]
    copies = chunk_copies(rows, range(2 * per), shares, qkv_hbm, out_hbm, buf, sems)
    for copy in copies.values():
        copy.start()
    if own:
        for copy in brought:
            copy.wait()
        tables = held
    gram, gv = (0.0, 0.0) if own else (gram_sum[...], gv_sum[...])
    for at in range(count):
        spot = slice(at * depth, (at + 1) * depth)
        left = [tables[3 * at][...].astype(F32), tables[3 * at + 1][...].astype(F32)]
        left.append(jnp.zeros((base - left[0].shape[0] - left[1].shape[0], depth), F32))
        left = jnp.concatenate(left, axis=0)
        vel = tables[3 * at + 2][...]
        right_ref[spot, :] = left.T.astype(BF16)
        down_ref[spot, :] = turned(vel)
        gram = gram + dot(left.astype(BF16), right_ref[spot, :])
        gv = gv + dot(vel, right_ref[spot, :])
    gram_ref[...] = gram if own else halves(gram, 1)
    gv_ref[...] = gv if own else halves(gv, 1)
    for chunk in range(2 * per):
        spot = slice(chunk * rows, (chunk + 1) * rows)
        total = None if own else sum_ref[spot, :]
        for at in range(count):
            copies[chunk, at].wait()
            product = dot(buf[at, chunk], right_ref[at * depth : (at + 1) * depth, :])
            total = product if total is None else total + product
        where = slice((chunk % per) * rows, (chunk % per + 1) * rows)
        if own:
            total_ref[spot, :] = total
        elif chunk < per:
            mq_ref[where, :] = halves(total, 1)
        else:
            mk_ref[:, where] = halves(total.T, 0)


def values_kernel(rows, shares, right_ref, down_ref, *refs):
    own, count = shares == (0,), len(shares)
    sums, refs = ((), refs) if own else (refs[:2], refs[2:])
    qkv_hbm, out_hbm = refs[:2]
    mv_ref, wo_ref, buf, sems = refs[-4:]
    per = out_hbm.shape[0] // rows
    depth = buf.shape[-1]
    copies = chunk_copies(rows, range(2 * per, 4 * per), shares, qkv_hbm, out_hbm, buf, sems)
    for copy in copies.values():
        copy.start()
    for place in range(2 * per):
        where = slice((place % per) * rows, (place % per + 1) * rows)
        total = None if own else sums[place // per][where, :]
        factor = right_ref if place < per else down_ref
        for at in range(count):
            copies[place, at].wait()
            product = dot(buf[at, place], factor[at * depth : (at + 1) * depth, :])
            total = product if total is None else total + product
        if own:
            (mv_ref if place < per else wo_ref)[where, :] = total
        elif place < per:
            mv_ref[where, :] = halves(total, 1)
        else:
            wo_ref[:, where] = halves(total.T, 0)


def advance(level_count, tok, first, g_ref, hpart_ref, xq_ref):
    shared = g_ref[0]
    for t in range(1, g_ref.shape[0]):
        shared = shared + g_ref[t]
    velocity = shared + hpart_ref[...]
    moved = xq_ref[...] - velocity * (1.0 / level_count)
    if first is None:
        return velocity, moved
    lane_frame = lax.broadcasted_iota(jnp.int32, (1, shared.shape[1]), 1) // tok
    return velocity, jnp.where(lane_frame + first == -1, shared, moved)


def own_rows(block, tok, part_rows, index, scratch):
    scratch[...] = block.T
    return scratch[pl.ds(pl.multiple_of(index * part_rows, 8), part_rows), :]


def step_kernel(step, cfg, *refs):
    tok, frames, channels, base, depth, level_count, heads, part_rows = cfg
    query_block = max(1, LANES // tok)
    n_query = query_block + 2 * HALO * (STEPS - 1 - step)
    n_key = n_query + 2 * HALO
    key_lanes, query_lanes = n_key * tok, n_query * tok
    width = heads * HD
    position, tok_index = lax.axis_index("queue"), lax.axis_index("tok")
    first_key = position - HALO - (HALO + 1) * (STEPS - 1 - step)
    refs = list(refs)
    slot_ref, reach_ref = refs[0], refs[1]
    if step == 0:
        count = tok // part_rows
        lat_refs, noise_refs = refs[2 : 2 + count], refs[2 + count : 1 + 2 * count]
        refs = refs[1 + 2 * count :]
    else:
        g_ref, hprev_ref, xprev_ref = refs[2:5]
        refs = refs[5:]
    fresh_ref = None
    if step < STEPS - 1:
        fresh_ref = refs.pop(0)
    gain_ref, mq_ref, mk_ref, mv_ref, wo_ref, gram_ref, gv_ref = refs[:7]
    refs = refs[7:]
    part_ref, hpart_ref, xq_ref = refs[:3]
    refs = refs[3:]
    own_ref = None
    if step > 0:
        own_ref = refs.pop(0)
    kbuf, vbuf, qbuf, att, tbuf, xbuf = refs

    if step == 0:
        noise = [fresh_ref[0]] + [ref[0] for ref in noise_refs]
        for w in range(n_key):
            source = lax.rem(first_key - 1 + w + 2 * frames, frames)
            apart, bits = position ^ source, frames.bit_length() - 2
            second = ((apart >> bits) & 1) == 1
            entry = sum(((apart >> bit) & 1) << (bits - 1 - bit) for bit in range(bits))
            for t in range(count):
                at = lax.rem(tok_index + t, count) * part_rows + w * tok
                beside = lat_refs[t][entry]
                rows = jnp.where(second, beside[:, channels:], beside[:, :channels])
                rows = jnp.where(source == frames - 1, noise[t], rows)
                xbuf[pl.ds(pl.multiple_of(at, 8), part_rows), :] = rows
        state = xbuf[...].T
    else:
        velocity, state = advance(level_count, tok, first_key - 1, g_ref, hprev_ref, xprev_ref)
        mine = (HALO + 1) * (STEPS - step)
        own_ref[...] = own_rows(velocity[:, mine * tok : (mine + 1) * tok], tok, part_rows, tok_index, tbuf)

    key_frame = lax.broadcasted_iota(jnp.int32, (1, key_lanes), 1) // tok
    level_row = jnp.full((1, key_lanes), -1, jnp.int32)
    for w in range(n_key):
        frame = first_key + w
        known = slot_ref[jnp.clip(frame - step - 1, 0, frames - 1)] + step
        level_row = jnp.where(key_frame == w, jnp.where(frame >= step + 1, known, frame), level_row)
    row = lax.broadcasted_iota(jnp.int32, (base - channels, key_lanes), 0)
    aug_t = jnp.concatenate([state, jnp.where(row == level_row, 1.0, 0.0)], axis=0)
    aug_t = aug_t.astype(BF16).astype(F32)
    aug_tb = aug_t.astype(BF16)
    both_t = jnp.concatenate([aug_tb, aug_tb], axis=0)
    mean_t = jnp.sum(dot(gram_ref[...], both_t) * aug_t, axis=0, keepdims=True) * (1.0 / depth)
    mean_t = jnp.maximum(mean_t, 0.0) + EPS
    queries = slice(HALO * tok, HALO * tok + query_lanes)
    mean_q = mean_t[:, queries]
    aug_qb = aug_t[:, queries].astype(BF16)
    both_q = jnp.concatenate([aug_qb, aug_qb], axis=0)
    last_row = lax.broadcasted_iota(jnp.int32, (base, key_lanes), 0) == base - 1
    aug = jnp.where(last_row, EPS * mean_t, aug_t).T
    eps_c = aug[:, base - 1 : base]
    aug_b = aug.astype(BF16)
    both = jnp.concatenate([aug_b, aug_b], axis=1)

    hpart_ref[...] = dot(gv_ref[...], both_q)
    xq_ref[...] = state[:, queries]

    gain = gain_ref[0:1, :] * gain_ref[1:2, :] * (HD ** -0.5 * math.log2(math.e))
    span = 256 if width % 256 == 0 else 128
    head_of = lambda axis: lax.broadcasted_iota(jnp.int32, (span, span), axis) // HD
    average = jnp.where(head_of(0) == head_of(1), 1.0 / HD, 0.0).astype(BF16)
    for at in range(0, width, span):
        raw = dot(both, mk_ref[:, at : at + span])
        spread = dot((raw * raw).astype(BF16), average)
        kbuf[:, at : at + span] = (raw * lax.rsqrt(spread + eps_c) * gain[:, at : at + span]).astype(BF16)
    vbuf[...] = (dot(mv_ref[...], both_t) * lax.rsqrt(mean_t)).astype(BF16)
    raw = dot(mq_ref[...], both_q).reshape(heads, HD, query_lanes)
    spread = jnp.sum(raw * raw, axis=1, keepdims=True) * (1.0 / HD)
    qbuf[...] = (raw * lax.rsqrt(spread + EPS * mean_q)[:, :, :]).reshape(width, query_lanes).astype(BF16)

    bound = HD * jnp.max(gain, axis=1, keepdims=True)
    upper = lax.broadcasted_iota(jnp.int32, (2 * HD, LANES), 0) < HD
    lane = lax.broadcasted_iota(jnp.int32, (1, 2 * LANES), 1)
    within = lax.rem(lane, LANES) // tok

    full = 2 * HALO + query_block
    if query_block == 1:
        cuts = [(HALO - r, 2 * r + 1) for r in range(HALO + 1)]
    else:
        cuts = [(2, full - 4), (2, full - 2), (0, full - 2), (0, full)]

    def reaches(lead):
        widths = []
        for j in range(query_block):
            frame = first_key + HALO + lead + j
            needed = (frame >= 0) & (frame < frames) & (lead + j <= n_query - query_block)
            widths.append(jnp.where(needed, reach_ref[jnp.clip(frame, 0, frames - 1)], -1))
        return widths

    def biases(lead, shift):
        rows, widths = [], reaches(lead)
        for k in range(full):
            target = first_key + lead + k
            inside = (target >= 0) & (target < frames)
            row = jnp.zeros((1, 2 * LANES), F32)
            for j in range(query_block):
                counted = (inside & (abs(k - HALO - j) <= widths[j])) | (widths[j] < 0)
                row = jnp.where(within == j, jnp.where(counted, 0.0, -1e30), row)
            rows.append(row - shift)
        return rows

    def span_of(first, count):
        return pl.ds(pl.multiple_of(first * tok, LANES), count * tok)

    def scores(keys, lanes, cols, rows):
        query = qbuf[cols, lanes]
        zero = jnp.zeros_like(query)
        query = jnp.concatenate([jnp.where(upper, query, zero), jnp.where(upper, zero, query)], axis=1)
        score = dot(kbuf[keys, cols], query)
        return jnp.concatenate([score[k * tok : (k + 1) * tok] + rows[k] for k in range(len(rows))], axis=0)

    def mix(keys, lanes, cols, weight):
        ones = jnp.ones((16, weight.shape[0]), BF16)
        mixed = dot(jnp.concatenate([vbuf[cols, keys], ones], axis=0), weight.astype(BF16))
        total = mixed[2 * HD : 2 * HD + 1, :]
        scale = 1.0 / total
        top = mixed[:HD, :LANES] * scale[:, :LANES]
        bottom = mixed[HD : 2 * HD, LANES:] * scale[:, LANES:]
        att[cols, lanes] = jnp.concatenate([top, bottom], axis=0).astype(BF16)
        return total

    def block(b, least):
        lead = (b * LANES) // tok
        lanes = pl.ds(pl.multiple_of(b * LANES, LANES), LANES)
        rows, widths = biases(lead, bound), reaches(lead)

        def run(first, count, least):
            keys = span_of(lead + first, count)
            held = None
            for pair in range(heads // 2):
                cols = slice(pair * 2 * HD, (pair + 1) * 2 * HD)
                weight = jnp.exp2(scores(keys, lanes, cols, rows[first : first + count])).astype(BF16)
                if held is not None:
                    least = jnp.minimum(least, mix(keys, lanes, *held))
                held = (cols, weight)
            return jnp.minimum(least, mix(keys, lanes, *held))

        if query_block == 1:
            chosen = jnp.maximum(widths[0], 0)
        else:
            left, right = widths[0], widths[0] - query_block + 1
            for j in range(1, query_block):
                left = jnp.maximum(left, widths[j] - j)
                right = jnp.maximum(right, widths[j] + j - query_block + 1)
            chosen = jnp.where(left > 1, 2, 0) + jnp.where(right > 1, 1, 0)
        return lax.switch(chosen, [functools.partial(run, *cut) for cut in cuts], least)

    def exact_block(at, carry):
        lead = (at // (heads // 2) * LANES) // tok
        keys = span_of(lead, full)
        lanes = pl.ds(pl.multiple_of(at // (heads // 2) * LANES, LANES), LANES)
        cols = pl.ds(pl.multiple_of(lax.rem(at, heads // 2) * 2 * HD, 2 * HD), 2 * HD)
        score = scores(keys, lanes, cols, biases(lead, 0.0))
        mix(keys, lanes, cols, jnp.exp2(score - jnp.max(score, axis=0, keepdims=True)))
        return carry

    blocks = query_lanes // LANES
    least = jnp.ones((1, 2 * LANES), F32)
    least = block(0, least) if blocks == 1 else lax.fori_loop(0, blocks, block, least)

    @pl.when(jnp.min(least) < 1e-25)
    def _():
        lax.fori_loop(0, blocks * (heads // 2), exact_block, 0)

    mixed = dot(wo_ref[...], att[...])
    partial = mixed[:channels] + mixed[channels:]
    if step < STEPS - 1:
        tbuf[...] = jnp.zeros_like(tbuf)
        tbuf[pl.ds(pl.multiple_of(tok_index * part_rows, 8), part_rows), :] = fresh_ref[step + 1]
        fresh_t = tbuf[...].T
        fresh_t = jnp.concatenate([fresh_t] * n_query, axis=1)
        slot = lax.broadcasted_iota(jnp.int32, (1, query_lanes), 1) // tok + first_key + HALO
        partial = jnp.where(slot == -1, fresh_t, partial)
    part_ref[...] = partial[:, : part_ref.shape[1]]


def last_kernel(cfg, *refs):
    tok, frames, channels, base, depth, level_count, heads, part_rows = cfg
    g_ref, hpart_ref, xq_ref = refs[:3]
    own = refs[3 : 3 + STEPS - 1]
    velocity_ref, queue_ref, tbuf = refs[3 + STEPS - 1 :]
    tok_index = lax.axis_index("tok")
    velocity, moved = advance(level_count, tok, None, g_ref, hpart_ref, xq_ref)
    for s in range(STEPS - 1):
        velocity_ref[s, 0] = own[s][...]
    velocity_ref[STEPS - 1, 0] = own_rows(velocity[:, :tok], tok, part_rows, tok_index, tbuf)
    queue_ref[0] = own_rows(moved[:, :tok], tok, part_rows, tok_index, tbuf)


def body(
    latent,
    fresh_noise,
    frame_slot,
    frame_reach,
    level_embed,
    embed_weight,
    qkv_weight,
    qk_gain,
    out_weight,
    vel_weight,
):
    frames, parts = lax.axis_size("queue"), lax.axis_size("tok")
    position = lax.axis_index("queue")
    part_rows, channels = latent.shape[1], latent.shape[2]
    tok = part_rows * parts
    level_count = level_embed.shape[0]
    depth = qkv_weight.shape[2]
    width = qkv_weight.shape[1]
    spare = round_up(width, 2 * LANES) - width
    if spare:
        qkv_weight = jnp.pad(qkv_weight, ((0, 0), (0, spare), (0, 0)))
        qk_gain = jnp.pad(qk_gain, ((0, 0), (0, spare)))
        out_weight = jnp.pad(out_weight, ((0, spare), (0, 0)))
        width += spare
    heads = width // HD
    base = round_up(channels + level_count + 1, LANES)
    cfg = (tok, frames, channels, base, depth, level_count, heads, part_rows)
    vmem, smem, hbm, anywhere = (
        pl.BlockSpec(memory_space=pltpu.VMEM),
        pl.BlockSpec(memory_space=pltpu.SMEM),
        pl.BlockSpec(memory_space=pltpu.HBM),
        pl.BlockSpec(memory_space=pl.ANY),
    )
    shape = jax.ShapeDtypeStruct

    def swapped(value, axis, distance):
        count = lax.axis_size(axis)
        return lax.ppermute(value, axis, [(source, source ^ distance) for source in range(count)])

    def from_ahead(value, distance):
        return lax.ppermute(value, "tok", [(source, (source - distance) % parts) for source in range(parts)])

    share = depth // parts
    table = (embed_weight, level_embed, vel_weight.T)
    around = range(1, parts)
    tables = [from_ahead(piece, d) for d in around for piece in table]
    noise = [from_ahead(fresh_noise, d) for d in around]
    in_hbm = lambda array: pltpu.with_memory_space_constraint(array, pltpu.HBM)
    table = tuple(in_hbm(piece) for piece in table)
    qkv_weight, out_weight = in_hbm(qkv_weight), in_hbm(out_weight)
    rows = 384 if width % 384 == 0 else 256
    chunks = 2 * width // rows

    def weights(kernel, shares, outs, held, after, *operands):
        count = len(shares)
        scratch = [pltpu.VMEM(piece.shape, BF16) for piece in held]
        if held:
            scratch.append(pltpu.SemaphoreType.DMA((len(held),)))
        scratch += [pltpu.VMEM((count, chunks, rows, share), BF16), pltpu.SemaphoreType.DMA((chunks, count))]
        return pl.pallas_call(
            functools.partial(kernel, shares),
            out_shape=tuple(outs),
            in_specs=[hbm] * len(held)
            + [vmem] * (len(operands) - len(held))
            + [hbm] * 2
            + [anywhere] * len(after),
            out_specs=(vmem,) * len(outs),
            scratch_shapes=scratch,
            compiler_params=pltpu.CompilerParams(vmem_limit_bytes=24 * 2**20),
            cost_estimate=pl.CostEstimate(
                flops=4 * base * width * share * count,
                bytes_accessed=4 * width * share * count,
                transcendentals=0,
            ),
            name="weights",
        )(*operands, qkv_weight, out_weight, *after)

    keys_part = lambda shares, *refs: keys_kernel(rows, base, shares, *refs)
    values_part = lambda shares, *refs: values_kernel(rows, shares, *refs)
    turned_tables = lambda count: [shape((count * share, base), BF16), shape((count * share, channels), BF16)]
    others = tuple(around)

    def own_keys(*after):
        outs = [shape((2 * width, base), F32), shape((base, base), F32), shape((channels, base), F32)]
        return weights(keys_part, (0,), outs + turned_tables(1), table, after, *table)

    def own_values(*after):
        outs = [shape((width, base), F32), shape((width, channels), F32)]
        return weights(values_part, (0,), outs, (), after, *done[0][3:])

    def other_keys(*after):
        outs = [
            shape((width, 2 * base), BF16),
            shape((2 * base, width), BF16),
            shape((base, 2 * base), BF16),
            shape((channels, 2 * base), BF16),
        ]
        return weights(keys_part, others, outs + turned_tables(parts - 1), (), after, *tables, *done[0][:3])

    def other_values(*after):
        outs = [shape((width, 2 * base), BF16), shape((2 * channels, width), BF16)]
        return weights(values_part, others, outs, (), after, *done[2][4:], *done[1])

    state = latent
    work = [own_keys, own_values, other_keys, other_values]
    done, after = [], ()
    distance = frames // 2
    while distance:
        moved = swapped(state, "queue", distance)
        if len(done) < len(work):
            moved, noise, result = lax.optimization_barrier((moved, noise, work[len(done)](*after)))
            done.append(result)
            after = (moved,)
        axis = 2 if distance == frames // 2 else 0
        state = lax.optimization_barrier(jnp.concatenate([state, moved], axis=axis))
        distance //= 2
    while len(done) < len(work):
        done.append(work[len(done)]())
    latents = [state] + [from_ahead(state, d) for d in range(1, parts)] + noise
    mq, mk, gram, gv = done[2][:4]
    mv, wo = done[3]

    query_block = max(1, LANES // tok)
    owned = []
    for step in range(STEPS):
        n_query = query_block + 2 * HALO * (STEPS - 1 - step)
        query_lanes, key_lanes = n_query * tok, (n_query + 2 * HALO) * tok
        args = [frame_slot, frame_reach]
        specs = [smem, smem]
        if step == 0:
            args += latents
            specs += [vmem] * len(latents)
        else:
            args += [gathered, hpart, xq]
            specs += [vmem] * 3
        if step < STEPS - 1:
            args += [fresh_noise]
            specs += [vmem]
        args += [qk_gain, mq, mk, mv, wo, gram, gv]
        specs += [vmem] * 7
        outs = [shape((channels, query_lanes), F32)] * 3
        if step > 0:
            outs += [shape((part_rows, channels), F32)]
        window = (2 * HALO + query_block) * tok
        result = pl.pallas_call(
            functools.partial(step_kernel, step, cfg),
            out_shape=tuple(outs),
            in_specs=specs,
            out_specs=(vmem,) * len(outs),
            scratch_shapes=[
                pltpu.VMEM((key_lanes, width), BF16),
                pltpu.VMEM((width, key_lanes), BF16),
                pltpu.VMEM((width, query_lanes), BF16),
                pltpu.VMEM((width, query_lanes), BF16),
                pltpu.VMEM((tok, channels), F32),
                pltpu.VMEM((key_lanes if step == 0 else tok, channels), F32),
            ],
            compiler_params=pltpu.CompilerParams(vmem_limit_bytes=48 * 2**20),
            cost_estimate=pl.CostEstimate(
                flops=4 * query_lanes * window * width + 12 * key_lanes * base * width,
                bytes_accessed=8 * width * base,
                transcendentals=query_lanes * window * heads,
            ),
            name="step%d" % step,
        )(*args)
        part, hpart, xq = result[:3]
        owned += list(result[3:])
        gathered = lax.all_gather(part, "tok", axis=0, tiled=False)

    return tuple(
        pl.pallas_call(
            functools.partial(last_kernel, cfg),
            out_shape=(
                shape((STEPS, 1, part_rows, channels), F32),
                shape((1, part_rows, channels), F32),
            ),
            in_specs=[vmem] * (3 + len(owned)),
            out_specs=(vmem, vmem),
            scratch_shapes=[pltpu.VMEM((tok, channels), F32)],
            compiler_params=pltpu.CompilerParams(vmem_limit_bytes=8 * 2**20),
            name="last",
        )(gathered, hpart, xq, *owned)
    )


def solution(mesh):
    return jax.shard_map(
        body,
        mesh=mesh,
        in_specs=(
            P("queue", "tok", None),
            P(None, "tok", None),
            P(),
            P(),
            P(None, "tok"),
            P(None, "tok"),
            P(None, "tok", None),
            P(None, "tok"),
            P("tok", None),
            P("tok", None),
        ),
        out_specs=(P(None, "queue", "tok", None), P("queue", "tok", None)),
        check_vma=False,
    )
```

```python
import functools
import math

import jax
import jax.numpy as jnp
from jax import lax
from jax.experimental import pallas as pl
from jax.experimental.pallas import tpu as pltpu
from jax.sharding import PartitionSpec as P

HD = 64
STEPS = 3
HALO = 3
LANES = 128
EPS = 1e-06
F32, BF16 = jnp.float32, jnp.bfloat16


def round_up(value, unit):
    return -(-value // unit) * unit


def dot(a, b):
    return jnp.dot(a, b, preferred_element_type=F32)


def dot_nt(a, b):
    return lax.dot_general(a, b, (((1,), (1,)), ((), ())), preferred_element_type=F32)


def halves(value, axis):
    high = value.astype(BF16)
    low = (value - high.astype(F32)).astype(BF16)
    return jnp.concatenate([high, low], axis=axis)


def chunk_copies(rows, chunks, parts, qkv_hbm, out_hbm, buf, sems):
    per = out_hbm.shape[0] // rows
    depth = buf.shape[-1]
    index, count = lax.axis_index("tok"), lax.axis_size("tok")
    copies = {}
    for place, chunk in enumerate(chunks):
        source = qkv_hbm.at[chunk // per] if chunk < 3 * per else out_hbm
        for at, part in enumerate(parts):
            columns = pl.ds(pl.multiple_of(lax.rem(index + part, count) * depth, LANES), depth)
            copies[place, at] = pltpu.make_async_copy(
                source.at[pl.ds((chunk % per) * rows, rows), columns],
                buf.at[at, place],
                sems.at[place, at],
            )
    return copies


def started(sources, targets, sems):
    copies = [pltpu.make_async_copy(a, b, sems.at[i]) for i, (a, b) in enumerate(zip(sources, targets))]
    for copy in copies:
        copy.start()
    return copies


def turned(value):
    return value.astype(F32).T.astype(BF16)


def keys_kernel(rows, base, shares, *refs):
    own, count = shares == (0,), len(shares)
    tables, refs = refs[: 2 * count], refs[2 * count :]
    if own:
        qkv_hbm, out_hbm = refs[:2]
        total_ref, gram_ref, right_ref, embed, level, small, buf, sems = refs[-8:]
        brought = started(tables, (embed, level), small)
    else:
        sum_ref, gram_sum, qkv_hbm, out_hbm = refs[:4]
        mq_ref, mk_ref, gram_ref, right_ref, buf, sems = refs[-6:]
    per = out_hbm.shape[0] // rows
    depth = buf.shape[-1]
    copies = chunk_copies(rows, range(2 * per), shares, qkv_hbm, out_hbm, buf, sems)
    for copy in copies.values():
        copy.start()
    if own:
        for copy in brought:
            copy.wait()
        tables = (embed, level)
    gram = jnp.zeros((base, base), F32) if own else gram_sum[...]
    for at in range(count):
        left = [tables[2 * at][...].astype(F32), tables[2 * at + 1][...].astype(F32)]
        left.append(jnp.zeros((base - left[0].shape[0] - left[1].shape[0], depth), F32))
        left = jnp.concatenate(left, axis=0)
        right_ref[at * depth : (at + 1) * depth, :] = left.T.astype(BF16)
        gram = gram + dot(left.astype(BF16), right_ref[at * depth : (at + 1) * depth, :])
    gram_ref[...] = gram if own else halves(gram, 1)
    for chunk in range(2 * per):
        spot = slice(chunk * rows, (chunk + 1) * rows)
        total = None if own else sum_ref[spot, :]
        for at in range(count):
            copies[chunk, at].wait()
            product = dot(buf[at, chunk], right_ref[at * depth : (at + 1) * depth, :])
            total = product if total is None else total + product
        where = slice((chunk % per) * rows, (chunk % per + 1) * rows)
        if own:
            total_ref[spot, :] = total
        elif chunk < per:
            mq_ref[where, :] = total.astype(BF16)
        else:
            mk_ref[:, where] = total.T.astype(BF16)


def values_kernel(rows, shares, *refs):
    own, count = shares == (0,), len(shares)
    tables, right_ref, refs = refs[:count], refs[count], refs[count + 1 :]
    if own:
        qkv_hbm, out_hbm = refs[:2]
        mv_ref, wo_ref, gv_ref, held, small, buf, sems = refs[-7:]
        brought = started(tables, (held,), small)
    else:
        mv_sum, wo_sum, gv_sum, qkv_hbm, out_hbm = refs[:5]
        mv_ref, wo_ref, gv_ref, buf, sems = refs[-5:]
    per = out_hbm.shape[0] // rows
    depth = buf.shape[-1]
    copies = chunk_copies(rows, range(2 * per, 4 * per), shares, qkv_hbm, out_hbm, buf, sems)
    for copy in copies.values():
        copy.start()
    if own:
        brought[0].wait()
        tables = (held,)
    vels = [table[...] for table in tables]
    gv = sum(dot(vel, right_ref[at * depth : (at + 1) * depth, :]) for at, vel in enumerate(vels))
    gv_ref[...] = gv if own else halves(gv_sum[...] + gv, 1)
    downs = [turned(vel) for vel in vels]
    for place in range(2 * per):
        where = slice((place % per) * rows, (place % per + 1) * rows)
        total = None if own else (mv_sum if place < per else wo_sum)[where, :]
        for at in range(count):
            copies[place, at].wait()
            right = right_ref[at * depth : (at + 1) * depth, :] if place < per else downs[at]
            product = dot(buf[at, place], right)
            total = product if total is None else total + product
        if own:
            (mv_ref if place < per else wo_ref)[where, :] = total
        elif place < per:
            mv_ref[where, :] = total.astype(BF16)
        else:
            wo_ref[:, where] = halves(total.T, 0)


def advance(level_count, tok, first, g_ref, hpart_ref, xq_ref):
    shared = g_ref[0]
    for t in range(1, g_ref.shape[0]):
        shared = shared + g_ref[t]
    velocity = shared + hpart_ref[...]
    moved = xq_ref[...] - velocity * (1.0 / level_count)
    if first is None:
        return velocity, moved
    lane_frame = lax.broadcasted_iota(jnp.int32, (1, shared.shape[1]), 1) // tok
    return velocity, jnp.where(lane_frame + first == -1, shared, moved)


def own_rows(block, tok, part_rows, index, scratch):
    scratch[...] = block.T
    return scratch[pl.ds(pl.multiple_of(index * part_rows, 8), part_rows), :]


def step_kernel(step, cfg, *refs):
    tok, frames, channels, base, depth, level_count, heads, part_rows = cfg
    query_block = max(1, LANES // tok)
    n_query = query_block + 2 * HALO * (STEPS - 1 - step)
    n_key = n_query + 2 * HALO
    key_lanes, query_lanes = n_key * tok, n_query * tok
    width = heads * HD
    position, tok_index = lax.axis_index("queue"), lax.axis_index("tok")
    first_key = position - HALO - (HALO + 1) * (STEPS - 1 - step)
    refs = list(refs)
    slot_ref, reach_ref = refs[0], refs[1]
    if step == 0:
        count = tok // part_rows
        lat_refs, noise_refs = refs[2 : 2 + count], refs[2 + count : 1 + 2 * count]
        refs = refs[1 + 2 * count :]
    else:
        g_ref, hprev_ref, xprev_ref = refs[2:5]
        refs = refs[5:]
    fresh_ref = None
    if step < STEPS - 1:
        fresh_ref = refs.pop(0)
    gain_ref, mq_ref, mk_ref, mv_ref, wo_ref, gram_ref, gv_ref = refs[:7]
    refs = refs[7:]
    part_ref, hpart_ref, xq_ref = refs[:3]
    refs = refs[3:]
    own_ref = None
    if step > 0:
        own_ref = refs.pop(0)
    kbuf, vbuf, qbuf, att, tbuf, xbuf = refs

    if step == 0:
        noise = [fresh_ref[0]] + [ref[0] for ref in noise_refs]
        for w in range(n_key):
            source = lax.rem(first_key - 1 + w + 2 * frames, frames)
            apart, bits = position ^ source, frames.bit_length() - 2
            second = ((apart >> bits) & 1) == 1
            entry = sum(((apart >> bit) & 1) << (bits - 1 - bit) for bit in range(bits))
            for t in range(count):
                at = lax.rem(tok_index + t, count) * part_rows + w * tok
                beside = lat_refs[t][entry]
                rows = jnp.where(second, beside[:, channels:], beside[:, :channels])
                rows = jnp.where(source == frames - 1, noise[t], rows)
                xbuf[pl.ds(pl.multiple_of(at, 8), part_rows), :] = rows
        state = xbuf[...].T
    else:
        velocity, state = advance(level_count, tok, first_key - 1, g_ref, hprev_ref, xprev_ref)
        mine = (HALO + 1) * (STEPS - step)
        own_ref[...] = own_rows(velocity[:, mine * tok : (mine + 1) * tok], tok, part_rows, tok_index, tbuf)

    key_frame = lax.broadcasted_iota(jnp.int32, (1, key_lanes), 1) // tok
    level_row = jnp.full((1, key_lanes), -1, jnp.int32)
    for w in range(n_key):
        frame = first_key + w
        known = slot_ref[jnp.clip(frame - step - 1, 0, frames - 1)] + step
        level_row = jnp.where(key_frame == w, jnp.where(frame >= step + 1, known, frame), level_row)
    row = lax.broadcasted_iota(jnp.int32, (base - channels, key_lanes), 0)
    aug_t = jnp.concatenate([state, jnp.where(row == level_row, 1.0, 0.0)], axis=0)
    aug_t = aug_t.astype(BF16).astype(F32)
    aug_tb = aug_t.astype(BF16)
    both_t = jnp.concatenate([aug_tb, aug_tb], axis=0)
    mean_t = jnp.sum(dot(gram_ref[...], both_t) * aug_t, axis=0, keepdims=True) * (1.0 / depth)
    mean_t = jnp.maximum(mean_t, 0.0) + EPS
    queries = slice(HALO * tok, HALO * tok + query_lanes)
    mean_q = mean_t[:, queries]
    aug_qb = aug_t[:, queries].astype(BF16)
    both_q = jnp.concatenate([aug_qb, aug_qb], axis=0)
    last_row = lax.broadcasted_iota(jnp.int32, (base, key_lanes), 0) == base - 1
    aug = jnp.where(last_row, EPS * mean_t, aug_t).T
    eps_c = aug[:, base - 1 : base]
    aug_b = aug.astype(BF16)

    hpart_ref[...] = dot(gv_ref[...], both_q)
    xq_ref[...] = state[:, queries]

    gain = gain_ref[0:1, :] * gain_ref[1:2, :] * (HD ** -0.5 * math.log2(math.e))
    span = 256 if width % 256 == 0 else 128
    head_of = lambda axis: lax.broadcasted_iota(jnp.int32, (span, span), axis) // HD
    average = jnp.where(head_of(0) == head_of(1), 1.0 / HD, 0.0).astype(BF16)
    for at in range(0, width, span):
        raw = dot(aug_b, mk_ref[:, at : at + span])
        spread = dot((raw * raw).astype(BF16), average)
        kbuf[:, at : at + span] = (raw * lax.rsqrt(spread + eps_c) * gain[:, at : at + span]).astype(BF16)
    vbuf[...] = (dot(mv_ref[...], aug_tb) * lax.rsqrt(mean_t)).astype(BF16)
    raw = dot(mq_ref[...], aug_qb).reshape(heads, HD, query_lanes)
    spread = jnp.sum(raw * raw, axis=1, keepdims=True) * (1.0 / HD)
    qbuf[...] = (raw * lax.rsqrt(spread + EPS * mean_q)[:, :, :]).reshape(width, query_lanes).astype(BF16)

    bound = HD * jnp.max(gain, axis=1, keepdims=True)
    upper = lax.broadcasted_iota(jnp.int32, (2 * HD, LANES), 0) < HD
    lane = lax.broadcasted_iota(jnp.int32, (1, 2 * LANES), 1)
    within = lax.rem(lane, LANES) // tok

    full = 2 * HALO + query_block
    if query_block == 1:
        cuts = [(HALO - r, 2 * r + 1) for r in range(HALO + 1)]
    else:
        cuts = [(2, full - 4), (2, full - 2), (0, full - 2), (0, full)]

    def reaches(lead):
        widths = []
        for j in range(query_block):
            frame = first_key + HALO + lead + j
            needed = (frame >= 0) & (frame < frames) & (lead + j <= n_query - query_block)
            widths.append(jnp.where(needed, reach_ref[jnp.clip(frame, 0, frames - 1)], -1))
        return widths

    def biases(lead, shift):
        rows, widths = [], reaches(lead)
        for k in range(full):
            target = first_key + lead + k
            inside = (target >= 0) & (target < frames)
            row = jnp.zeros((1, 2 * LANES), F32)
            for j in range(query_block):
                counted = (inside & (abs(k - HALO - j) <= widths[j])) | (widths[j] < 0)
                row = jnp.where(within == j, jnp.where(counted, 0.0, -1e30), row)
            rows.append(row - shift)
        return rows

    def span_of(first, count):
        return pl.ds(pl.multiple_of(first * tok, LANES), count * tok)

    def scores(keys, lanes, cols, rows):
        query = qbuf[cols, lanes]
        zero = jnp.zeros_like(query)
        query = jnp.concatenate([jnp.where(upper, query, zero), jnp.where(upper, zero, query)], axis=1)
        score = dot(kbuf[keys, cols], query)
        return jnp.concatenate([score[k * tok : (k + 1) * tok] + rows[k] for k in range(len(rows))], axis=0)

    def mix(keys, lanes, cols, weight):
        ones = jnp.ones((16, weight.shape[0]), BF16)
        mixed = dot(jnp.concatenate([vbuf[cols, keys], ones], axis=0), weight.astype(BF16))
        total = mixed[2 * HD : 2 * HD + 1, :]
        scale = 1.0 / total
        top = mixed[:HD, :LANES] * scale[:, :LANES]
        bottom = mixed[HD : 2 * HD, LANES:] * scale[:, LANES:]
        att[cols, lanes] = jnp.concatenate([top, bottom], axis=0).astype(BF16)
        return total

    def block(b, least):
        lead = (b * LANES) // tok
        lanes = pl.ds(pl.multiple_of(b * LANES, LANES), LANES)
        rows, widths = biases(lead, bound), reaches(lead)

        def run(first, count, least):
            keys = span_of(lead + first, count)
            held = None
            for pair in range(heads // 2):
                cols = slice(pair * 2 * HD, (pair + 1) * 2 * HD)
                weight = jnp.exp2(scores(keys, lanes, cols, rows[first : first + count])).astype(BF16)
                if held is not None:
                    least = jnp.minimum(least, mix(keys, lanes, *held))
                held = (cols, weight)
            return jnp.minimum(least, mix(keys, lanes, *held))

        if query_block == 1:
            chosen = jnp.maximum(widths[0], 0)
        else:
            left, right = widths[0], widths[0] - query_block + 1
            for j in range(1, query_block):
                left = jnp.maximum(left, widths[j] - j)
                right = jnp.maximum(right, widths[j] + j - query_block + 1)
            chosen = jnp.where(left > 1, 2, 0) + jnp.where(right > 1, 1, 0)
        return lax.switch(chosen, [functools.partial(run, *cut) for cut in cuts], least)

    def exact_block(at, carry):
        lead = (at // (heads // 2) * LANES) // tok
        keys = span_of(lead, full)
        lanes = pl.ds(pl.multiple_of(at // (heads // 2) * LANES, LANES), LANES)
        cols = pl.ds(pl.multiple_of(lax.rem(at, heads // 2) * 2 * HD, 2 * HD), 2 * HD)
        score = scores(keys, lanes, cols, biases(lead, 0.0))
        mix(keys, lanes, cols, jnp.exp2(score - jnp.max(score, axis=0, keepdims=True)))
        return carry

    blocks = query_lanes // LANES
    least = jnp.ones((1, 2 * LANES), F32)
    least = block(0, least) if blocks == 1 else lax.fori_loop(0, blocks, block, least)

    @pl.when(jnp.min(least) < 1e-25)
    def _():
        lax.fori_loop(0, blocks * (heads // 2), exact_block, 0)

    mixed = dot(wo_ref[...], att[...])
    partial = mixed[:channels] + mixed[channels:]
    if step < STEPS - 1:
        tbuf[...] = jnp.zeros_like(tbuf)
        tbuf[pl.ds(pl.multiple_of(tok_index * part_rows, 8), part_rows), :] = fresh_ref[step + 1]
        fresh_t = tbuf[...].T
        fresh_t = jnp.concatenate([fresh_t] * n_query, axis=1)
        slot = lax.broadcasted_iota(jnp.int32, (1, query_lanes), 1) // tok + first_key + HALO
        partial = jnp.where(slot == -1, fresh_t, partial)
    part_ref[...] = partial[:, : part_ref.shape[1]]


def last_kernel(cfg, *refs):
    tok, frames, channels, base, depth, level_count, heads, part_rows = cfg
    g_ref, hpart_ref, xq_ref = refs[:3]
    own = refs[3 : 3 + STEPS - 1]
    velocity_ref, queue_ref, tbuf = refs[3 + STEPS - 1 :]
    tok_index = lax.axis_index("tok")
    velocity, moved = advance(level_count, tok, None, g_ref, hpart_ref, xq_ref)
    for s in range(STEPS - 1):
        velocity_ref[s, 0] = own[s][...]
    velocity_ref[STEPS - 1, 0] = own_rows(velocity[:, :tok], tok, part_rows, tok_index, tbuf)
    queue_ref[0] = own_rows(moved[:, :tok], tok, part_rows, tok_index, tbuf)


def body(
    latent,
    fresh_noise,
    frame_slot,
    frame_reach,
    level_embed,
    embed_weight,
    qkv_weight,
    qk_gain,
    out_weight,
    vel_weight,
):
    frames, parts = lax.axis_size("queue"), lax.axis_size("tok")
    position = lax.axis_index("queue")
    part_rows, channels = latent.shape[1], latent.shape[2]
    tok = part_rows * parts
    level_count = level_embed.shape[0]
    depth = qkv_weight.shape[2]
    width = qkv_weight.shape[1]
    spare = round_up(width, 2 * LANES) - width
    if spare:
        qkv_weight = jnp.pad(qkv_weight, ((0, 0), (0, spare), (0, 0)))
        qk_gain = jnp.pad(qk_gain, ((0, 0), (0, spare)))
        out_weight = jnp.pad(out_weight, ((0, spare), (0, 0)))
        width += spare
    heads = width // HD
    base = round_up(channels + level_count + 1, LANES)
    cfg = (tok, frames, channels, base, depth, level_count, heads, part_rows)
    vmem, smem, hbm, anywhere = (
        pl.BlockSpec(memory_space=pltpu.VMEM),
        pl.BlockSpec(memory_space=pltpu.SMEM),
        pl.BlockSpec(memory_space=pltpu.HBM),
        pl.BlockSpec(memory_space=pl.ANY),
    )
    shape = jax.ShapeDtypeStruct

    def swapped(value, axis, distance):
        count = lax.axis_size(axis)
        return lax.ppermute(value, axis, [(source, source ^ distance) for source in range(count)])

    def from_ahead(value, distance):
        return lax.ppermute(value, "tok", [(source, (source - distance) % parts) for source in range(parts)])

    share = depth // parts
    table = (embed_weight, level_embed, vel_weight.T)
    around = range(1, parts)
    tables = [from_ahead(piece, d) for d in around for piece in table[:2]]
    vel_tables = [from_ahead(table[2], d) for d in around]
    noise = [from_ahead(fresh_noise, d) for d in around]
    in_hbm = lambda array: pltpu.with_memory_space_constraint(array, pltpu.HBM)
    table = tuple(in_hbm(piece) for piece in table)
    qkv_weight, out_weight = in_hbm(qkv_weight), in_hbm(out_weight)
    rows = 384 if width % 384 == 0 else 256
    chunks = 2 * width // rows

    def weights(kernel, shares, outs, held, after, *operands):
        count = len(shares)
        scratch = [pltpu.VMEM(piece.shape, BF16) for piece in held]
        if held:
            scratch.append(pltpu.SemaphoreType.DMA((len(held),)))
        scratch += [pltpu.VMEM((count, chunks, rows, share), BF16), pltpu.SemaphoreType.DMA((chunks, count))]
        return pl.pallas_call(
            functools.partial(kernel, shares),
            out_shape=tuple(outs),
            in_specs=[hbm] * len(held)
            + [vmem] * (len(operands) - len(held))
            + [hbm] * 2
            + [anywhere] * len(after),
            out_specs=(vmem,) * len(outs),
            scratch_shapes=scratch,
            compiler_params=pltpu.CompilerParams(vmem_limit_bytes=24 * 2**20),
            cost_estimate=pl.CostEstimate(
                flops=4 * base * width * share * count,
                bytes_accessed=4 * width * share * count,
                transcendentals=0,
            ),
            name="weights",
        )(*operands, qkv_weight, out_weight, *after)

    keys_part = lambda shares, *refs: keys_kernel(rows, base, shares, *refs)
    values_part = lambda shares, *refs: values_kernel(rows, shares, *refs)
    right = lambda count: shape((count * share, base), BF16)
    others = tuple(around)

    def own_keys(*after):
        outs = [shape((2 * width, base), F32), shape((base, base), F32), right(1)]
        return weights(keys_part, (0,), outs, table[:2], after, *table[:2])

    def own_values(*after):
        outs = [shape((width, base), F32), shape((width, channels), F32), shape((channels, base), F32)]
        return weights(values_part, (0,), outs, table[2:], after, table[2], done[0][2])

    def other_keys(*after):
        outs = [
            shape((width, base), BF16),
            shape((base, width), BF16),
            shape((base, 2 * base), BF16),
            right(parts - 1),
        ]
        return weights(keys_part, others, outs, (), after, *tables, *done[0][:2])

    def other_values(*after):
        outs = [
            shape((width, base), BF16),
            shape((2 * channels, width), BF16),
            shape((channels, 2 * base), BF16),
        ]
        return weights(values_part, others, outs, (), after, *vel_tables, done[2][3], *done[1])

    state = latent
    work = [own_keys, own_values, other_keys, other_values]
    done, after = [], ()
    distance = frames // 2
    while distance:
        moved = swapped(state, "queue", distance)
        if len(done) < len(work):
            moved, noise, result = lax.optimization_barrier((moved, noise, work[len(done)](*after)))
            done.append(result)
            after = (moved,)
        axis = 2 if distance == frames // 2 else 0
        state = lax.optimization_barrier(jnp.concatenate([state, moved], axis=axis))
        distance //= 2
    while len(done) < len(work):
        done.append(work[len(done)]())
    latents = [state] + [from_ahead(state, d) for d in range(1, parts)] + noise
    mq, mk, gram = done[2][:3]
    mv, wo, gv = done[3]

    query_block = max(1, LANES // tok)
    owned = []
    for step in range(STEPS):
        n_query = query_block + 2 * HALO * (STEPS - 1 - step)
        query_lanes, key_lanes = n_query * tok, (n_query + 2 * HALO) * tok
        args = [frame_slot, frame_reach]
        specs = [smem, smem]
        if step == 0:
            args += latents
            specs += [vmem] * len(latents)
        else:
            args += [gathered, hpart, xq]
            specs += [vmem] * 3
        if step < STEPS - 1:
            args += [fresh_noise]
            specs += [vmem]
        args += [qk_gain, mq, mk, mv, wo, gram, gv]
        specs += [vmem] * 7
        outs = [shape((channels, query_lanes), F32)] * 3
        if step > 0:
            outs += [shape((part_rows, channels), F32)]
        window = (2 * HALO + query_block) * tok
        result = pl.pallas_call(
            functools.partial(step_kernel, step, cfg),
            out_shape=tuple(outs),
            in_specs=specs,
            out_specs=(vmem,) * len(outs),
            scratch_shapes=[
                pltpu.VMEM((key_lanes, width), BF16),
                pltpu.VMEM((width, key_lanes), BF16),
                pltpu.VMEM((width, query_lanes), BF16),
                pltpu.VMEM((width, query_lanes), BF16),
                pltpu.VMEM((tok, channels), F32),
                pltpu.VMEM((key_lanes if step == 0 else tok, channels), F32),
            ],
            compiler_params=pltpu.CompilerParams(vmem_limit_bytes=48 * 2**20),
            cost_estimate=pl.CostEstimate(
                flops=4 * query_lanes * window * width + 12 * key_lanes * base * width,
                bytes_accessed=8 * width * base,
                transcendentals=query_lanes * window * heads,
            ),
            name="step%d" % step,
        )(*args)
        part, hpart, xq = result[:3]
        owned += list(result[3:])
        gathered = lax.all_gather(part, "tok", axis=0, tiled=False)

    return tuple(
        pl.pallas_call(
            functools.partial(last_kernel, cfg),
            out_shape=(
                shape((STEPS, 1, part_rows, channels), F32),
                shape((1, part_rows, channels), F32),
            ),
            in_specs=[vmem] * (3 + len(owned)),
            out_specs=(vmem, vmem),
            scratch_shapes=[pltpu.VMEM((tok, channels), F32)],
            compiler_params=pltpu.CompilerParams(vmem_limit_bytes=8 * 2**20),
            name="last",
        )(gathered, hpart, xq, *owned)
    )


def solution(mesh):
    return jax.shard_map(
        body,
        mesh=mesh,
        in_specs=(
            P("queue", "tok", None),
            P(None, "tok", None),
            P(),
            P(),
            P(None, "tok"),
            P(None, "tok"),
            P(None, "tok", None),
            P(None, "tok"),
            P("tok", None),
            P("tok", None),
        ),
        out_specs=(P(None, "queue", "tok", None), P("queue", "tok", None)),
        check_vma=False,
    )
```

```python
import functools
import math

import jax
import jax.numpy as jnp
from jax import lax
from jax.experimental import pallas as pl
from jax.experimental.pallas import tpu as pltpu
from jax.sharding import PartitionSpec as P

HD = 64
STEPS = 3
HALO = 3
LANES = 128
EPS = 1e-06
F32, BF16 = jnp.float32, jnp.bfloat16


def round_up(value, unit):
    return -(-value // unit) * unit


def dot(a, b):
    return jnp.dot(a, b, preferred_element_type=F32)


def dot_nt(a, b):
    return lax.dot_general(a, b, (((1,), (1,)), ((), ())), preferred_element_type=F32)


def halves(value, axis):
    high = value.astype(BF16)
    low = (value - high.astype(F32)).astype(BF16)
    return jnp.concatenate([high, low], axis=axis)


def chunk_copies(rows, chunks, parts, qkv_hbm, out_hbm, buf, sems):
    per = out_hbm.shape[0] // rows
    depth = buf.shape[-1]
    index, count = lax.axis_index("tok"), lax.axis_size("tok")
    copies = {}
    for place, chunk in enumerate(chunks):
        source = qkv_hbm.at[chunk // per] if chunk < 3 * per else out_hbm
        for at, part in enumerate(parts):
            columns = pl.ds(pl.multiple_of(lax.rem(index + part, count) * depth, LANES), depth)
            copies[place, at] = pltpu.make_async_copy(
                source.at[pl.ds((chunk % per) * rows, rows), columns],
                buf.at[at, place],
                sems.at[place, at],
            )
    return copies


def started(sources, targets, sems):
    copies = [pltpu.make_async_copy(a, b, sems.at[i]) for i, (a, b) in enumerate(zip(sources, targets))]
    for copy in copies:
        copy.start()
    return copies


def turned(value):
    return value.astype(F32).T.astype(BF16)


def keys_kernel(rows, base, shares, *refs):
    own, count = shares == (0,), len(shares)
    tables, refs = refs[: 3 * count], refs[3 * count :]
    if own:
        qkv_hbm, out_hbm = refs[:2]
        total_ref, gram_ref, gv_ref, right_ref, down_ref, *held, small, buf, sems = refs[-11:]
        brought = started(tables, held, small)
    else:
        sum_ref, gram_sum, gv_sum, qkv_hbm, out_hbm = refs[:5]
        mq_ref, mk_ref, gram_ref, gv_ref, right_ref, down_ref, buf, sems = refs[-8:]
    per = out_hbm.shape[0] // rows
    depth = buf.shape[-1]
    copies = chunk_copies(rows, range(2 * per), shares, qkv_hbm, out_hbm, buf, sems)
    for copy in copies.values():
        copy.start()
    if own:
        for copy in brought:
            copy.wait()
        tables = held
    gram, gv = (0.0, 0.0) if own else (gram_sum[...], gv_sum[...])
    for at in range(count):
        spot = slice(at * depth, (at + 1) * depth)
        left = [tables[3 * at][...].astype(F32), tables[3 * at + 1][...].astype(F32)]
        left.append(jnp.zeros((base - left[0].shape[0] - left[1].shape[0], depth), F32))
        left = jnp.concatenate(left, axis=0)
        vel = tables[3 * at + 2][...]
        right_ref[spot, :] = left.T.astype(BF16)
        down_ref[spot, :] = turned(vel)
        gram = gram + dot(left.astype(BF16), right_ref[spot, :])
        gv = gv + dot(vel, right_ref[spot, :])
    gram_ref[...] = gram if own else halves(gram, 1)
    gv_ref[...] = gv if own else halves(gv, 1)
    for chunk in range(2 * per):
        spot = slice(chunk * rows, (chunk + 1) * rows)
        total = None if own else sum_ref[spot, :]
        for at in range(count):
            copies[chunk, at].wait()
            product = dot(buf[at, chunk], right_ref[at * depth : (at + 1) * depth, :])
            total = product if total is None else total + product
        where = slice((chunk % per) * rows, (chunk % per + 1) * rows)
        if own:
            total_ref[spot, :] = total
        elif chunk < per:
            mq_ref[where, :] = total.astype(BF16)
        else:
            mk_ref[:, where] = total.T.astype(BF16)


def values_kernel(rows, shares, right_ref, down_ref, *refs):
    own, count = shares == (0,), len(shares)
    sums, refs = ((), refs) if own else (refs[:2], refs[2:])
    qkv_hbm, out_hbm = refs[:2]
    mv_ref, wo_ref, buf, sems = refs[-4:]
    per = out_hbm.shape[0] // rows
    depth = buf.shape[-1]
    copies = chunk_copies(rows, range(2 * per, 4 * per), shares, qkv_hbm, out_hbm, buf, sems)
    for copy in copies.values():
        copy.start()
    for place in range(2 * per):
        where = slice((place % per) * rows, (place % per + 1) * rows)
        total = None if own else sums[place // per][where, :]
        factor = right_ref if place < per else down_ref
        for at in range(count):
            copies[place, at].wait()
            product = dot(buf[at, place], factor[at * depth : (at + 1) * depth, :])
            total = product if total is None else total + product
        if own:
            (mv_ref if place < per else wo_ref)[where, :] = total
        elif place < per:
            mv_ref[where, :] = total.astype(BF16)
        else:
            wo_ref[:, where] = halves(total.T, 0)


def advance(level_count, tok, first, g_ref, hpart_ref, xq_ref):
    shared = g_ref[0]
    for t in range(1, g_ref.shape[0]):
        shared = shared + g_ref[t]
    velocity = shared + hpart_ref[...]
    moved = xq_ref[...] - velocity * (1.0 / level_count)
    if first is None:
        return velocity, moved
    lane_frame = lax.broadcasted_iota(jnp.int32, (1, shared.shape[1]), 1) // tok
    return velocity, jnp.where(lane_frame + first == -1, shared, moved)


def own_rows(block, tok, part_rows, index, scratch):
    scratch[...] = block.T
    return scratch[pl.ds(pl.multiple_of(index * part_rows, 8), part_rows), :]


def step_kernel(step, cfg, *refs):
    tok, frames, channels, base, depth, level_count, heads, part_rows = cfg
    query_block = max(1, LANES // tok)
    n_query = query_block + 2 * HALO * (STEPS - 1 - step)
    n_key = n_query + 2 * HALO
    key_lanes, query_lanes = n_key * tok, n_query * tok
    width = heads * HD
    position, tok_index = lax.axis_index("queue"), lax.axis_index("tok")
    first_key = position - HALO - (HALO + 1) * (STEPS - 1 - step)
    refs = list(refs)
    slot_ref, reach_ref = refs[0], refs[1]
    if step == 0:
        count = tok // part_rows
        lat_refs, noise_refs = refs[2 : 2 + count], refs[2 + count : 1 + 2 * count]
        refs = refs[1 + 2 * count :]
    else:
        g_ref, hprev_ref, xprev_ref = refs[2:5]
        refs = refs[5:]
    fresh_ref = None
    if step < STEPS - 1:
        fresh_ref = refs.pop(0)
    gain_ref, mq_ref, mk_ref, mv_ref, wo_ref, gram_ref, gv_ref = refs[:7]
    refs = refs[7:]
    part_ref, hpart_ref, xq_ref = refs[:3]
    refs = refs[3:]
    own_ref = None
    if step > 0:
        own_ref = refs.pop(0)
    kbuf, vbuf, qbuf, att, tbuf, xbuf = refs

    if step == 0:
        noise = [fresh_ref[0]] + [ref[0] for ref in noise_refs]
        for w in range(n_key):
            source = lax.rem(first_key - 1 + w + 2 * frames, frames)
            apart, bits = position ^ source, frames.bit_length() - 2
            second = ((apart >> bits) & 1) == 1
            entry = sum(((apart >> bit) & 1) << (bits - 1 - bit) for bit in range(bits))
            for t in range(count):
                at = lax.rem(tok_index + t, count) * part_rows + w * tok
                beside = lat_refs[t][entry]
                rows = jnp.where(second, beside[:, channels:], beside[:, :channels])
                rows = jnp.where(source == frames - 1, noise[t], rows)
                xbuf[pl.ds(pl.multiple_of(at, 8), part_rows), :] = rows
        state = xbuf[...].T
    else:
        velocity, state = advance(level_count, tok, first_key - 1, g_ref, hprev_ref, xprev_ref)
        mine = (HALO + 1) * (STEPS - step)
        own_ref[...] = own_rows(velocity[:, mine * tok : (mine + 1) * tok], tok, part_rows, tok_index, tbuf)

    key_frame = lax.broadcasted_iota(jnp.int32, (1, key_lanes), 1) // tok
    level_row = jnp.full((1, key_lanes), -1, jnp.int32)
    for w in range(n_key):
        frame = first_key + w
        known = slot_ref[jnp.clip(frame - step - 1, 0, frames - 1)] + step
        level_row = jnp.where(key_frame == w, jnp.where(frame >= step + 1, known, frame), level_row)
    row = lax.broadcasted_iota(jnp.int32, (base - channels, key_lanes), 0)
    aug_t = jnp.concatenate([state, jnp.where(row == level_row, 1.0, 0.0)], axis=0)
    aug_t = aug_t.astype(BF16).astype(F32)
    aug_tb = aug_t.astype(BF16)
    both_t = jnp.concatenate([aug_tb, aug_tb], axis=0)
    mean_t = jnp.sum(dot(gram_ref[...], both_t) * aug_t, axis=0, keepdims=True) * (1.0 / depth)
    mean_t = jnp.maximum(mean_t, 0.0) + EPS
    queries = slice(HALO * tok, HALO * tok + query_lanes)
    mean_q = mean_t[:, queries]
    aug_qb = aug_t[:, queries].astype(BF16)
    both_q = jnp.concatenate([aug_qb, aug_qb], axis=0)
    last_row = lax.broadcasted_iota(jnp.int32, (base, key_lanes), 0) == base - 1
    aug = jnp.where(last_row, EPS * mean_t, aug_t).T
    eps_c = aug[:, base - 1 : base]
    aug_b = aug.astype(BF16)

    hpart_ref[...] = dot(gv_ref[...], both_q)
    xq_ref[...] = state[:, queries]

    gain = gain_ref[0:1, :] * gain_ref[1:2, :] * (HD ** -0.5 * math.log2(math.e))
    span = 256 if width % 256 == 0 else 128
    head_of = lambda axis: lax.broadcasted_iota(jnp.int32, (span, span), axis) // HD
    average = jnp.where(head_of(0) == head_of(1), 1.0 / HD, 0.0).astype(BF16)
    for at in range(0, width, span):
        raw = dot(aug_b, mk_ref[:, at : at + span])
        spread = dot((raw * raw).astype(BF16), average)
        kbuf[:, at : at + span] = (raw * lax.rsqrt(spread + eps_c) * gain[:, at : at + span]).astype(BF16)
    vbuf[...] = (dot(mv_ref[...], aug_tb) * lax.rsqrt(mean_t)).astype(BF16)
    raw = dot(mq_ref[...], aug_qb).reshape(heads, HD, query_lanes)
    spread = jnp.sum(raw * raw, axis=1, keepdims=True) * (1.0 / HD)
    qbuf[...] = (raw * lax.rsqrt(spread + EPS * mean_q)[:, :, :]).reshape(width, query_lanes).astype(BF16)

    bound = HD * jnp.max(gain, axis=1, keepdims=True)
    upper = lax.broadcasted_iota(jnp.int32, (2 * HD, LANES), 0) < HD
    lane = lax.broadcasted_iota(jnp.int32, (1, 2 * LANES), 1)
    within = lax.rem(lane, LANES) // tok

    full = 2 * HALO + query_block
    if query_block == 1:
        cuts = [(HALO - r, 2 * r + 1) for r in range(HALO + 1)]
    else:
        cuts = [(2, full - 4), (2, full - 2), (0, full - 2), (0, full)]

    def reaches(lead):
        widths = []
        for j in range(query_block):
            frame = first_key + HALO + lead + j
            needed = (frame >= 0) & (frame < frames) & (lead + j <= n_query - query_block)
            widths.append(jnp.where(needed, reach_ref[jnp.clip(frame, 0, frames - 1)], -1))
        return widths

    def biases(lead, shift):
        rows, widths = [], reaches(lead)
        for k in range(full):
            target = first_key + lead + k
            inside = (target >= 0) & (target < frames)
            row = jnp.zeros((1, 2 * LANES), F32)
            for j in range(query_block):
                counted = (inside & (abs(k - HALO - j) <= widths[j])) | (widths[j] < 0)
                row = jnp.where(within == j, jnp.where(counted, 0.0, -1e30), row)
            rows.append(row - shift)
        return rows

    def span_of(first, count):
        return pl.ds(pl.multiple_of(first * tok, LANES), count * tok)

    def scores(keys, lanes, cols, rows):
        query = qbuf[cols, lanes]
        zero = jnp.zeros_like(query)
        query = jnp.concatenate([jnp.where(upper, query, zero), jnp.where(upper, zero, query)], axis=1)
        score = dot(kbuf[keys, cols], query)
        return jnp.concatenate([score[k * tok : (k + 1) * tok] + rows[k] for k in range(len(rows))], axis=0)

    def mix(keys, lanes, cols, weight):
        ones = jnp.ones((16, weight.shape[0]), BF16)
        mixed = dot(jnp.concatenate([vbuf[cols, keys], ones], axis=0), weight.astype(BF16))
        total = mixed[2 * HD : 2 * HD + 1, :]
        scale = 1.0 / total
        top = mixed[:HD, :LANES] * scale[:, :LANES]
        bottom = mixed[HD : 2 * HD, LANES:] * scale[:, LANES:]
        att[cols, lanes] = jnp.concatenate([top, bottom], axis=0).astype(BF16)
        return total

    def block(b, least):
        lead = (b * LANES) // tok
        lanes = pl.ds(pl.multiple_of(b * LANES, LANES), LANES)
        rows, widths = biases(lead, bound), reaches(lead)

        def run(first, count, least):
            keys = span_of(lead + first, count)
            held = None
            for pair in range(heads // 2):
                cols = slice(pair * 2 * HD, (pair + 1) * 2 * HD)
                weight = jnp.exp2(scores(keys, lanes, cols, rows[first : first + count])).astype(BF16)
                if held is not None:
                    least = jnp.minimum(least, mix(keys, lanes, *held))
                held = (cols, weight)
            return jnp.minimum(least, mix(keys, lanes, *held))

        if query_block == 1:
            chosen = jnp.maximum(widths[0], 0)
        else:
            left, right = widths[0], widths[0] - query_block + 1
            for j in range(1, query_block):
                left = jnp.maximum(left, widths[j] - j)
                right = jnp.maximum(right, widths[j] + j - query_block + 1)
            chosen = jnp.where(left > 1, 2, 0) + jnp.where(right > 1, 1, 0)
        return lax.switch(chosen, [functools.partial(run, *cut) for cut in cuts], least)

    def exact_block(at, carry):
        lead = (at // (heads // 2) * LANES) // tok
        keys = span_of(lead, full)
        lanes = pl.ds(pl.multiple_of(at // (heads // 2) * LANES, LANES), LANES)
        cols = pl.ds(pl.multiple_of(lax.rem(at, heads // 2) * 2 * HD, 2 * HD), 2 * HD)
        score = scores(keys, lanes, cols, biases(lead, 0.0))
        mix(keys, lanes, cols, jnp.exp2(score - jnp.max(score, axis=0, keepdims=True)))
        return carry

    blocks = query_lanes // LANES
    least = jnp.ones((1, 2 * LANES), F32)
    least = block(0, least) if blocks == 1 else lax.fori_loop(0, blocks, block, least)

    @pl.when(jnp.min(least) < 1e-25)
    def _():
        lax.fori_loop(0, blocks * (heads // 2), exact_block, 0)

    mixed = dot(wo_ref[...], att[...])
    partial = mixed[:channels] + mixed[channels:]
    if step < STEPS - 1:
        tbuf[...] = jnp.zeros_like(tbuf)
        tbuf[pl.ds(pl.multiple_of(tok_index * part_rows, 8), part_rows), :] = fresh_ref[step + 1]
        fresh_t = tbuf[...].T
        fresh_t = jnp.concatenate([fresh_t] * n_query, axis=1)
        slot = lax.broadcasted_iota(jnp.int32, (1, query_lanes), 1) // tok + first_key + HALO
        partial = jnp.where(slot == -1, fresh_t, partial)
    part_ref[...] = partial[:, : part_ref.shape[1]]


def last_kernel(cfg, *refs):
    tok, frames, channels, base, depth, level_count, heads, part_rows = cfg
    g_ref, hpart_ref, xq_ref = refs[:3]
    own = refs[3 : 3 + STEPS - 1]
    velocity_ref, queue_ref, tbuf = refs[3 + STEPS - 1 :]
    tok_index = lax.axis_index("tok")
    velocity, moved = advance(level_count, tok, None, g_ref, hpart_ref, xq_ref)
    for s in range(STEPS - 1):
        velocity_ref[s, 0] = own[s][...]
    velocity_ref[STEPS - 1, 0] = own_rows(velocity[:, :tok], tok, part_rows, tok_index, tbuf)
    queue_ref[0] = own_rows(moved[:, :tok], tok, part_rows, tok_index, tbuf)


def body(
    latent,
    fresh_noise,
    frame_slot,
    frame_reach,
    level_embed,
    embed_weight,
    qkv_weight,
    qk_gain,
    out_weight,
    vel_weight,
):
    frames, parts = lax.axis_size("queue"), lax.axis_size("tok")
    position = lax.axis_index("queue")
    part_rows, channels = latent.shape[1], latent.shape[2]
    tok = part_rows * parts
    level_count = level_embed.shape[0]
    depth = qkv_weight.shape[2]
    width = qkv_weight.shape[1]
    spare = round_up(width, 2 * LANES) - width
    if spare:
        qkv_weight = jnp.pad(qkv_weight, ((0, 0), (0, spare), (0, 0)))
        qk_gain = jnp.pad(qk_gain, ((0, 0), (0, spare)))
        out_weight = jnp.pad(out_weight, ((0, spare), (0, 0)))
        width += spare
    heads = width // HD
    base = round_up(channels + level_count + 1, LANES)
    cfg = (tok, frames, channels, base, depth, level_count, heads, part_rows)
    vmem, smem, hbm, anywhere = (
        pl.BlockSpec(memory_space=pltpu.VMEM),
        pl.BlockSpec(memory_space=pltpu.SMEM),
        pl.BlockSpec(memory_space=pltpu.HBM),
        pl.BlockSpec(memory_space=pl.ANY),
    )
    shape = jax.ShapeDtypeStruct

    def swapped(value, axis, distance):
        count = lax.axis_size(axis)
        return lax.ppermute(value, axis, [(source, source ^ distance) for source in range(count)])

    def from_ahead(value, distance):
        return lax.ppermute(value, "tok", [(source, (source - distance) % parts) for source in range(parts)])

    share = depth // parts
    table = (embed_weight, level_embed, vel_weight.T)
    around = range(1, parts)
    tables = [from_ahead(piece, d) for d in around for piece in table]
    noise = [from_ahead(fresh_noise, d) for d in around]
    in_hbm = lambda array: pltpu.with_memory_space_constraint(array, pltpu.HBM)
    table = tuple(in_hbm(piece) for piece in table)
    qkv_weight, out_weight = in_hbm(qkv_weight), in_hbm(out_weight)
    rows = 384 if width % 384 == 0 else 256
    chunks = 2 * width // rows

    def weights(kernel, shares, outs, held, after, *operands):
        count = len(shares)
        scratch = [pltpu.VMEM(piece.shape, BF16) for piece in held]
        if held:
            scratch.append(pltpu.SemaphoreType.DMA((len(held),)))
        scratch += [pltpu.VMEM((count, chunks, rows, share), BF16), pltpu.SemaphoreType.DMA((chunks, count))]
        return pl.pallas_call(
            functools.partial(kernel, shares),
            out_shape=tuple(outs),
            in_specs=[hbm] * len(held)
            + [vmem] * (len(operands) - len(held))
            + [hbm] * 2
            + [anywhere] * len(after),
            out_specs=(vmem,) * len(outs),
            scratch_shapes=scratch,
            compiler_params=pltpu.CompilerParams(vmem_limit_bytes=24 * 2**20),
            cost_estimate=pl.CostEstimate(
                flops=4 * base * width * share * count,
                bytes_accessed=4 * width * share * count,
                transcendentals=0,
            ),
            name="weights",
        )(*operands, qkv_weight, out_weight, *after)

    keys_part = lambda shares, *refs: keys_kernel(rows, base, shares, *refs)
    values_part = lambda shares, *refs: values_kernel(rows, shares, *refs)
    turned_tables = lambda count: [shape((count * share, base), BF16), shape((count * share, channels), BF16)]
    others = tuple(around)

    def own_keys(*after):
        outs = [shape((2 * width, base), F32), shape((base, base), F32), shape((channels, base), F32)]
        return weights(keys_part, (0,), outs + turned_tables(1), table, after, *table)

    def own_values(*after):
        outs = [shape((width, base), F32), shape((width, channels), F32)]
        return weights(values_part, (0,), outs, (), after, *done[0][3:])

    def other_keys(*after):
        outs = [
            shape((width, base), BF16),
            shape((base, width), BF16),
            shape((base, 2 * base), BF16),
            shape((channels, 2 * base), BF16),
        ]
        return weights(keys_part, others, outs + turned_tables(parts - 1), (), after, *tables, *done[0][:3])

    def other_values(*after):
        outs = [shape((width, base), BF16), shape((2 * channels, width), BF16)]
        return weights(values_part, others, outs, (), after, *done[2][4:], *done[1])

    state = latent
    work = [own_keys, own_values, other_keys, other_values]
    done, after = [], ()
    distance = frames // 2
    while distance:
        moved = swapped(state, "queue", distance)
        if len(done) < len(work):
            moved, noise, result = lax.optimization_barrier((moved, noise, work[len(done)](*after)))
            done.append(result)
            after = (moved,)
        axis = 2 if distance == frames // 2 else 0
        state = lax.optimization_barrier(jnp.concatenate([state, moved], axis=axis))
        distance //= 2
    while len(done) < len(work):
        done.append(work[len(done)]())
    latents = [state] + [from_ahead(state, d) for d in range(1, parts)] + noise
    mq, mk, gram, gv = done[2][:4]
    mv, wo = done[3]

    query_block = max(1, LANES // tok)
    owned = []
    for step in range(STEPS):
        n_query = query_block + 2 * HALO * (STEPS - 1 - step)
        query_lanes, key_lanes = n_query * tok, (n_query + 2 * HALO) * tok
        args = [frame_slot, frame_reach]
        specs = [smem, smem]
        if step == 0:
            args += latents
            specs += [vmem] * len(latents)
        else:
            args += [gathered, hpart, xq]
            specs += [vmem] * 3
        if step < STEPS - 1:
            args += [fresh_noise]
            specs += [vmem]
        args += [qk_gain, mq, mk, mv, wo, gram, gv]
        specs += [vmem] * 7
        outs = [shape((channels, query_lanes), F32)] * 3
        if step > 0:
            outs += [shape((part_rows, channels), F32)]
        window = (2 * HALO + query_block) * tok
        result = pl.pallas_call(
            functools.partial(step_kernel, step, cfg),
            out_shape=tuple(outs),
            in_specs=specs,
            out_specs=(vmem,) * len(outs),
            scratch_shapes=[
                pltpu.VMEM((key_lanes, width), BF16),
                pltpu.VMEM((width, key_lanes), BF16),
                pltpu.VMEM((width, query_lanes), BF16),
                pltpu.VMEM((width, query_lanes), BF16),
                pltpu.VMEM((tok, channels), F32),
                pltpu.VMEM((key_lanes if step == 0 else tok, channels), F32),
            ],
            compiler_params=pltpu.CompilerParams(vmem_limit_bytes=48 * 2**20),
            cost_estimate=pl.CostEstimate(
                flops=4 * query_lanes * window * width + 12 * key_lanes * base * width,
                bytes_accessed=8 * width * base,
                transcendentals=query_lanes * window * heads,
            ),
            name="step%d" % step,
        )(*args)
        part, hpart, xq = result[:3]
        owned += list(result[3:])
        gathered = lax.all_gather(part, "tok", axis=0, tiled=False)

    return tuple(
        pl.pallas_call(
            functools.partial(last_kernel, cfg),
            out_shape=(
                shape((STEPS, 1, part_rows, channels), F32),
                shape((1, part_rows, channels), F32),
            ),
            in_specs=[vmem] * (3 + len(owned)),
            out_specs=(vmem, vmem),
            scratch_shapes=[pltpu.VMEM((tok, channels), F32)],
            compiler_params=pltpu.CompilerParams(vmem_limit_bytes=8 * 2**20),
            name="last",
        )(gathered, hpart, xq, *owned)
    )


def solution(mesh):
    return jax.shard_map(
        body,
        mesh=mesh,
        in_specs=(
            P("queue", "tok", None),
            P(None, "tok", None),
            P(),
            P(),
            P(None, "tok"),
            P(None, "tok"),
            P(None, "tok", None),
            P(None, "tok"),
            P("tok", None),
            P("tok", None),
        ),
        out_specs=(P(None, "queue", "tok", None), P("queue", "tok", None)),
        check_vma=False,
    )
```

```python
import functools
import math

import jax
import jax.numpy as jnp
from jax import lax
from jax.experimental import pallas as pl
from jax.experimental.pallas import tpu as pltpu
from jax.sharding import PartitionSpec as P

HD = 64
STEPS = 3
HALO = 3
LANES = 128
EPS = 1e-06
F32, BF16 = jnp.float32, jnp.bfloat16


def round_up(value, unit):
    return -(-value // unit) * unit


def dot(a, b):
    return jnp.dot(a, b, preferred_element_type=F32)


def dot_nt(a, b):
    return lax.dot_general(a, b, (((1,), (1,)), ((), ())), preferred_element_type=F32)


def halves(value, axis):
    high = value.astype(BF16)
    low = (value - high.astype(F32)).astype(BF16)
    return jnp.concatenate([high, low], axis=axis)


def chunk_copies(rows, chunks, parts, qkv_hbm, out_hbm, buf, sems):
    per = out_hbm.shape[0] // rows
    depth = buf.shape[-1]
    index, count = lax.axis_index("tok"), lax.axis_size("tok")
    copies = {}
    for place, chunk in enumerate(chunks):
        source = qkv_hbm.at[chunk // per] if chunk < 3 * per else out_hbm
        for at, part in enumerate(parts):
            columns = pl.ds(pl.multiple_of(lax.rem(index + part, count) * depth, LANES), depth)
            copies[place, at] = pltpu.make_async_copy(
                source.at[pl.ds((chunk % per) * rows, rows), columns],
                buf.at[at, place],
                sems.at[place, at],
            )
    return copies


def started(sources, targets, sems):
    copies = [pltpu.make_async_copy(a, b, sems.at[i]) for i, (a, b) in enumerate(zip(sources, targets))]
    for copy in copies:
        copy.start()
    return copies


def turned(value):
    return value.astype(F32).T.astype(BF16)


def keys_kernel(rows, base, shares, *refs):
    own, count = shares == (0,), len(shares)
    tables, refs = refs[: 2 * count], refs[2 * count :]
    if own:
        qkv_hbm, out_hbm = refs[:2]
        total_ref, gram_ref, right_ref, embed, level, small, buf, sems = refs[-8:]
        brought = started(tables, (embed, level), small)
    else:
        sum_ref, gram_sum, qkv_hbm, out_hbm = refs[:4]
        mq_ref, mk_ref, gram_ref, right_ref, buf, sems = refs[-6:]
    per = out_hbm.shape[0] // rows
    depth = buf.shape[-1]
    copies = chunk_copies(rows, range(2 * per), shares, qkv_hbm, out_hbm, buf, sems)
    for copy in copies.values():
        copy.start()
    if own:
        for copy in brought:
            copy.wait()
        tables = (embed, level)
    gram = jnp.zeros((base, base), F32) if own else gram_sum[...]
    for at in range(count):
        left = [tables[2 * at][...].astype(F32), tables[2 * at + 1][...].astype(F32)]
        left.append(jnp.zeros((base - left[0].shape[0] - left[1].shape[0], depth), F32))
        left = jnp.concatenate(left, axis=0)
        right_ref[at * depth : (at + 1) * depth, :] = left.T.astype(BF16)
        gram = gram + dot(left.astype(BF16), right_ref[at * depth : (at + 1) * depth, :])
    gram_ref[...] = gram if own else halves(gram, 1)
    for chunk in range(2 * per):
        spot = slice(chunk * rows, (chunk + 1) * rows)
        total = None if own else sum_ref[spot, :]
        for at in range(count):
            copies[chunk, at].wait()
            product = dot(buf[at, chunk], right_ref[at * depth : (at + 1) * depth, :])
            total = product if total is None else total + product
        where = slice((chunk % per) * rows, (chunk % per + 1) * rows)
        if own:
            total_ref[spot, :] = total
        elif chunk < per:
            mq_ref[where, :] = total.astype(BF16)
        else:
            mk_ref[:, where] = total.T.astype(BF16)


def values_kernel(rows, shares, *refs):
    own, count = shares == (0,), len(shares)
    tables, right_ref, refs = refs[:count], refs[count], refs[count + 1 :]
    if own:
        qkv_hbm, out_hbm = refs[:2]
        mv_ref, wo_ref, gv_ref, held, small, buf, sems = refs[-7:]
        brought = started(tables, (held,), small)
    else:
        mv_sum, wo_sum, gv_sum, qkv_hbm, out_hbm = refs[:5]
        mv_ref, wo_ref, gv_ref, buf, sems = refs[-5:]
    per = out_hbm.shape[0] // rows
    depth = buf.shape[-1]
    copies = chunk_copies(rows, range(2 * per, 4 * per), shares, qkv_hbm, out_hbm, buf, sems)
    for copy in copies.values():
        copy.start()
    if own:
        brought[0].wait()
        tables = (held,)
    vels = [table[...] for table in tables]
    gv = sum(dot(vel, right_ref[at * depth : (at + 1) * depth, :]) for at, vel in enumerate(vels))
    gv_ref[...] = gv if own else halves(gv_sum[...] + gv, 1)
    downs = [turned(vel) for vel in vels]
    for place in range(2 * per):
        where = slice((place % per) * rows, (place % per + 1) * rows)
        total = None if own else (mv_sum if place < per else wo_sum)[where, :]
        for at in range(count):
            copies[place, at].wait()
            right = right_ref[at * depth : (at + 1) * depth, :] if place < per else downs[at]
            product = dot(buf[at, place], right)
            total = product if total is None else total + product
        if own:
            (mv_ref if place < per else wo_ref)[where, :] = total
        elif place < per:
            mv_ref[where, :] = total.astype(BF16)
        else:
            wo_ref[:, where] = halves(total.T, 0)


def advance(level_count, tok, first, g_ref, hpart_ref, xq_ref):
    shared = g_ref[0]
    for t in range(1, g_ref.shape[0]):
        shared = shared + g_ref[t]
    velocity = shared + hpart_ref[...]
    moved = xq_ref[...] - velocity * (1.0 / level_count)
    if first is None:
        return velocity, moved
    lane_frame = lax.broadcasted_iota(jnp.int32, (1, shared.shape[1]), 1) // tok
    return velocity, jnp.where(lane_frame + first == -1, shared, moved)


def own_rows(block, tok, part_rows, index, scratch):
    scratch[...] = block.T
    return scratch[pl.ds(pl.multiple_of(index * part_rows, 8), part_rows), :]


def step_kernel(step, cfg, *refs):
    tok, frames, channels, base, depth, level_count, heads, part_rows = cfg
    query_block = max(1, LANES // tok)
    n_query = query_block + 2 * HALO * (STEPS - 1 - step)
    n_key = n_query + 2 * HALO
    key_lanes, query_lanes = n_key * tok, n_query * tok
    width = heads * HD
    position, tok_index = lax.axis_index("queue"), lax.axis_index("tok")
    first_key = position - HALO - (HALO + 1) * (STEPS - 1 - step)
    refs = list(refs)
    slot_ref, reach_ref = refs[0], refs[1]
    if step == 0:
        count = tok // part_rows
        lat_refs, noise_refs = refs[2 : 2 + count], refs[2 + count : 1 + 2 * count]
        refs = refs[1 + 2 * count :]
    else:
        g_ref, hprev_ref, xprev_ref = refs[2:5]
        refs = refs[5:]
    fresh_ref = None
    if step < STEPS - 1:
        fresh_ref = refs.pop(0)
    gain_ref, mq_ref, mk_ref, mv_ref, wo_ref, gram_ref, gv_ref = refs[:7]
    refs = refs[7:]
    part_ref, hpart_ref, xq_ref = refs[:3]
    refs = refs[3:]
    own_ref = None
    if step > 0:
        own_ref = refs.pop(0)
    kbuf, vbuf, qbuf, att, tbuf, xbuf = refs

    if step == 0:
        noise = [fresh_ref[0]] + [ref[0] for ref in noise_refs]
        for w in range(n_key):
            source = lax.rem(first_key - 1 + w + 2 * frames, frames)
            apart, bits = position ^ source, frames.bit_length() - 2
            second = ((apart >> bits) & 1) == 1
            entry = sum(((apart >> bit) & 1) << (bits - 1 - bit) for bit in range(bits))
            for t in range(count):
                at = lax.rem(tok_index + t, count) * part_rows + w * tok
                beside = lat_refs[t][entry]
                rows = jnp.where(second, beside[:, channels:], beside[:, :channels])
                rows = jnp.where(source == frames - 1, noise[t], rows)
                xbuf[pl.ds(pl.multiple_of(at, 8), part_rows), :] = rows
        state = xbuf[...].T
    else:
        velocity, state = advance(level_count, tok, first_key - 1, g_ref, hprev_ref, xprev_ref)
        mine = (HALO + 1) * (STEPS - step)
        own_ref[...] = own_rows(velocity[:, mine * tok : (mine + 1) * tok], tok, part_rows, tok_index, tbuf)

    key_frame = lax.broadcasted_iota(jnp.int32, (1, key_lanes), 1) // tok
    level_row = jnp.full((1, key_lanes), -1, jnp.int32)
    for w in range(n_key):
        frame = first_key + w
        known = slot_ref[jnp.clip(frame - step - 1, 0, frames - 1)] + step
        level_row = jnp.where(key_frame == w, jnp.where(frame >= step + 1, known, frame), level_row)
    row = lax.broadcasted_iota(jnp.int32, (base - channels, key_lanes), 0)
    aug_t = jnp.concatenate([state, jnp.where(row == level_row, 1.0, 0.0)], axis=0)
    aug_t = aug_t.astype(BF16).astype(F32)
    aug_tb = aug_t.astype(BF16)
    both_t = jnp.concatenate([aug_tb, aug_tb], axis=0)
    mean_t = jnp.sum(dot(gram_ref[...], both_t) * aug_t, axis=0, keepdims=True) * (1.0 / depth)
    mean_t = jnp.maximum(mean_t, 0.0) + EPS
    queries = slice(HALO * tok, HALO * tok + query_lanes)
    mean_q = mean_t[:, queries]
    aug_qb = aug_t[:, queries].astype(BF16)
    both_q = jnp.concatenate([aug_qb, aug_qb], axis=0)
    last_row = lax.broadcasted_iota(jnp.int32, (base, key_lanes), 0) == base - 1
    aug = jnp.where(last_row, EPS * mean_t, aug_t).T
    eps_c = aug[:, base - 1 : base]
    aug_b = aug.astype(BF16)

    hpart_ref[...] = dot(gv_ref[...], both_q)
    xq_ref[...] = state[:, queries]

    gain = gain_ref[0:1, :] * gain_ref[1:2, :] * (HD ** -0.5 * math.log2(math.e))
    span = 256 if width % 256 == 0 else 128
    head_of = lambda axis: lax.broadcasted_iota(jnp.int32, (span, span), axis) // HD
    average = jnp.where(head_of(0) == head_of(1), 1.0 / HD, 0.0).astype(BF16)
    for at in range(0, width, span):
        raw = dot(aug_b, mk_ref[:, at : at + span])
        spread = dot((raw * raw).astype(BF16), average)
        kbuf[:, at : at + span] = (raw * lax.rsqrt(spread + eps_c) * gain[:, at : at + span]).astype(BF16)
    vbuf[...] = (dot(mv_ref[...], aug_tb) * lax.rsqrt(mean_t)).astype(BF16)
    raw = dot(mq_ref[...], aug_qb).reshape(heads, HD, query_lanes)
    spread = jnp.sum(raw * raw, axis=1, keepdims=True) * (1.0 / HD)
    qbuf[...] = (raw * lax.rsqrt(spread + EPS * mean_q)[:, :, :]).reshape(width, query_lanes).astype(BF16)

    bound = HD * jnp.max(gain, axis=1, keepdims=True)
    upper = lax.broadcasted_iota(jnp.int32, (2 * HD, LANES), 0) < HD
    lane = lax.broadcasted_iota(jnp.int32, (1, 2 * LANES), 1)
    within = lax.rem(lane, LANES) // tok

    full = 2 * HALO + query_block
    if query_block == 1:
        cuts = [(HALO - r, 2 * r + 1) for r in range(HALO + 1)]
    else:
        cuts = [(2, full - 4), (2, full - 2), (0, full - 2), (0, full)]

    def reaches(lead):
        widths = []
        for j in range(query_block):
            frame = first_key + HALO + lead + j
            needed = (frame >= 0) & (frame < frames) & (lead + j <= n_query - query_block)
            widths.append(jnp.where(needed, reach_ref[jnp.clip(frame, 0, frames - 1)], -1))
        return widths

    def biases(lead, shift):
        rows, widths = [], reaches(lead)
        for k in range(full):
            target = first_key + lead + k
            inside = (target >= 0) & (target < frames)
            row = jnp.zeros((1, 2 * LANES), F32)
            for j in range(query_block):
                counted = (inside & (abs(k - HALO - j) <= widths[j])) | (widths[j] < 0)
                row = jnp.where(within == j, jnp.where(counted, 0.0, -1e30), row)
            rows.append(row - shift)
        return rows

    def span_of(first, count):
        return pl.ds(pl.multiple_of(first * tok, LANES), count * tok)

    def scores(keys, lanes, cols, rows):
        query = qbuf[cols, lanes]
        zero = jnp.zeros_like(query)
        query = jnp.concatenate([jnp.where(upper, query, zero), jnp.where(upper, zero, query)], axis=1)
        score = dot(kbuf[keys, cols], query)
        return jnp.concatenate([score[k * tok : (k + 1) * tok] + rows[k] for k in range(len(rows))], axis=0)

    def mix(keys, lanes, cols, weight):
        ones = jnp.ones((16, weight.shape[0]), BF16)
        mixed = dot(jnp.concatenate([vbuf[cols, keys], ones], axis=0), weight.astype(BF16))
        total = mixed[2 * HD : 2 * HD + 1, :]
        scale = 1.0 / total
        top = mixed[:HD, :LANES] * scale[:, :LANES]
        bottom = mixed[HD : 2 * HD, LANES:] * scale[:, LANES:]
        att[cols, lanes] = jnp.concatenate([top, bottom], axis=0).astype(BF16)
        return total

    def block(b, least):
        lead = (b * LANES) // tok
        lanes = pl.ds(pl.multiple_of(b * LANES, LANES), LANES)
        rows, widths = biases(lead, bound), reaches(lead)

        def run(first, count, least):
            keys = span_of(lead + first, count)
            held = None
            for pair in range(heads // 2):
                cols = slice(pair * 2 * HD, (pair + 1) * 2 * HD)
                weight = jnp.exp2(scores(keys, lanes, cols, rows[first : first + count])).astype(BF16)
                if held is not None:
                    least = jnp.minimum(least, mix(keys, lanes, *held))
                held = (cols, weight)
            return jnp.minimum(least, mix(keys, lanes, *held))

        if query_block == 1:
            chosen = jnp.maximum(widths[0], 0)
        else:
            left, right = widths[0], widths[0] - query_block + 1
            for j in range(1, query_block):
                left = jnp.maximum(left, widths[j] - j)
                right = jnp.maximum(right, widths[j] + j - query_block + 1)
            chosen = jnp.where(left > 1, 2, 0) + jnp.where(right > 1, 1, 0)
        return lax.switch(chosen, [functools.partial(run, *cut) for cut in cuts], least)

    def exact_block(at, carry):
        lead = (at // (heads // 2) * LANES) // tok
        keys = span_of(lead, full)
        lanes = pl.ds(pl.multiple_of(at // (heads // 2) * LANES, LANES), LANES)
        cols = pl.ds(pl.multiple_of(lax.rem(at, heads // 2) * 2 * HD, 2 * HD), 2 * HD)
        score = scores(keys, lanes, cols, biases(lead, 0.0))
        mix(keys, lanes, cols, jnp.exp2(score - jnp.max(score, axis=0, keepdims=True)))
        return carry

    blocks = query_lanes // LANES
    least = jnp.ones((1, 2 * LANES), F32)
    least = block(0, least) if blocks == 1 else lax.fori_loop(0, blocks, block, least)

    @pl.when(jnp.min(least) < 1e-25)
    def _():
        lax.fori_loop(0, blocks * (heads // 2), exact_block, 0)

    mixed = dot(wo_ref[...], att[...])
    partial = mixed[:channels] + mixed[channels:]
    if step < STEPS - 1:
        tbuf[...] = jnp.zeros_like(tbuf)
        tbuf[pl.ds(pl.multiple_of(tok_index * part_rows, 8), part_rows), :] = fresh_ref[step + 1]
        fresh_t = tbuf[...].T
        fresh_t = jnp.concatenate([fresh_t] * n_query, axis=1)
        slot = lax.broadcasted_iota(jnp.int32, (1, query_lanes), 1) // tok + first_key + HALO
        partial = jnp.where(slot == -1, fresh_t, partial)
    part_ref[...] = partial[:, : part_ref.shape[1]]


def last_kernel(cfg, *refs):
    tok, frames, channels, base, depth, level_count, heads, part_rows = cfg
    g_ref, hpart_ref, xq_ref = refs[:3]
    own = refs[3 : 3 + STEPS - 1]
    velocity_ref, queue_ref, tbuf = refs[3 + STEPS - 1 :]
    tok_index = lax.axis_index("tok")
    velocity, moved = advance(level_count, tok, None, g_ref, hpart_ref, xq_ref)
    for s in range(STEPS - 1):
        velocity_ref[s, 0] = own[s][...]
    velocity_ref[STEPS - 1, 0] = own_rows(velocity[:, :tok], tok, part_rows, tok_index, tbuf)
    queue_ref[0] = own_rows(moved[:, :tok], tok, part_rows, tok_index, tbuf)


def body(
    latent,
    fresh_noise,
    frame_slot,
    frame_reach,
    level_embed,
    embed_weight,
    qkv_weight,
    qk_gain,
    out_weight,
    vel_weight,
):
    frames, parts = lax.axis_size("queue"), lax.axis_size("tok")
    position = lax.axis_index("queue")
    part_rows, channels = latent.shape[1], latent.shape[2]
    tok = part_rows * parts
    level_count = level_embed.shape[0]
    depth = qkv_weight.shape[2]
    width = qkv_weight.shape[1]
    spare = round_up(width, 2 * LANES) - width
    if spare:
        qkv_weight = jnp.pad(qkv_weight, ((0, 0), (0, spare), (0, 0)))
        qk_gain = jnp.pad(qk_gain, ((0, 0), (0, spare)))
        out_weight = jnp.pad(out_weight, ((0, spare), (0, 0)))
        width += spare
    heads = width // HD
    base = round_up(channels + level_count + 1, LANES)
    cfg = (tok, frames, channels, base, depth, level_count, heads, part_rows)
    vmem, smem, hbm, anywhere = (
        pl.BlockSpec(memory_space=pltpu.VMEM),
        pl.BlockSpec(memory_space=pltpu.SMEM),
        pl.BlockSpec(memory_space=pltpu.HBM),
        pl.BlockSpec(memory_space=pl.ANY),
    )
    shape = jax.ShapeDtypeStruct

    def swapped(value, axis, distance):
        count = lax.axis_size(axis)
        return lax.ppermute(value, axis, [(source, source ^ distance) for source in range(count)])

    def from_ahead(value, distance):
        return lax.ppermute(value, "tok", [(source, (source - distance) % parts) for source in range(parts)])

    share = depth // parts
    table = (embed_weight, level_embed, vel_weight.T)
    around = range(1, parts)
    tables = [from_ahead(piece, d) for d in around for piece in table[:2]]
    vel_tables = [from_ahead(table[2], d) for d in around]
    noise = [from_ahead(fresh_noise, d) for d in around]
    in_hbm = lambda array: pltpu.with_memory_space_constraint(array, pltpu.HBM)
    table = tuple(in_hbm(piece) for piece in table)
    qkv_weight, out_weight = in_hbm(qkv_weight), in_hbm(out_weight)
    rows = 768 if width % 768 == 0 else 256
    chunks = 2 * width // rows

    def weights(kernel, shares, outs, held, after, *operands):
        count = len(shares)
        scratch = [pltpu.VMEM(piece.shape, BF16) for piece in held]
        if held:
            scratch.append(pltpu.SemaphoreType.DMA((len(held),)))
        scratch += [pltpu.VMEM((count, chunks, rows, share), BF16), pltpu.SemaphoreType.DMA((chunks, count))]
        return pl.pallas_call(
            functools.partial(kernel, shares),
            out_shape=tuple(outs),
            in_specs=[hbm] * len(held)
            + [vmem] * (len(operands) - len(held))
            + [hbm] * 2
            + [anywhere] * len(after),
            out_specs=(vmem,) * len(outs),
            scratch_shapes=scratch,
            compiler_params=pltpu.CompilerParams(vmem_limit_bytes=24 * 2**20),
            cost_estimate=pl.CostEstimate(
                flops=4 * base * width * share * count,
                bytes_accessed=4 * width * share * count,
                transcendentals=0,
            ),
            name="weights",
        )(*operands, qkv_weight, out_weight, *after)

    keys_part = lambda shares, *refs: keys_kernel(rows, base, shares, *refs)
    values_part = lambda shares, *refs: values_kernel(rows, shares, *refs)
    right = lambda count: shape((count * share, base), BF16)
    others = tuple(around)

    def own_keys(*after):
        outs = [shape((2 * width, base), F32), shape((base, base), F32), right(1)]
        return weights(keys_part, (0,), outs, table[:2], after, *table[:2])

    def own_values(*after):
        outs = [shape((width, base), F32), shape((width, channels), F32), shape((channels, base), F32)]
        return weights(values_part, (0,), outs, table[2:], after, table[2], done[0][2])

    def other_keys(*after):
        outs = [
            shape((width, base), BF16),
            shape((base, width), BF16),
            shape((base, 2 * base), BF16),
            right(parts - 1),
        ]
        return weights(keys_part, others, outs, (), after, *tables, *done[0][:2])

    def other_values(*after):
        outs = [
            shape((width, base), BF16),
            shape((2 * channels, width), BF16),
            shape((channels, 2 * base), BF16),
        ]
        return weights(values_part, others, outs, (), after, *vel_tables, done[2][3], *done[1])

    state = latent
    work = [own_keys, own_values, other_keys, other_values]
    done, after = [], ()
    distance = frames // 2
    while distance:
        moved = swapped(state, "queue", distance)
        if len(done) < len(work):
            moved, noise, result = lax.optimization_barrier((moved, noise, work[len(done)](*after)))
            done.append(result)
            after = (moved,)
        axis = 2 if distance == frames // 2 else 0
        state = lax.optimization_barrier(jnp.concatenate([state, moved], axis=axis))
        distance //= 2
    while len(done) < len(work):
        done.append(work[len(done)]())
    latents = [state] + [from_ahead(state, d) for d in range(1, parts)] + noise
    mq, mk, gram = done[2][:3]
    mv, wo, gv = done[3]

    query_block = max(1, LANES // tok)
    owned = []
    for step in range(STEPS):
        n_query = query_block + 2 * HALO * (STEPS - 1 - step)
        query_lanes, key_lanes = n_query * tok, (n_query + 2 * HALO) * tok
        args = [frame_slot, frame_reach]
        specs = [smem, smem]
        if step == 0:
            args += latents
            specs += [vmem] * len(latents)
        else:
            args += [gathered, hpart, xq]
            specs += [vmem] * 3
        if step < STEPS - 1:
            args += [fresh_noise]
            specs += [vmem]
        args += [qk_gain, mq, mk, mv, wo, gram, gv]
        specs += [vmem] * 7
        outs = [shape((channels, query_lanes), F32)] * 3
        if step > 0:
            outs += [shape((part_rows, channels), F32)]
        window = (2 * HALO + query_block) * tok
        result = pl.pallas_call(
            functools.partial(step_kernel, step, cfg),
            out_shape=tuple(outs),
            in_specs=specs,
            out_specs=(vmem,) * len(outs),
            scratch_shapes=[
                pltpu.VMEM((key_lanes, width), BF16),
                pltpu.VMEM((width, key_lanes), BF16),
                pltpu.VMEM((width, query_lanes), BF16),
                pltpu.VMEM((width, query_lanes), BF16),
                pltpu.VMEM((tok, channels), F32),
                pltpu.VMEM((key_lanes if step == 0 else tok, channels), F32),
            ],
            compiler_params=pltpu.CompilerParams(vmem_limit_bytes=48 * 2**20),
            cost_estimate=pl.CostEstimate(
                flops=4 * query_lanes * window * width + 12 * key_lanes * base * width,
                bytes_accessed=8 * width * base,
                transcendentals=query_lanes * window * heads,
            ),
            name="step%d" % step,
        )(*args)
        part, hpart, xq = result[:3]
        owned += list(result[3:])
        gathered = lax.all_gather(part, "tok", axis=0, tiled=False)

    return tuple(
        pl.pallas_call(
            functools.partial(last_kernel, cfg),
            out_shape=(
                shape((STEPS, 1, part_rows, channels), F32),
                shape((1, part_rows, channels), F32),
            ),
            in_specs=[vmem] * (3 + len(owned)),
            out_specs=(vmem, vmem),
            scratch_shapes=[pltpu.VMEM((tok, channels), F32)],
            compiler_params=pltpu.CompilerParams(vmem_limit_bytes=8 * 2**20),
            name="last",
        )(gathered, hpart, xq, *owned)
    )


def solution(mesh):
    return jax.shard_map(
        body,
        mesh=mesh,
        in_specs=(
            P("queue", "tok", None),
            P(None, "tok", None),
            P(),
            P(),
            P(None, "tok"),
            P(None, "tok"),
            P(None, "tok", None),
            P(None, "tok"),
            P("tok", None),
            P("tok", None),
        ),
        out_specs=(P(None, "queue", "tok", None), P("queue", "tok", None)),
        check_vma=False,
    )
```
